1024 devices in a mesh: group: 8 (over x, core), dev: 128 (over y, z).
Axes of the slice: x: 4, y: 4, z: 32, core: 2. Of those that a mesh axis runs over, the one named last changes fastest.
Arguments:
- guess: float32 [64, 2048, 256], P('group', 'dev'), may hold values from -6 to 6
- divergence: float32 [64, 2048, 256], P('group', 'dev'), may hold values from -24 to 24
- counts: int32 [64, 2048, 256], P('group', 'dev'), may hold values from 0 to 15
Outputs:
- solution_field: float32 [64, 2048, 256], P('group', 'dev')
The draws below stay inside these ranges and needn't reach their ends.
All inputs are finite; a program needn't handle non-finite values.
Results may differ from the reference program's by a relative error of at most 0.00002.
Values sent between devices are 32-bit elements; how exact they have to be, the bound alone decides.
No kernel may reach another device: no remote copies, remote signals or barrier semaphores. Data moves between devices by JAX's collectives and lax.ppermute only.
A program may use at most 64 MiB of HBM per device.

```python
import jax
import jax.numpy as jnp

NU_PRE = 2
NU_POST = 2
NU_COARSE = 4
NX = 64
NY = 2048
NZ = 256


def plant(values, rng, least, largest):
    longest = values.shape.index(max(values.shape))
    spots = []
    for shift in (0, 1):
        where = [jax.random.randint(jax.random.fold_in(rng, axis), (), 0, length) for axis, length in enumerate(values.shape)]
        where[longest] = (where[longest] + shift) % values.shape[longest]
        spots.append(tuple(where))
    return values.at[spots[0]].set(least).at[spots[1]].set(largest)


def steps_of(key, dims, shards, smallest, top_value):
    gain, own = 1.0, jax.random.fold_in(key, 6)
    for axis_at, shards_of in shards:
        heights = jnp.exp(jax.random.uniform(jax.random.fold_in(own, axis_at), (shards_of,), jnp.float32, smallest / len(shards), top_value / len(shards)))
        gain = gain * jnp.repeat(heights, dims[axis_at] // shards_of).reshape([-1 if axis == axis_at else 1 for axis in range(len(dims))])
    return gain


def noise(key, shape, scale, bound, cuts=(), dtype=jnp.bfloat16):
    loudness = steps_of(key, shape, cuts, -0.22, 0.18) if cuts else 1.0
    entries = jax.random.normal(key, shape, jnp.float32) * scale * loudness
    return jnp.minimum(jnp.maximum(entries, -bound), bound).astype(dtype)


def setup_inputs(seed: int = 0) -> dict:
    streams_of = jax.random.split(jax.random.key(seed), 4)
    guess = noise(streams_of[0], (NX, NY, NZ), 1.0, 6.0, ((0, 8), (1, 128)), jnp.float32)
    divergence = noise(streams_of[1], (NX, NY, NZ), 4.0, 24.0, ((0, 8), (1, 128)), jnp.float32)
    counts = plant(jax.random.randint(streams_of[2], (NX, NY, NZ), 0, 16), jax.random.fold_in(streams_of[2], 1), 0, 15).astype(jnp.int32)
    return {"guess": guess, "divergence": divergence, "counts": counts}


def apply_op(field, diag):
    padded = jnp.pad(field, 1)
    beside = padded[2:, 1:-1, 1:-1] + padded[:-2, 1:-1, 1:-1]
    beside = beside + padded[1:-1, 2:, 1:-1] + padded[1:-1, :-2, 1:-1]
    beside = beside + padded[1:-1, 1:-1, 2:] + padded[1:-1, 1:-1, :-2]
    return diag * field - beside


def block_sum(field):
    nx, ny, nz = field.shape
    return field.reshape(nx // 2, 2, ny // 2, 2, nz // 2, 2).sum(axis=(1, 3, 5))


def reference(guess, divergence, counts):
    weights = counts.astype(jnp.float32)
    fine_diag = 6.0 + 0.25 * weights
    field = guess
    for sweep in range(NU_PRE):
        field = field + 0.8 * (divergence - apply_op(field, fine_diag)) / fine_diag
    fine_residual = divergence - apply_op(field, fine_diag)
    coarse_rhs = 0.5 * block_sum(fine_residual)
    coarse_diag = 6.0 + block_sum(weights) / 8.0
    correction = jnp.zeros_like(coarse_rhs)
    for sweep in range(NU_COARSE):
        correction = correction + 0.8 * (coarse_rhs - apply_op(correction, coarse_diag)) / coarse_diag
    spread_out = jnp.repeat(jnp.repeat(jnp.repeat(correction, 2, axis=0), 2, axis=1), 2, axis=2)
    field = field + spread_out
    for sweep in range(NU_POST):
        field = field + 0.8 * (divergence - apply_op(field, fine_diag)) / fine_diag
    return field
```

```python
import jax
import jax.numpy as jnp
from jax import lax
from jax.sharding import PartitionSpec as P
from jax.experimental import pallas as pl
from jax.experimental.pallas import tpu as pltpu

OMEGA = 0.8
KEEP = 1.0 - OMEGA
VM = pl.BlockSpec(memory_space=pltpu.VMEM)
F32 = jnp.float32
BX, BY, NZ = 8, 16, 256
CX, CY, CZ = 4, 8, 128


def call(kernel, outs, *args, scratch=(), hbm_out=False):
    make = jax.ShapeDtypeStruct if hbm_out else pltpu.VMEM
    return pl.pallas_call(
        kernel,
        out_shape=[make(s, F32) for s in outs],
        in_specs=[VM] * len(args),
        out_specs=[VM] * len(outs),
        scratch_shapes=[pltpu.VMEM(s, F32) for s in scratch],
        compiler_params=pltpu.CompilerParams(vmem_limit_bytes=8 * 2**20),
    )(*args)


def beside_z(v):
    lane = lax.broadcasted_iota(jnp.int32, v.shape, 1)
    last = v.shape[1] - 1
    below = jnp.where(lane == 0, 0.0, pltpu.roll(v, 1, 1))
    above = jnp.where(lane == last, 0.0, pltpu.roll(v, last, 1))
    return below + above


def shift_y(v, low, high):
    row = lax.broadcasted_iota(jnp.int32, v.shape, 0)
    last = v.shape[0] - 1
    below = jnp.where(row == 0, low, pltpu.roll(v, 1, 0))
    above = jnp.where(row == last, high, pltpu.roll(v, last, 0))
    return below, above


def beside_y(v, low, high):
    below, above = shift_y(v, low, high)
    return below + above


def slab(ref, k, rows=BY):
    return ref[k * rows : (k + 1) * rows, :]


def row(ref, k):
    return ref[k : k + 1, :]


def halved(n, m):
    a = lax.broadcasted_iota(jnp.int32, (n, m), 0)
    b = lax.broadcasted_iota(jnp.int32, (n, m), 1)
    return jnp.where((a // 2 == b) if n > m else (a == b // 2), 1.0, 0.0).astype(F32)


def diag_of(n):
    return 6.0 + 0.25 * n.astype(F32)


def pack_x_kernel(g, b, n, lo, hi):
    for out, layers in ((lo, (0, 1, 2)), (hi, (7, 6, 5))):
        for k in range(3):
            out[k * BY : (k + 1) * BY, :] = g[layers[k]]
        for k in range(2):
            out[(3 + k) * BY : (4 + k) * BY, :] = OMEGA / diag_of(n[layers[k]])
            out[(5 + k) * BY : (6 + k) * BY, :] = b[layers[k]]


class Wide:
    def __init__(self, g, b, n, left, right):
        self.g, self.b, self.n, self.left, self.right = g, b, n, left, right
        self.ws = {}

    def _side(self, x):
        return (self.left, -1 - x) if x < 0 else (self.right, x - BX)

    def guess(self, x):
        if 0 <= x < BX:
            return self.g[x]
        ref, k = self._side(x)
        return slab(ref, k)

    def w(self, x):
        if x not in self.ws:
            if 0 <= x < BX:
                self.ws[x] = OMEGA / diag_of(self.n[x])
            else:
                ref, k = self._side(x)
                self.ws[x] = slab(ref, 3 + k)
        return self.ws[x]

    def rhs(self, x):
        if 0 <= x < BX:
            return self.b[x]
        ref, k = self._side(x)
        return slab(ref, 5 + k)


Y_G, Y_P, Y_W, Y_Q = 0, 12, 22, 32
Y_ROWS = 40


def pack_y_kernel(g, b, n, left, right, lo, hi, f1z):
    a = Wide(g, b, n, left, right)
    for x in range(-2, 10):
        here = a.guess(x)
        f = KEEP * here + a.w(x) * (
            a.rhs(x) + a.guess(x - 1) + a.guess(x + 1) + beside_z(here) + beside_y(here, 0.0, 0.0)
        )
        f1z[(x + 2) * BY : (x + 3) * BY, :] = f
        for out, y, inner in ((lo, 0, 1), (hi, BY - 1, BY - 2)):
            k = Y_G + x + 2
            out[k : k + 1, :] = here[y : y + 1]
            if -1 <= x <= 8:
                k = Y_P + x + 1
                out[k : k + 1, :] = f[y : y + 1]
                k = Y_W + x + 1
                out[k : k + 1, :] = a.w(x)[y : y + 1]
            if 0 <= x <= 7:
                k = Y_Q + x
                out[k : k + 1, :] = a.w(x)[y : y + 1] * (a.rhs(x)[y : y + 1] + f[inner : inner + 1])


X2_ROWS = 3 * BY


def middle_kernel(g, b, n, left, right, f1z, low, high, f2, f2low, f2high, c1, wc, lo, hi, col, line, sums):
    a = Wide(g, b, n, left, right)
    rows = lax.broadcasted_iota(jnp.int32, (BY, NZ), 0)
    f1 = {}
    for x in range(-2, 10):
        k = Y_G + x + 2
        beyond = jnp.where(rows == 0, row(low, k), jnp.where(rows == BY - 1, row(high, k), 0.0))
        f1[x] = slab(f1z, x + 2) + a.w(x) * beyond
    for s, (side, y, out) in enumerate(((low, 0, f2low), (high, BY - 1, f2high))):
        for x in range(-1, 9):
            col[x + 1 : x + 2, :] = a.guess(x)[y : y + 1]
        line[s, 0:10, :] = side[Y_P : Y_P + 10, :] + side[Y_W : Y_W + 10, :] * col[0:10, :]
        for x in range(0, 8):
            col[x : x + 1, :] = f1[x][y : y + 1]
        mid = line[s, 1:9, :]
        out[...] = (
            KEEP * mid
            + side[Y_Q : Y_Q + 8, :]
            + side[Y_W + 1 : Y_W + 9, :]
            * (line[s, 0:8, :] + line[s, 2:10, :] + beside_z(mid) + col[0:8, :])
        )
    sec = {}
    for x in range(-1, 9):
        f = f1[x]
        sec[x] = KEEP * f + a.w(x) * (
            a.rhs(x)
            + f1[x - 1]
            + f1[x + 1]
            + beside_z(f)
            + beside_y(f, line[0, x + 1 : x + 2, :], line[1, x + 1 : x + 2, :])
        )
        f2[(x + 1) * BY : (x + 2) * BY, :] = sec[x]
    lo[2 * BY :, :] = sec[1]
    hi[2 * BY :, :] = sec[6]
    pairs, points = [], []
    for x in range(0, 8):
        f = sec[x]
        r = (
            a.rhs(x)
            - diag_of(n[x]) * f
            + sec[x - 1]
            + sec[x + 1]
            + beside_z(f)
            + beside_y(f, row(f2low, x), row(f2high, x))
        )
        if x % 2:
            pairs[-1] = pairs[-1] + r
            points[-1] = points[-1] + n[x].astype(F32)
        else:
            pairs.append(r)
            points.append(n[x].astype(F32))
    sums[...] = lax.dot_general(
        jnp.concatenate(pairs + points, axis=0),
        halved(NZ, CZ),
        (((1,), (0,)), ((), ())),
        precision=lax.Precision.HIGHEST,
        preferred_element_type=F32,
    )
    for x in range(CX):
        at = x * BY
        total = sums[pl.ds(at, CY, stride=2), :] + sums[pl.ds(at + 1, CY, stride=2), :]
        at = (CX + x) * BY
        count = sums[pl.ds(at, CY, stride=2), :] + sums[pl.ds(at + 1, CY, stride=2), :]
        weight = OMEGA / (6.0 + count / 8.0)
        first = weight * (0.5 * total)
        c1[x * CY : (x + 1) * CY, :] = first
        wc[x * CY : (x + 1) * CY, :] = weight
        for out, k in ((lo, x), (hi, CX - 1 - x)):
            out[k * CY : (k + 1) * CY, 0:CZ] = first
            out[k * CY : (k + 1) * CY, CZ:] = weight


class Coarse:
    def __init__(self, c1, wc, left, right):
        self.c1, self.wc, self.left, self.right = c1, wc, left, right

    def _get(self, x, own, lanes):
        if 0 <= x < CX:
            return slab(own, x, CY)
        ref, k = (self.left, -1 - x) if x < 0 else (self.right, x - CX)
        return ref[k * CY : (k + 1) * CY, lanes]

    def first(self, x):
        return self._get(x, self.c1, slice(0, CZ))

    def w(self, x):
        return self._get(x, self.wc, slice(CZ, 2 * CZ))


Z_C, Z_P, Z_W, Z_Q, Z_R, Z_V, Z_S, Z_K = 0, 10, 20, 30, 38, 44, 50, 66
Z_ROWS = 72


def pack_c_kernel(b, n, f2, c1, wc, left, right, lo, hi, c2z):
    a = Coarse(c1, wc, left, right)
    second = {}
    for x in range(-3, 7):
        c, w = a.first(x), a.w(x)
        second[x] = (1.0 + KEEP) * c + w * (
            a.first(x - 1) + a.first(x + 1) + beside_z(c) + beside_y(c, 0.0, 0.0)
        )
        c2z[(x + 3) * CY : (x + 4) * CY, :] = second[x]
        for out, y in ((lo, 0), (hi, CY - 1)):
            for base, v in ((Z_C, c), (Z_P, second[x]), (Z_W, w)):
                k = base + x + 3
                out[k : k + 1, :] = v[y : y + 1]
    for x in range(-2, 6):
        s, c, w = second[x], a.first(x), a.w(x)
        below, above = shift_y(s, 0.0, 0.0)
        inner = {0: above, 1: below}
        for side, (out, y, y2) in enumerate(((lo, 0, 1), (hi, CY - 1, CY - 2))):
            k = Z_Q + x + 2
            out[k : k + 1, :] = (c + w * inner[side])[y : y + 1]
        if -1 <= x <= 4:
            part = KEEP * s + c + w * (second[x - 1] + second[x + 1] + beside_z(s))
            for side, (out, y, y2) in enumerate(((lo, 0, 1), (hi, CY - 1, CY - 2))):
                k = Z_R + x + 1
                out[k : k + 1, :] = (part + w * inner[side])[y2 : y2 + 1]
                k = Z_V + x + 1
                out[k : k + 1, :] = w[y2 : y2 + 1]
    for out, y, inner in ((lo, 0, 1), (hi, BY - 1, BY - 2)):
        for x in range(BX):
            at = (x + 1) * BY
            w = OMEGA / diag_of(n[x][y : y + 1])
            v = w * (b[x][y : y + 1] + f2[at + inner : at + inner + 1, :])
            for half in range(2):
                k = Z_S + 2 * x + half
                out[k : k + 1, :] = v[:, half * CZ : (half + 1) * CZ]
        for j, x in enumerate((-1, 8)):
            at = (x + 1) * BY + y
            v = f2[at : at + 1, :]
            for half in range(2):
                k = Z_K + 2 * j + half
                out[k : k + 1, :] = v[:, half * CZ : (half + 1) * CZ]


def last_kernel(
    b, n, left, right, low, high, f2, f2low, f2high, c1, wc, cleft, cright, c2z, clow, chigh,
    out, col, line, line3, fine, corr, col2, s1, gline, g1line,
):
    a = Coarse(c1, wc, cleft, cright)
    wide = Wide(None, b, n, left, right)
    crow = lax.broadcasted_iota(jnp.int32, (CY, CZ), 0)
    c2 = {}
    for x in range(-3, 7):
        k = Z_C + x + 3
        beyond = jnp.where(crow == 0, row(clow, k), jnp.where(crow == CY - 1, row(chigh, k), 0.0))
        c2[x] = slab(c2z, x + 3, CY) + a.w(x) * beyond
    sides = ((clow, 0), (chigh, CY - 1))
    for s, (side, y) in enumerate(sides):
        for x in range(-3, 7):
            col[x + 3 : x + 4, :] = a.first(x)[y : y + 1]
        line[s, 0:10, :] = side[Z_P : Z_P + 10, :] + side[Z_W : Z_W + 10, :] * col[0:10, :]
        for x in range(-2, 6):
            col[x + 2 : x + 3, :] = c2[x][y : y + 1]
        mid = line[s, 1:9, :]
        line3[s, 0:8, :] = (
            KEEP * mid
            + side[Z_Q : Z_Q + 8, :]
            + side[Z_W + 1 : Z_W + 9, :]
            * (line[s, 0:8, :] + line[s, 2:10, :] + beside_z(mid) + col[0:8, :])
        )
    c3 = {}
    for x in range(-2, 6):
        c = c2[x]
        c3[x] = KEEP * c + a.first(x) + a.w(x) * (
            c2[x - 1]
            + c2[x + 1]
            + beside_z(c)
            + beside_y(c, line[0, x + 3 : x + 4, :], line[1, x + 3 : x + 4, :])
        )
    for x in range(-1, 5):
        c = c3[x]
        c4 = KEEP * c + a.first(x) + a.w(x) * (
            c3[x - 1]
            + c3[x + 1]
            + beside_z(c)
            + beside_y(c, line3[0, x + 2 : x + 3, :], line3[1, x + 2 : x + 3, :])
        )
        fine[pl.ds((x + 1) * BY, CY, stride=2), :] = c4
        fine[pl.ds((x + 1) * BY + 1, CY, stride=2), :] = c4
    for s, (side, y) in enumerate(sides):
        for x in range(-1, 5):
            col[x + 1 : x + 2, :] = c3[x][y : y + 1]
        mid = line3[s, 1:7, :]
        third = side[Z_R : Z_R + 6, :] + side[Z_V : Z_V + 6, :] * line[s, 2:8, :]
        fine[6 * BY + 8 * s : 6 * BY + 8 * s + 6, :] = (
            KEEP * mid
            + side[Z_C + 2 : Z_C + 8, :]
            + side[Z_W + 2 : Z_W + 8, :]
            * (line3[s, 0:6, :] + line3[s, 2:8, :] + beside_z(mid) + third + col[0:6, :])
        )
        fine[6 * BY + 8 * s + 6 : 6 * BY + 8 * s + 8, :] = jnp.zeros((2, CZ), F32)
    corr[...] = lax.dot_general(
        fine[...],
        halved(CZ, NZ),
        (((1,), (0,)), ((), ())),
        precision=lax.Precision.HIGHEST,
        preferred_element_type=F32,
    )
    g0 = {}
    for x in range(-2, 10):
        if x == -2:
            f = slab(cleft, 2)
        elif x == 9:
            f = slab(cright, 2)
        else:
            f = slab(f2, x + 1)
        g0[x] = f + slab(corr, (x + 2) // 2)
    for s, (cside, side, y, f2side) in enumerate(((clow, low, 0, f2low), (chigh, high, BY - 1, f2high))):
        base = 6 * BY + 8 * s
        for x in range(-1, 9):
            k = base + (x + 2) // 2
            col2[x + 1 : x + 2, :] = corr[k : k + 1, :]
        gline[s, 1:9, :] = f2side[...] + col2[1:9, :]
        for j, x in enumerate((-1, 8)):
            k = Z_K + 2 * j
            gline[s, x + 1 : x + 2, 0:CZ] = row(cside, k) + col2[x + 1 : x + 2, 0:CZ]
            gline[s, x + 1 : x + 2, CZ:] = row(cside, k + 1) + col2[x + 1 : x + 2, CZ:]
        for x in range(BX):
            k = Z_S + 2 * x
            s1[x : x + 1, 0:CZ] = row(cside, k)
            s1[x : x + 1, CZ:] = row(cside, k + 1)
        moved = col2[1:9, :]
        for x in range(BX):
            col2[x : x + 1, :] = g0[x][y : y + 1]
        mid = gline[s, 1:9, :]
        g1line[s, 0:8, :] = (
            KEEP * mid
            + s1[0:8, :]
            + side[Y_W + 1 : Y_W + 9, :]
            * (moved + gline[s, 0:8, :] + gline[s, 2:10, :] + beside_z(mid) + col2[0:8, :])
        )
    g1 = {}
    for x in range(-1, 9):
        f = g0[x]
        g1[x] = KEEP * f + wide.w(x) * (
            wide.rhs(x)
            + g0[x - 1]
            + g0[x + 1]
            + beside_z(f)
            + beside_y(f, gline[0, x + 1 : x + 2, :], gline[1, x + 1 : x + 2, :])
        )
    for x in range(BX):
        f = g1[x]
        out[x] = KEEP * f + wide.w(x) * (
            wide.rhs(x)
            + g1[x - 1]
            + g1[x + 1]
            + beside_z(f)
            + beside_y(f, g1line[0, x : x + 1, :], g1line[1, x : x + 1, :])
        )


def exchange(to_low, to_high, axis):
    n = lax.axis_size(axis)
    from_low = lax.ppermute(to_high, axis, [(i, i + 1) for i in range(n - 1)])
    from_high = lax.ppermute(to_low, axis, [(i + 1, i) for i in range(n - 1)])
    return from_low, from_high


def body(g, b, n):
    lo, hi = call(pack_x_kernel, [(7 * BY, NZ)] * 2, g, b, n)
    left, right = exchange(lo, hi, "group")
    lo, hi, f1z = call(pack_y_kernel, [(Y_ROWS, NZ)] * 2 + [(12 * BY, NZ)], g, b, n, left, right)
    low, high = exchange(lo, hi, "dev")
    f2, f2low, f2high, c1, wc, lo, hi = call(
        middle_kernel,
        [(10 * BY, NZ), (BX, NZ), (BX, NZ), (CX * CY, CZ), (CX * CY, CZ), (X2_ROWS, NZ), (X2_ROWS, NZ)],
        g, b, n, left, right, f1z, low, high,
        scratch=[(16, NZ), (2, 16, NZ), (8 * BY, CZ)],
    )
    cleft, cright = exchange(lo, hi, "group")
    lo, hi, c2z = call(
        pack_c_kernel, [(Z_ROWS, CZ)] * 2 + [(10 * CY, CZ)], b, n, f2, c1, wc, cleft, cright
    )
    clow, chigh = exchange(lo, hi, "dev")
    (out,) = call(
        last_kernel,
        [(BX, BY, NZ)],
        b, n, left, right, low, high, f2, f2low, f2high, c1, wc, cleft, cright, c2z, clow, chigh,
        scratch=[
            (16, CZ), (2, 16, CZ), (2, 8, CZ), (6 * BY + 16, CZ), (6 * BY + 16, NZ), (16, NZ), (8, NZ), (2, 16, NZ), (2, 8, NZ),
        ],
        hbm_out=True,
    )
    return out


def solution(mesh):
    s = P("group", "dev", None)
    return jax.shard_map(body, mesh=mesh, in_specs=(s, s, s), out_specs=s, check_vma=False)
```

```python
import jax
import jax.numpy as jnp
from jax import lax
from jax.sharding import PartitionSpec as P
from jax.experimental import pallas as pl
from jax.experimental.pallas import tpu as pltpu

OMEGA = 0.8
KEEP = 1.0 - OMEGA
VM = pl.BlockSpec(memory_space=pltpu.VMEM)
F32 = jnp.float32
BX, BY, NZ = 8, 16, 256
CX, CY, CZ = 4, 8, 128


def call(kernel, outs, *args, scratch=(), hbm=0, hbm_out=False, vmem=8 * 2**20):
    make = jax.ShapeDtypeStruct if hbm_out else pltpu.VMEM
    return pl.pallas_call(
        kernel,
        out_shape=[make(s, F32) for s in outs],
        in_specs=[pl.BlockSpec(memory_space=pltpu.HBM)] * hbm + [VM] * (len(args) - hbm),
        out_specs=[VM] * len(outs),
        scratch_shapes=[pltpu.VMEM(s, F32) if isinstance(s, tuple) else s for s in scratch],
        compiler_params=pltpu.CompilerParams(vmem_limit_bytes=vmem),
    )(*args)


def beside_z(v):
    lane = lax.broadcasted_iota(jnp.int32, v.shape, 1)
    last = v.shape[1] - 1
    below = jnp.where(lane == 0, 0.0, pltpu.roll(v, 1, 1))
    above = jnp.where(lane == last, 0.0, pltpu.roll(v, last, 1))
    return below + above


def shift_y(v, low, high):
    row = lax.broadcasted_iota(jnp.int32, v.shape, 0)
    last = v.shape[0] - 1
    below = jnp.where(row == 0, low, pltpu.roll(v, 1, 0))
    above = jnp.where(row == last, high, pltpu.roll(v, last, 0))
    return below, above


def beside_y(v, low, high):
    below, above = shift_y(v, low, high)
    return below + above


def slab(ref, k, rows=BY):
    return ref[k * rows : (k + 1) * rows, :]


def row(ref, k):
    return ref[k : k + 1, :]


def halved(n, m):
    a = lax.broadcasted_iota(jnp.int32, (n, m), 0)
    b = lax.broadcasted_iota(jnp.int32, (n, m), 1)
    return jnp.where((a // 2 == b) if n > m else (a == b // 2), 1.0, 0.0).astype(F32)


def diag_of(n):
    return 6.0 + 0.25 * n.astype(F32)


def place(x):
    odd = lax.axis_index("group") % 2
    return x + odd * (BX - 1 - 2 * x)


def side_of_dev():
    return lax.axis_index("dev") % 2


def load_kernel(g_hbm, b_hbm, n_hbm, cross, chip, g, b, w, d, n, sems):
    copies = [
        pltpu.make_async_copy(src, dst, sems.at[k])
        for k, (src, dst) in enumerate(((g_hbm, g), (b_hbm, b), (n_hbm, n)))
    ]
    for c in copies:
        c.start()
    for c in copies:
        c.wait()
    for x in range(BX):
        diag = diag_of(n[x])
        d[x] = diag
        w[x] = OMEGA / diag
    for out, layers in ((cross, (0, 1, 2)), (chip, (7, 6, 5))):
        for k in range(3):
            out[k * BY : (k + 1) * BY, :] = g[place(layers[k])]
        for k in range(2):
            out[(3 + k) * BY : (4 + k) * BY, :] = w[place(layers[k])]
            out[(5 + k) * BY : (6 + k) * BY, :] = b[place(layers[k])]


class Wide:
    def __init__(self, g, b, w, left, right):
        self.own, self.left, self.right = (g, w, b), left, right

    def _get(self, which, base, x):
        if 0 <= x < BX:
            return self.own[which][place(x)]
        ref, k = (self.left, -1 - x) if x < 0 else (self.right, x - BX)
        return slab(ref, base + k)

    def guess(self, x):
        return self._get(0, 0, x)

    def w(self, x):
        return self._get(1, 3, x)

    def rhs(self, x):
        return self._get(2, 5, x)


def give(both, first, second):
    p = side_of_dev()
    first[...] = both[p]
    second[...] = both[1 - p]


def take(both, first, second):
    p = side_of_dev()
    both[p] = first[...]
    both[1 - p] = second[...]


Y_G, Y_P, Y_W, Y_Q = 0, 12, 22, 32
Y_ROWS = 40


def pack_y_kernel(g, b, w, left, right, first, second, f1z, both):
    a = Wide(g, b, w, left, right)
    lo, hi = both.at[0], both.at[1]
    for x in range(-2, 10):
        here = a.guess(x)
        f = KEEP * here + a.w(x) * (
            a.rhs(x) + a.guess(x - 1) + a.guess(x + 1) + beside_z(here) + beside_y(here, 0.0, 0.0)
        )
        f1z[(x + 2) * BY : (x + 3) * BY, :] = f
        for out, y, inner in ((lo, 0, 1), (hi, BY - 1, BY - 2)):
            k = Y_G + x + 2
            out[k : k + 1, :] = here[y : y + 1]
            if -1 <= x <= 8:
                k = Y_P + x + 1
                out[k : k + 1, :] = f[y : y + 1]
                k = Y_W + x + 1
                out[k : k + 1, :] = a.w(x)[y : y + 1]
            if 0 <= x <= 7:
                k = Y_Q + x
                out[k : k + 1, :] = a.w(x)[y : y + 1] * (a.rhs(x)[y : y + 1] + f[inner : inner + 1])
    give(both, first, second)


X2_ROWS = 3 * BY


def middle_kernel(
    g, b, w, d, left, right, f1z, first, second, f2, f2low, f2high, c1, wc, lo, hi, both, col, line, sums
):
    a = Wide(g, b, w, left, right)
    take(both, first, second)
    low, high = both.at[0], both.at[1]
    rows = lax.broadcasted_iota(jnp.int32, (BY, NZ), 0)
    f1 = {}
    for x in range(-2, 10):
        k = Y_G + x + 2
        beyond = jnp.where(rows == 0, row(low, k), jnp.where(rows == BY - 1, row(high, k), 0.0))
        f1[x] = slab(f1z, x + 2) + a.w(x) * beyond
    for s, (side, y, out) in enumerate(((low, 0, f2low), (high, BY - 1, f2high))):
        for x in range(-1, 9):
            col[x + 1 : x + 2, :] = a.guess(x)[y : y + 1]
        line[s, 0:10, :] = side[Y_P : Y_P + 10, :] + side[Y_W : Y_W + 10, :] * col[0:10, :]
        for x in range(0, 8):
            col[x : x + 1, :] = f1[x][y : y + 1]
        mid = line[s, 1:9, :]
        out[...] = (
            KEEP * mid
            + side[Y_Q : Y_Q + 8, :]
            + side[Y_W + 1 : Y_W + 9, :]
            * (line[s, 0:8, :] + line[s, 2:10, :] + beside_z(mid) + col[0:8, :])
        )
    sec = {}
    for x in range(-1, 9):
        f = f1[x]
        sec[x] = KEEP * f + a.w(x) * (
            a.rhs(x)
            + f1[x - 1]
            + f1[x + 1]
            + beside_z(f)
            + beside_y(f, line[0, x + 1 : x + 2, :], line[1, x + 1 : x + 2, :])
        )
        f2[(x + 1) * BY : (x + 2) * BY, :] = sec[x]
    lo[2 * BY :, :] = sec[1]
    hi[2 * BY :, :] = sec[6]
    pairs, points = [], []
    for x in range(0, 8):
        f = sec[x]
        r = (
            a.rhs(x)
            - d[place(x)] * f
            + sec[x - 1]
            + sec[x + 1]
            + beside_z(f)
            + beside_y(f, row(f2low, x), row(f2high, x))
        )
        if x % 2:
            pairs[-1] = pairs[-1] + r
            points[-1] = points[-1] + d[place(x)]
        else:
            pairs.append(r)
            points.append(d[place(x)])
    sums[...] = lax.dot_general(
        jnp.concatenate(pairs + points, axis=0),
        halved(NZ, CZ),
        (((1,), (0,)), ((), ())),
        precision=lax.Precision.HIGHEST,
        preferred_element_type=F32,
    )
    for x in range(CX):
        at = x * BY
        total = sums[pl.ds(at, CY, stride=2), :] + sums[pl.ds(at + 1, CY, stride=2), :]
        at = (CX + x) * BY
        diags = sums[pl.ds(at, CY, stride=2), :] + sums[pl.ds(at + 1, CY, stride=2), :]
        weight = OMEGA / (0.5 * diags - 18.0)
        first = weight * (0.5 * total)
        c1[x * CY : (x + 1) * CY, :] = first
        wc[x * CY : (x + 1) * CY, :] = weight
        for out, k in ((lo, x), (hi, CX - 1 - x)):
            out[k * CY : (k + 1) * CY, 0:CZ] = first
            out[k * CY : (k + 1) * CY, CZ:] = weight


class Coarse:
    def __init__(self, c1, wc, left, right):
        self.c1, self.wc, self.left, self.right = c1, wc, left, right

    def _get(self, x, own, lanes):
        if 0 <= x < CX:
            return slab(own, x, CY)
        ref, k = (self.left, -1 - x) if x < 0 else (self.right, x - CX)
        return ref[k * CY : (k + 1) * CY, lanes]

    def first(self, x):
        return self._get(x, self.c1, slice(0, CZ))

    def w(self, x):
        return self._get(x, self.wc, slice(CZ, 2 * CZ))


Z_C, Z_P, Z_W, Z_Q, Z_R, Z_V, Z_S, Z_K = 0, 10, 20, 30, 38, 44, 50, 66
Z_ROWS = 72


def pack_c_kernel(b, w, f2, c1, wc, left, right, one, two, c2z, both):
    a = Coarse(c1, wc, left, right)
    lo, hi = both.at[0], both.at[1]
    second = {}
    for x in range(-3, 7):
        c, cw = a.first(x), a.w(x)
        second[x] = (1.0 + KEEP) * c + cw * (
            a.first(x - 1) + a.first(x + 1) + beside_z(c) + beside_y(c, 0.0, 0.0)
        )
        c2z[(x + 3) * CY : (x + 4) * CY, :] = second[x]
        for out, y in ((lo, 0), (hi, CY - 1)):
            for base, v in ((Z_C, c), (Z_P, second[x]), (Z_W, cw)):
                k = base + x + 3
                out[k : k + 1, :] = v[y : y + 1]
    for x in range(-2, 6):
        s, c, cw = second[x], a.first(x), a.w(x)
        below, above = shift_y(s, 0.0, 0.0)
        inner = {0: above, 1: below}
        for side, (out, y, y2) in enumerate(((lo, 0, 1), (hi, CY - 1, CY - 2))):
            k = Z_Q + x + 2
            out[k : k + 1, :] = (c + cw * inner[side])[y : y + 1]
        if -1 <= x <= 4:
            part = KEEP * s + c + cw * (second[x - 1] + second[x + 1] + beside_z(s))
            for side, (out, y, y2) in enumerate(((lo, 0, 1), (hi, CY - 1, CY - 2))):
                k = Z_R + x + 1
                out[k : k + 1, :] = (part + cw * inner[side])[y2 : y2 + 1]
                k = Z_V + x + 1
                out[k : k + 1, :] = cw[y2 : y2 + 1]
    for out, y, inner in ((lo, 0, 1), (hi, BY - 1, BY - 2)):
        for x in range(BX):
            at = (x + 1) * BY
            at_x = place(x)
            v = w[at_x][y : y + 1] * (b[at_x][y : y + 1] + f2[at + inner : at + inner + 1, :])
            for half in range(2):
                k = Z_S + 2 * x + half
                out[k : k + 1, :] = v[:, half * CZ : (half + 1) * CZ]
        for j, x in enumerate((-1, 8)):
            at = (x + 1) * BY + y
            v = f2[at : at + 1, :]
            for half in range(2):
                k = Z_K + 2 * j + half
                out[k : k + 1, :] = v[:, half * CZ : (half + 1) * CZ]
    give(both, one, two)


def last_kernel(
    b, w, left, right, first, second, f2, f2low, f2high, c1, wc, cleft, cright, c2z, one, two,
    out, both, cboth, col, line, line3, fine, corr, col2, s1, gline, g1line,
):
    a = Coarse(c1, wc, cleft, cright)
    wide = Wide(None, b, w, left, right)
    take(both, first, second)
    take(cboth, one, two)
    low, high, clow, chigh = both.at[0], both.at[1], cboth.at[0], cboth.at[1]
    crow = lax.broadcasted_iota(jnp.int32, (CY, CZ), 0)
    c2 = {}
    for x in range(-3, 7):
        k = Z_C + x + 3
        beyond = jnp.where(crow == 0, row(clow, k), jnp.where(crow == CY - 1, row(chigh, k), 0.0))
        c2[x] = slab(c2z, x + 3, CY) + a.w(x) * beyond
    sides = ((clow, 0), (chigh, CY - 1))
    for s, (side, y) in enumerate(sides):
        for x in range(-3, 7):
            col[x + 3 : x + 4, :] = a.first(x)[y : y + 1]
        line[s, 0:10, :] = side[Z_P : Z_P + 10, :] + side[Z_W : Z_W + 10, :] * col[0:10, :]
        for x in range(-2, 6):
            col[x + 2 : x + 3, :] = c2[x][y : y + 1]
        mid = line[s, 1:9, :]
        line3[s, 0:8, :] = (
            KEEP * mid
            + side[Z_Q : Z_Q + 8, :]
            + side[Z_W + 1 : Z_W + 9, :]
            * (line[s, 0:8, :] + line[s, 2:10, :] + beside_z(mid) + col[0:8, :])
        )
    c3 = {}
    for x in range(-2, 6):
        c = c2[x]
        c3[x] = KEEP * c + a.first(x) + a.w(x) * (
            c2[x - 1]
            + c2[x + 1]
            + beside_z(c)
            + beside_y(c, line[0, x + 3 : x + 4, :], line[1, x + 3 : x + 4, :])
        )
    for x in range(-1, 5):
        c = c3[x]
        c4 = KEEP * c + a.first(x) + a.w(x) * (
            c3[x - 1]
            + c3[x + 1]
            + beside_z(c)
            + beside_y(c, line3[0, x + 2 : x + 3, :], line3[1, x + 2 : x + 3, :])
        )
        fine[pl.ds((x + 1) * BY, CY, stride=2), :] = c4
        fine[pl.ds((x + 1) * BY + 1, CY, stride=2), :] = c4
    for s, (side, y) in enumerate(sides):
        for x in range(-1, 5):
            col[x + 1 : x + 2, :] = c3[x][y : y + 1]
        mid = line3[s, 1:7, :]
        third = side[Z_R : Z_R + 6, :] + side[Z_V : Z_V + 6, :] * line[s, 2:8, :]
        fine[6 * BY + 8 * s : 6 * BY + 8 * s + 6, :] = (
            KEEP * mid
            + side[Z_C + 2 : Z_C + 8, :]
            + side[Z_W + 2 : Z_W + 8, :]
            * (line3[s, 0:6, :] + line3[s, 2:8, :] + beside_z(mid) + third + col[0:6, :])
        )
        fine[6 * BY + 8 * s + 6 : 6 * BY + 8 * s + 8, :] = jnp.zeros((2, CZ), F32)
    corr[...] = lax.dot_general(
        fine[...],
        halved(CZ, NZ),
        (((1,), (0,)), ((), ())),
        precision=lax.Precision.HIGHEST,
        preferred_element_type=F32,
    )
    g0 = {}
    for x in range(-2, 10):
        if x == -2:
            f = slab(cleft, 2)
        elif x == 9:
            f = slab(cright, 2)
        else:
            f = slab(f2, x + 1)
        g0[x] = f + slab(corr, (x + 2) // 2)
    for s, (cside, side, y, f2side) in enumerate(((clow, low, 0, f2low), (chigh, high, BY - 1, f2high))):
        base = 6 * BY + 8 * s
        for x in range(-1, 9):
            k = base + (x + 2) // 2
            col2[x + 1 : x + 2, :] = corr[k : k + 1, :]
        gline[s, 1:9, :] = f2side[...] + col2[1:9, :]
        for j, x in enumerate((-1, 8)):
            k = Z_K + 2 * j
            gline[s, x + 1 : x + 2, 0:CZ] = row(cside, k) + col2[x + 1 : x + 2, 0:CZ]
            gline[s, x + 1 : x + 2, CZ:] = row(cside, k + 1) + col2[x + 1 : x + 2, CZ:]
        for x in range(BX):
            k = Z_S + 2 * x
            s1[x : x + 1, 0:CZ] = row(cside, k)
            s1[x : x + 1, CZ:] = row(cside, k + 1)
        moved = col2[1:9, :]
        for x in range(BX):
            col2[x : x + 1, :] = g0[x][y : y + 1]
        mid = gline[s, 1:9, :]
        g1line[s, 0:8, :] = (
            KEEP * mid
            + s1[0:8, :]
            + side[Y_W + 1 : Y_W + 9, :]
            * (moved + gline[s, 0:8, :] + gline[s, 2:10, :] + beside_z(mid) + col2[0:8, :])
        )
    g1 = {}
    for x in range(-1, 9):
        f = g0[x]
        g1[x] = KEEP * f + wide.w(x) * (
            wide.rhs(x)
            + g0[x - 1]
            + g0[x + 1]
            + beside_z(f)
            + beside_y(f, gline[0, x + 1 : x + 2, :], gline[1, x + 1 : x + 2, :])
        )
    for x in range(BX):
        f = g1[x]
        out[place(x)] = KEEP * f + wide.w(x) * (
            wide.rhs(x)
            + g1[x - 1]
            + g1[x + 1]
            + beside_z(f)
            + beside_y(f, g1line[0, x : x + 1, :], g1line[1, x : x + 1, :])
        )


def swap(v, axis, start):
    pairs = [(i, i + 1) for i in range(start, lax.axis_size(axis) - 1, 2)]
    return lax.ppermute(v, axis, pairs + [(j, i) for i, j in pairs])


def exchange(first, second, axis):
    return swap(first, axis, 1), swap(second, axis, 0)


def body(g, b, n):
    block = (BX, BY, NZ)
    cross, chip, g, b, w, d = call(
        load_kernel,
        [(7 * BY, NZ)] * 2 + [block] * 4,
        g, b, n,
        hbm=3,
        vmem=None,
        scratch=[pltpu.VMEM(block, jnp.int32), pltpu.SemaphoreType.DMA((3,))],
    )
    left, right = exchange(cross, chip, "group")
    first, second, f1z = call(
        pack_y_kernel,
        [(Y_ROWS, NZ)] * 2 + [(12 * BY, NZ)],
        g, b, w, left, right,
        scratch=[(2, Y_ROWS, NZ)],
    )
    first, second = exchange(first, second, "dev")
    f2, f2low, f2high, c1, wc, cross, chip = call(
        middle_kernel,
        [(10 * BY, NZ), (BX, NZ), (BX, NZ), (CX * CY, CZ), (CX * CY, CZ), (X2_ROWS, NZ), (X2_ROWS, NZ)],
        g, b, w, d, left, right, f1z, first, second,
        scratch=[(2, Y_ROWS, NZ), (16, NZ), (2, 16, NZ), (8 * BY, CZ)],
    )
    cleft, cright = exchange(cross, chip, "group")
    one, two, c2z = call(
        pack_c_kernel,
        [(Z_ROWS, CZ)] * 2 + [(10 * CY, CZ)],
        b, w, f2, c1, wc, cleft, cright,
        scratch=[(2, Z_ROWS, CZ)],
    )
    one, two = exchange(one, two, "dev")
    (out,) = call(
        last_kernel,
        [block],
        b, w, left, right, first, second, f2, f2low, f2high, c1, wc, cleft, cright, c2z, one, two,
        scratch=[
            (2, Y_ROWS, NZ), (2, Z_ROWS, CZ),
            (16, CZ), (2, 16, CZ), (2, 8, CZ), (6 * BY + 16, CZ), (6 * BY + 16, NZ), (16, NZ), (8, NZ), (2, 16, NZ), (2, 8, NZ),
        ],
        hbm_out=True,
    )
    return out


def solution(mesh):
    s = P("group", "dev", None)
    return jax.shard_map(body, mesh=mesh, in_specs=(s, s, s), out_specs=s, check_vma=False)
```

```python
import jax
import jax.numpy as jnp
from jax import lax
from jax.sharding import PartitionSpec as P
from jax.experimental import pallas as pl
from jax.experimental.pallas import tpu as pltpu

OMEGA = 0.8
KEEP = 1.0 - OMEGA
VM = pl.BlockSpec(memory_space=pltpu.VMEM)
F32 = jnp.float32
BX, BY, NZ = 8, 16, 256
CX, CY, CZ = 4, 8, 128


def call(kernel, outs, *args, scratch=(), hbm=0, hbm_out=False, vmem=8 * 2**20):
    make = jax.ShapeDtypeStruct if hbm_out else pltpu.VMEM
    return pl.pallas_call(
        kernel,
        out_shape=[make(s, F32) for s in outs],
        in_specs=[pl.BlockSpec(memory_space=pltpu.HBM)] * hbm + [VM] * (len(args) - hbm),
        out_specs=[VM] * len(outs),
        scratch_shapes=[pltpu.VMEM(s, F32) if isinstance(s, tuple) else s for s in scratch],
        compiler_params=pltpu.CompilerParams(vmem_limit_bytes=vmem),
    )(*args)


def beside_z(v):
    lane = lax.broadcasted_iota(jnp.int32, v.shape, 1)
    last = v.shape[1] - 1
    below = jnp.where(lane == 0, 0.0, pltpu.roll(v, 1, 1))
    above = jnp.where(lane == last, 0.0, pltpu.roll(v, last, 1))
    return below + above


def shift_y(v, low, high):
    row = lax.broadcasted_iota(jnp.int32, v.shape, 0)
    last = v.shape[0] - 1
    below = jnp.where(row == 0, low, pltpu.roll(v, 1, 0))
    above = jnp.where(row == last, high, pltpu.roll(v, last, 0))
    return below, above


def beside_y(v, low, high):
    below, above = shift_y(v, low, high)
    return below + above


def slab(ref, k, rows=BY):
    return ref[k * rows : (k + 1) * rows, :]


def row(ref, k):
    return ref[k : k + 1, :]


def halved(n, m):
    a = lax.broadcasted_iota(jnp.int32, (n, m), 0)
    b = lax.broadcasted_iota(jnp.int32, (n, m), 1)
    return jnp.where((a // 2 == b) if n > m else (a == b // 2), 1.0, 0.0).astype(F32)


def diag_of(n):
    return 6.0 + 0.25 * n.astype(F32)


def place(x):
    odd = lax.axis_index("group") % 2
    return x + odd * (BX - 1 - 2 * x)


def partner(ref):
    return ref.at[1 - lax.axis_index("group") % 2]


def side_of_dev():
    return lax.axis_index("dev") % 2


def load_kernel(g_hbm, b_hbm, n_hbm, cross, chip, g, b, w, d, n, sems):
    copies = [
        pltpu.make_async_copy(src, dst, sems.at[k])
        for k, (src, dst) in enumerate(((g_hbm, g), (b_hbm, b), (n_hbm, n)))
    ]
    for c in copies:
        c.start()
    for c in copies:
        c.wait()
    for x in range(BX):
        diag = diag_of(n[x])
        d[x] = diag
        w[x] = OMEGA / diag
    for out, layers in ((cross, (0, 1, 2)), (chip, (7, 6, 5))):
        for k in range(3):
            out[k * BY : (k + 1) * BY, :] = g[place(layers[k])]
        for k in range(2):
            out[(3 + k) * BY : (4 + k) * BY, :] = w[place(layers[k])]
            out[(5 + k) * BY : (6 + k) * BY, :] = b[place(layers[k])]


class Wide:
    def __init__(self, g, b, w, left, right):
        self.own, self.left, self.right = (g, w, b), left, partner(right)

    def _get(self, which, base, x):
        if 0 <= x < BX:
            return self.own[which][place(x)]
        ref, k = (self.left, -1 - x) if x < 0 else (self.right, x - BX)
        return slab(ref, base + k)

    def guess(self, x):
        return self._get(0, 0, x)

    def w(self, x):
        return self._get(1, 3, x)

    def rhs(self, x):
        return self._get(2, 5, x)


def give(both, first, second):
    p = side_of_dev()
    first[...] = both[p]
    second[...] = both[1 - p]


def take(both, first, second):
    p = side_of_dev()
    both[p] = first[...]
    both[1 - p] = second[1 - p]


Y_G, Y_P, Y_W, Y_Q = 0, 12, 22, 32
Y_ROWS = 40


def pack_y_kernel(g, b, w, left, right, first, second, f1z, both):
    a = Wide(g, b, w, left, right)
    lo, hi = both.at[0], both.at[1]
    for x in range(-2, 10):
        here = a.guess(x)
        f = KEEP * here + a.w(x) * (
            a.rhs(x) + a.guess(x - 1) + a.guess(x + 1) + beside_z(here) + beside_y(here, 0.0, 0.0)
        )
        f1z[(x + 2) * BY : (x + 3) * BY, :] = f
        for out, y, inner in ((lo, 0, 1), (hi, BY - 1, BY - 2)):
            k = Y_G + x + 2
            out[k : k + 1, :] = here[y : y + 1]
            if -1 <= x <= 8:
                k = Y_P + x + 1
                out[k : k + 1, :] = f[y : y + 1]
                k = Y_W + x + 1
                out[k : k + 1, :] = a.w(x)[y : y + 1]
            if 0 <= x <= 7:
                k = Y_Q + x
                out[k : k + 1, :] = a.w(x)[y : y + 1] * (a.rhs(x)[y : y + 1] + f[inner : inner + 1])
    give(both, first, second)


X2_ROWS = 3 * BY


def middle_kernel(
    g, b, w, d, left, right, f1z, first, second, f2, f2low, f2high, c1, wc, lo, hi, both, col, line, sums
):
    a = Wide(g, b, w, left, right)
    take(both, first, second)
    low, high = both.at[0], both.at[1]
    rows = lax.broadcasted_iota(jnp.int32, (BY, NZ), 0)
    f1 = {}
    for x in range(-2, 10):
        k = Y_G + x + 2
        beyond = jnp.where(rows == 0, row(low, k), jnp.where(rows == BY - 1, row(high, k), 0.0))
        f1[x] = slab(f1z, x + 2) + a.w(x) * beyond
    for s, (side, y, out) in enumerate(((low, 0, f2low), (high, BY - 1, f2high))):
        for x in range(-1, 9):
            col[x + 1 : x + 2, :] = a.guess(x)[y : y + 1]
        line[s, 0:10, :] = side[Y_P : Y_P + 10, :] + side[Y_W : Y_W + 10, :] * col[0:10, :]
        for x in range(0, 8):
            col[x : x + 1, :] = f1[x][y : y + 1]
        mid = line[s, 1:9, :]
        out[...] = (
            KEEP * mid
            + side[Y_Q : Y_Q + 8, :]
            + side[Y_W + 1 : Y_W + 9, :]
            * (line[s, 0:8, :] + line[s, 2:10, :] + beside_z(mid) + col[0:8, :])
        )
    sec = {}
    for x in range(-1, 9):
        f = f1[x]
        sec[x] = KEEP * f + a.w(x) * (
            a.rhs(x)
            + f1[x - 1]
            + f1[x + 1]
            + beside_z(f)
            + beside_y(f, line[0, x + 1 : x + 2, :], line[1, x + 1 : x + 2, :])
        )
        f2[(x + 1) * BY : (x + 2) * BY, :] = sec[x]
    lo[2 * BY :, :] = sec[1]
    hi[2 * BY :, :] = sec[6]
    pairs, points = [], []
    for x in range(0, 8):
        f = sec[x]
        r = (
            a.rhs(x)
            - d[place(x)] * f
            + sec[x - 1]
            + sec[x + 1]
            + beside_z(f)
            + beside_y(f, row(f2low, x), row(f2high, x))
        )
        if x % 2:
            pairs[-1] = pairs[-1] + r
            points[-1] = points[-1] + d[place(x)]
        else:
            pairs.append(r)
            points.append(d[place(x)])
    sums[...] = lax.dot_general(
        jnp.concatenate(pairs + points, axis=0),
        halved(NZ, CZ),
        (((1,), (0,)), ((), ())),
        precision=lax.Precision.HIGHEST,
        preferred_element_type=F32,
    )
    for x in range(CX):
        at = x * BY
        total = sums[pl.ds(at, CY, stride=2), :] + sums[pl.ds(at + 1, CY, stride=2), :]
        at = (CX + x) * BY
        diags = sums[pl.ds(at, CY, stride=2), :] + sums[pl.ds(at + 1, CY, stride=2), :]
        weight = OMEGA / (0.5 * diags - 18.0)
        first = weight * (0.5 * total)
        c1[x * CY : (x + 1) * CY, :] = first
        wc[x * CY : (x + 1) * CY, :] = weight
        for out, k in ((lo, x), (hi, CX - 1 - x)):
            out[k * CY : (k + 1) * CY, 0:CZ] = first
            out[k * CY : (k + 1) * CY, CZ:] = weight


class Coarse:
    def __init__(self, c1, wc, left, right):
        self.c1, self.wc, self.left, self.right = c1, wc, left, partner(right)

    def _get(self, x, own, lanes):
        if 0 <= x < CX:
            return slab(own, x, CY)
        ref, k = (self.left, -1 - x) if x < 0 else (self.right, x - CX)
        return ref[k * CY : (k + 1) * CY, lanes]

    def first(self, x):
        return self._get(x, self.c1, slice(0, CZ))

    def w(self, x):
        return self._get(x, self.wc, slice(CZ, 2 * CZ))


Z_C, Z_P, Z_W, Z_Q, Z_R, Z_V, Z_S, Z_K = 0, 10, 20, 30, 38, 44, 50, 66
Z_ROWS = 72


def pack_c_kernel(b, w, f2, c1, wc, left, right, one, two, c2z, both):
    a = Coarse(c1, wc, left, right)
    lo, hi = both.at[0], both.at[1]
    second = {}
    for x in range(-3, 7):
        c, cw = a.first(x), a.w(x)
        second[x] = (1.0 + KEEP) * c + cw * (
            a.first(x - 1) + a.first(x + 1) + beside_z(c) + beside_y(c, 0.0, 0.0)
        )
        c2z[(x + 3) * CY : (x + 4) * CY, :] = second[x]
        for out, y in ((lo, 0), (hi, CY - 1)):
            for base, v in ((Z_C, c), (Z_P, second[x]), (Z_W, cw)):
                k = base + x + 3
                out[k : k + 1, :] = v[y : y + 1]
    for x in range(-2, 6):
        s, c, cw = second[x], a.first(x), a.w(x)
        below, above = shift_y(s, 0.0, 0.0)
        inner = {0: above, 1: below}
        for side, (out, y, y2) in enumerate(((lo, 0, 1), (hi, CY - 1, CY - 2))):
            k = Z_Q + x + 2
            out[k : k + 1, :] = (c + cw * inner[side])[y : y + 1]
        if -1 <= x <= 4:
            part = KEEP * s + c + cw * (second[x - 1] + second[x + 1] + beside_z(s))
            for side, (out, y, y2) in enumerate(((lo, 0, 1), (hi, CY - 1, CY - 2))):
                k = Z_R + x + 1
                out[k : k + 1, :] = (part + cw * inner[side])[y2 : y2 + 1]
                k = Z_V + x + 1
                out[k : k + 1, :] = cw[y2 : y2 + 1]
    for out, y, inner in ((lo, 0, 1), (hi, BY - 1, BY - 2)):
        for x in range(BX):
            at = (x + 1) * BY
            at_x = place(x)
            v = w[at_x][y : y + 1] * (b[at_x][y : y + 1] + f2[at + inner : at + inner + 1, :])
            for half in range(2):
                k = Z_S + 2 * x + half
                out[k : k + 1, :] = v[:, half * CZ : (half + 1) * CZ]
        for j, x in enumerate((-1, 8)):
            at = (x + 1) * BY + y
            v = f2[at : at + 1, :]
            for half in range(2):
                k = Z_K + 2 * j + half
                out[k : k + 1, :] = v[:, half * CZ : (half + 1) * CZ]
    give(both, one, two)


def last_kernel(
    b, w, left, right, first, second, f2, f2low, f2high, c1, wc, cleft, cright, c2z, one, two,
    out, both, cboth, col, line, line3, fine, corr, col2, s1, gline, g1line,
):
    a = Coarse(c1, wc, cleft, cright)
    wide = Wide(None, b, w, left, right)
    take(both, first, second)
    take(cboth, one, two)
    low, high, clow, chigh = both.at[0], both.at[1], cboth.at[0], cboth.at[1]
    crow = lax.broadcasted_iota(jnp.int32, (CY, CZ), 0)
    c2 = {}
    for x in range(-3, 7):
        k = Z_C + x + 3
        beyond = jnp.where(crow == 0, row(clow, k), jnp.where(crow == CY - 1, row(chigh, k), 0.0))
        c2[x] = slab(c2z, x + 3, CY) + a.w(x) * beyond
    sides = ((clow, 0), (chigh, CY - 1))
    for s, (side, y) in enumerate(sides):
        for x in range(-3, 7):
            col[x + 3 : x + 4, :] = a.first(x)[y : y + 1]
        line[s, 0:10, :] = side[Z_P : Z_P + 10, :] + side[Z_W : Z_W + 10, :] * col[0:10, :]
        for x in range(-2, 6):
            col[x + 2 : x + 3, :] = c2[x][y : y + 1]
        mid = line[s, 1:9, :]
        line3[s, 0:8, :] = (
            KEEP * mid
            + side[Z_Q : Z_Q + 8, :]
            + side[Z_W + 1 : Z_W + 9, :]
            * (line[s, 0:8, :] + line[s, 2:10, :] + beside_z(mid) + col[0:8, :])
        )
    c3 = {}
    for x in range(-2, 6):
        c = c2[x]
        c3[x] = KEEP * c + a.first(x) + a.w(x) * (
            c2[x - 1]
            + c2[x + 1]
            + beside_z(c)
            + beside_y(c, line[0, x + 3 : x + 4, :], line[1, x + 3 : x + 4, :])
        )
    for x in range(-1, 5):
        c = c3[x]
        c4 = KEEP * c + a.first(x) + a.w(x) * (
            c3[x - 1]
            + c3[x + 1]
            + beside_z(c)
            + beside_y(c, line3[0, x + 2 : x + 3, :], line3[1, x + 2 : x + 3, :])
        )
        fine[pl.ds((x + 1) * BY, CY, stride=2), :] = c4
        fine[pl.ds((x + 1) * BY + 1, CY, stride=2), :] = c4
    for s, (side, y) in enumerate(sides):
        for x in range(-1, 5):
            col[x + 1 : x + 2, :] = c3[x][y : y + 1]
        mid = line3[s, 1:7, :]
        third = side[Z_R : Z_R + 6, :] + side[Z_V : Z_V + 6, :] * line[s, 2:8, :]
        fine[6 * BY + 8 * s : 6 * BY + 8 * s + 6, :] = (
            KEEP * mid
            + side[Z_C + 2 : Z_C + 8, :]
            + side[Z_W + 2 : Z_W + 8, :]
            * (line3[s, 0:6, :] + line3[s, 2:8, :] + beside_z(mid) + third + col[0:6, :])
        )
        fine[6 * BY + 8 * s + 6 : 6 * BY + 8 * s + 8, :] = jnp.zeros((2, CZ), F32)
    corr[...] = lax.dot_general(
        fine[...],
        halved(CZ, NZ),
        (((1,), (0,)), ((), ())),
        precision=lax.Precision.HIGHEST,
        preferred_element_type=F32,
    )
    g0 = {}
    for x in range(-2, 10):
        if x == -2:
            f = slab(cleft, 2)
        elif x == 9:
            f = slab(a.right, 2)
        else:
            f = slab(f2, x + 1)
        g0[x] = f + slab(corr, (x + 2) // 2)
    for s, (cside, side, y, f2side) in enumerate(((clow, low, 0, f2low), (chigh, high, BY - 1, f2high))):
        base = 6 * BY + 8 * s
        for x in range(-1, 9):
            k = base + (x + 2) // 2
            col2[x + 1 : x + 2, :] = corr[k : k + 1, :]
        gline[s, 1:9, :] = f2side[...] + col2[1:9, :]
        for j, x in enumerate((-1, 8)):
            k = Z_K + 2 * j
            gline[s, x + 1 : x + 2, 0:CZ] = row(cside, k) + col2[x + 1 : x + 2, 0:CZ]
            gline[s, x + 1 : x + 2, CZ:] = row(cside, k + 1) + col2[x + 1 : x + 2, CZ:]
        for x in range(BX):
            k = Z_S + 2 * x
            s1[x : x + 1, 0:CZ] = row(cside, k)
            s1[x : x + 1, CZ:] = row(cside, k + 1)
        moved = col2[1:9, :]
        for x in range(BX):
            col2[x : x + 1, :] = g0[x][y : y + 1]
        mid = gline[s, 1:9, :]
        g1line[s, 0:8, :] = (
            KEEP * mid
            + s1[0:8, :]
            + side[Y_W + 1 : Y_W + 9, :]
            * (moved + gline[s, 0:8, :] + gline[s, 2:10, :] + beside_z(mid) + col2[0:8, :])
        )
    g1 = {}
    for x in range(-1, 9):
        f = g0[x]
        g1[x] = KEEP * f + wide.w(x) * (
            wide.rhs(x)
            + g0[x - 1]
            + g0[x + 1]
            + beside_z(f)
            + beside_y(f, gline[0, x + 1 : x + 2, :], gline[1, x + 1 : x + 2, :])
        )
    for x in range(BX):
        f = g1[x]
        out[place(x)] = KEEP * f + wide.w(x) * (
            wide.rhs(x)
            + g1[x - 1]
            + g1[x + 1]
            + beside_z(f)
            + beside_y(f, g1line[0, x : x + 1, :], g1line[1, x : x + 1, :])
        )


def swap(v, axis, start):
    pairs = [(i, i + 1) for i in range(start, lax.axis_size(axis) - 1, 2)]
    return lax.ppermute(v, axis, pairs + [(j, i) for i, j in pairs])


def exchange(first, second, axis):
    groups = [[i, i + 1] for i in range(0, lax.axis_size(axis), 2)]
    return swap(first, axis, 1), lax.all_gather(second, axis, axis_index_groups=groups)


def body(g, b, n):
    block = (BX, BY, NZ)
    cross, chip, g, b, w, d = call(
        load_kernel,
        [(7 * BY, NZ)] * 2 + [block] * 4,
        g, b, n,
        hbm=3,
        vmem=None,
        scratch=[pltpu.VMEM(block, jnp.int32), pltpu.SemaphoreType.DMA((3,))],
    )
    left, right = exchange(cross, chip, "group")
    first, second, f1z = call(
        pack_y_kernel,
        [(Y_ROWS, NZ)] * 2 + [(12 * BY, NZ)],
        g, b, w, left, right,
        scratch=[(2, Y_ROWS, NZ)],
    )
    first, second = exchange(first, second, "dev")
    f2, f2low, f2high, c1, wc, cross, chip = call(
        middle_kernel,
        [(10 * BY, NZ), (BX, NZ), (BX, NZ), (CX * CY, CZ), (CX * CY, CZ), (X2_ROWS, NZ), (X2_ROWS, NZ)],
        g, b, w, d, left, right, f1z, first, second,
        scratch=[(2, Y_ROWS, NZ), (16, NZ), (2, 16, NZ), (8 * BY, CZ)],
    )
    cleft, cright = exchange(cross, chip, "group")
    one, two, c2z = call(
        pack_c_kernel,
        [(Z_ROWS, CZ)] * 2 + [(10 * CY, CZ)],
        b, w, f2, c1, wc, cleft, cright,
        scratch=[(2, Z_ROWS, CZ)],
    )
    one, two = exchange(one, two, "dev")
    (out,) = call(
        last_kernel,
        [block],
        b, w, left, right, first, second, f2, f2low, f2high, c1, wc, cleft, cright, c2z, one, two,
        scratch=[
            (2, Y_ROWS, NZ), (2, Z_ROWS, CZ),
            (16, CZ), (2, 16, CZ), (2, 8, CZ), (6 * BY + 16, CZ), (6 * BY + 16, NZ), (16, NZ), (8, NZ), (2, 16, NZ), (2, 8, NZ),
        ],
        hbm_out=True,
    )
    return out


def solution(mesh):
    s = P("group", "dev", None)
    return jax.shard_map(body, mesh=mesh, in_specs=(s, s, s), out_specs=s, check_vma=False)
```

```python
import jax
import jax.numpy as jnp
from jax import lax
from jax.sharding import PartitionSpec as P
from jax.experimental import pallas as pl
from jax.experimental.pallas import tpu as pltpu

OMEGA = 0.8
KEEP = 1.0 - OMEGA
VM = pl.BlockSpec(memory_space=pltpu.VMEM)
F32 = jnp.float32
BX, BY, NZ = 8, 16, 256
CX, CY, CZ = 4, 8, 128


def call(kernel, outs, *args, scratch=(), hbm=0, hbm_out=False, vmem=8 * 2**20):
    make = jax.ShapeDtypeStruct if hbm_out else pltpu.VMEM
    return pl.pallas_call(
        kernel,
        out_shape=[make(s, F32) for s in outs],
        in_specs=[pl.BlockSpec(memory_space=pltpu.HBM)] * hbm + [VM] * (len(args) - hbm),
        out_specs=[VM] * len(outs),
        scratch_shapes=[pltpu.VMEM(s, F32) if isinstance(s, tuple) else s for s in scratch],
        compiler_params=pltpu.CompilerParams(vmem_limit_bytes=vmem),
    )(*args)


def beside_z(v):
    lane = lax.broadcasted_iota(jnp.int32, v.shape, 1)
    last = v.shape[1] - 1
    below = jnp.where(lane == 0, 0.0, pltpu.roll(v, 1, 1))
    above = jnp.where(lane == last, 0.0, pltpu.roll(v, last, 1))
    return below + above


def shift_y(v, low, high):
    row = lax.broadcasted_iota(jnp.int32, v.shape, 0)
    last = v.shape[0] - 1
    below = jnp.where(row == 0, low, pltpu.roll(v, 1, 0))
    above = jnp.where(row == last, high, pltpu.roll(v, last, 0))
    return below, above


def beside_y(v, low, high):
    below, above = shift_y(v, low, high)
    return below + above


def slab(ref, k, rows=BY):
    return ref[k * rows : (k + 1) * rows, :]


def row(ref, k):
    return ref[k : k + 1, :]


def halved(n, m):
    a = lax.broadcasted_iota(jnp.int32, (n, m), 0)
    b = lax.broadcasted_iota(jnp.int32, (n, m), 1)
    return jnp.where((a // 2 == b) if n > m else (a == b // 2), 1.0, 0.0).astype(F32)


def diag_of(n):
    return 6.0 + 0.25 * n.astype(F32)


def place(x):
    odd = lax.axis_index("group") % 2
    return x + odd * (BX - 1 - 2 * x)


def partner(ref):
    return ref.at[1 - lax.axis_index("group") % 2]


def side_of_dev():
    return lax.axis_index("dev") % 2


def load_kernel(g_hbm, b_hbm, n_hbm, cross, chip, g, b, w, d, n, sems):
    copies = [
        pltpu.make_async_copy(src, dst, sems.at[k])
        for k, (src, dst) in enumerate(((g_hbm, g), (b_hbm, b), (n_hbm, n)))
    ]
    for c in copies:
        c.start()
    for c in copies:
        c.wait()
    for x in range(BX):
        diag = diag_of(n[x])
        d[x] = diag
        w[x] = OMEGA / diag
    for out, layers in ((cross, (0, 1, 2)), (chip, (7, 6, 5))):
        for k in range(3):
            out[k * BY : (k + 1) * BY, :] = g[place(layers[k])]
        for k in range(2):
            out[(3 + k) * BY : (4 + k) * BY, :] = w[place(layers[k])]
            out[(5 + k) * BY : (6 + k) * BY, :] = b[place(layers[k])]


class Wide:
    def __init__(self, g, b, w, left, right):
        self.own, self.left, self.right = (g, w, b), left, partner(right)

    def _get(self, which, base, x):
        if 0 <= x < BX:
            return self.own[which][place(x)]
        ref, k = (self.left, -1 - x) if x < 0 else (self.right, x - BX)
        return slab(ref, base + k)

    def guess(self, x):
        return self._get(0, 0, x)

    def w(self, x):
        return self._get(1, 3, x)

    def rhs(self, x):
        return self._get(2, 5, x)


def give(both, even, odd):
    p = side_of_dev()
    even[...] = both[1 - p]
    odd[...] = both[p]


def take(both, even, odd):
    p = side_of_dev()
    at = lax.axis_index("dev")
    at_end = (at == 0) | (at == lax.axis_size("dev") - 1)
    both[1 - p] = even[...]
    both[p] = jnp.where(at_end, 0.0, odd[p])


Y_G, Y_P, Y_W, Y_Q = 0, 12, 22, 32
Y_ROWS = 40


def pack_y_kernel(g, b, w, left, right, first, second, f1z, both):
    a = Wide(g, b, w, left, right)
    lo, hi = both.at[0], both.at[1]
    for x in range(-2, 10):
        here = a.guess(x)
        f = KEEP * here + a.w(x) * (
            a.rhs(x) + a.guess(x - 1) + a.guess(x + 1) + beside_z(here) + beside_y(here, 0.0, 0.0)
        )
        f1z[(x + 2) * BY : (x + 3) * BY, :] = f
        for out, y, inner in ((lo, 0, 1), (hi, BY - 1, BY - 2)):
            k = Y_G + x + 2
            out[k : k + 1, :] = here[y : y + 1]
            if -1 <= x <= 8:
                k = Y_P + x + 1
                out[k : k + 1, :] = f[y : y + 1]
                k = Y_W + x + 1
                out[k : k + 1, :] = a.w(x)[y : y + 1]
            if 0 <= x <= 7:
                k = Y_Q + x
                out[k : k + 1, :] = a.w(x)[y : y + 1] * (a.rhs(x)[y : y + 1] + f[inner : inner + 1])
    give(both, first, second)


X2_ROWS = 3 * BY


def middle_kernel(
    g, b, w, d, left, right, f1z, first, second, f2, f2low, f2high, c1, wc, lo, hi, both, col, line, sums
):
    a = Wide(g, b, w, left, right)
    take(both, first, second)
    low, high = both.at[0], both.at[1]
    rows = lax.broadcasted_iota(jnp.int32, (BY, NZ), 0)
    f1 = {}
    for x in range(-2, 10):
        k = Y_G + x + 2
        beyond = jnp.where(rows == 0, row(low, k), jnp.where(rows == BY - 1, row(high, k), 0.0))
        f1[x] = slab(f1z, x + 2) + a.w(x) * beyond
    for s, (side, y, out) in enumerate(((low, 0, f2low), (high, BY - 1, f2high))):
        for x in range(-1, 9):
            col[x + 1 : x + 2, :] = a.guess(x)[y : y + 1]
        line[s, 0:10, :] = side[Y_P : Y_P + 10, :] + side[Y_W : Y_W + 10, :] * col[0:10, :]
        for x in range(0, 8):
            col[x : x + 1, :] = f1[x][y : y + 1]
        mid = line[s, 1:9, :]
        out[...] = (
            KEEP * mid
            + side[Y_Q : Y_Q + 8, :]
            + side[Y_W + 1 : Y_W + 9, :]
            * (line[s, 0:8, :] + line[s, 2:10, :] + beside_z(mid) + col[0:8, :])
        )
    sec = {}
    for x in range(-1, 9):
        f = f1[x]
        sec[x] = KEEP * f + a.w(x) * (
            a.rhs(x)
            + f1[x - 1]
            + f1[x + 1]
            + beside_z(f)
            + beside_y(f, line[0, x + 1 : x + 2, :], line[1, x + 1 : x + 2, :])
        )
        f2[(x + 1) * BY : (x + 2) * BY, :] = sec[x]
    lo[2 * BY :, :] = sec[1]
    hi[2 * BY :, :] = sec[6]
    pairs, points = [], []
    for x in range(0, 8):
        f = sec[x]
        r = (
            a.rhs(x)
            - d[place(x)] * f
            + sec[x - 1]
            + sec[x + 1]
            + beside_z(f)
            + beside_y(f, row(f2low, x), row(f2high, x))
        )
        if x % 2:
            pairs[-1] = pairs[-1] + r
            points[-1] = points[-1] + d[place(x)]
        else:
            pairs.append(r)
            points.append(d[place(x)])
    sums[...] = lax.dot_general(
        jnp.concatenate(pairs + points, axis=0),
        halved(NZ, CZ),
        (((1,), (0,)), ((), ())),
        precision=lax.Precision.HIGHEST,
        preferred_element_type=F32,
    )
    for x in range(CX):
        at = x * BY
        total = sums[pl.ds(at, CY, stride=2), :] + sums[pl.ds(at + 1, CY, stride=2), :]
        at = (CX + x) * BY
        diags = sums[pl.ds(at, CY, stride=2), :] + sums[pl.ds(at + 1, CY, stride=2), :]
        weight = OMEGA / (0.5 * diags - 18.0)
        first = weight * (0.5 * total)
        c1[x * CY : (x + 1) * CY, :] = first
        wc[x * CY : (x + 1) * CY, :] = weight
        for out, k in ((lo, x), (hi, CX - 1 - x)):
            out[k * CY : (k + 1) * CY, 0:CZ] = first
            out[k * CY : (k + 1) * CY, CZ:] = weight


class Coarse:
    def __init__(self, c1, wc, left, right):
        self.c1, self.wc, self.left, self.right = c1, wc, left, partner(right)

    def _get(self, x, own, lanes):
        if 0 <= x < CX:
            return slab(own, x, CY)
        ref, k = (self.left, -1 - x) if x < 0 else (self.right, x - CX)
        return ref[k * CY : (k + 1) * CY, lanes]

    def first(self, x):
        return self._get(x, self.c1, slice(0, CZ))

    def w(self, x):
        return self._get(x, self.wc, slice(CZ, 2 * CZ))


Z_C, Z_P, Z_W, Z_Q, Z_R, Z_V, Z_S, Z_K = 0, 10, 20, 30, 38, 44, 50, 66
Z_ROWS = 72


def pack_c_kernel(b, w, f2, c1, wc, left, right, one, two, c2z, both):
    a = Coarse(c1, wc, left, right)
    lo, hi = both.at[0], both.at[1]
    second = {}
    for x in range(-3, 7):
        c, cw = a.first(x), a.w(x)
        second[x] = (1.0 + KEEP) * c + cw * (
            a.first(x - 1) + a.first(x + 1) + beside_z(c) + beside_y(c, 0.0, 0.0)
        )
        c2z[(x + 3) * CY : (x + 4) * CY, :] = second[x]
        for out, y in ((lo, 0), (hi, CY - 1)):
            for base, v in ((Z_C, c), (Z_P, second[x]), (Z_W, cw)):
                k = base + x + 3
                out[k : k + 1, :] = v[y : y + 1]
    for x in range(-2, 6):
        s, c, cw = second[x], a.first(x), a.w(x)
        below, above = shift_y(s, 0.0, 0.0)
        inner = {0: above, 1: below}
        for side, (out, y, y2) in enumerate(((lo, 0, 1), (hi, CY - 1, CY - 2))):
            k = Z_Q + x + 2
            out[k : k + 1, :] = (c + cw * inner[side])[y : y + 1]
        if -1 <= x <= 4:
            part = KEEP * s + c + cw * (second[x - 1] + second[x + 1] + beside_z(s))
            for side, (out, y, y2) in enumerate(((lo, 0, 1), (hi, CY - 1, CY - 2))):
                k = Z_R + x + 1
                out[k : k + 1, :] = (part + cw * inner[side])[y2 : y2 + 1]
                k = Z_V + x + 1
                out[k : k + 1, :] = cw[y2 : y2 + 1]
    for out, y, inner in ((lo, 0, 1), (hi, BY - 1, BY - 2)):
        for x in range(BX):
            at = (x + 1) * BY
            at_x = place(x)
            v = w[at_x][y : y + 1] * (b[at_x][y : y + 1] + f2[at + inner : at + inner + 1, :])
            for half in range(2):
                k = Z_S + 2 * x + half
                out[k : k + 1, :] = v[:, half * CZ : (half + 1) * CZ]
        for j, x in enumerate((-1, 8)):
            at = (x + 1) * BY + y
            v = f2[at : at + 1, :]
            for half in range(2):
                k = Z_K + 2 * j + half
                out[k : k + 1, :] = v[:, half * CZ : (half + 1) * CZ]
    give(both, one, two)


def last_kernel(
    b, w, left, right, first, second, f2, f2low, f2high, c1, wc, cleft, cright, c2z, one, two,
    out, both, cboth, col, line, line3, fine, corr, col2, s1, gline, g1line,
):
    a = Coarse(c1, wc, cleft, cright)
    wide = Wide(None, b, w, left, right)
    take(both, first, second)
    take(cboth, one, two)
    low, high, clow, chigh = both.at[0], both.at[1], cboth.at[0], cboth.at[1]
    crow = lax.broadcasted_iota(jnp.int32, (CY, CZ), 0)
    c2 = {}
    for x in range(-3, 7):
        k = Z_C + x + 3
        beyond = jnp.where(crow == 0, row(clow, k), jnp.where(crow == CY - 1, row(chigh, k), 0.0))
        c2[x] = slab(c2z, x + 3, CY) + a.w(x) * beyond
    sides = ((clow, 0), (chigh, CY - 1))
    for s, (side, y) in enumerate(sides):
        for x in range(-3, 7):
            col[x + 3 : x + 4, :] = a.first(x)[y : y + 1]
        line[s, 0:10, :] = side[Z_P : Z_P + 10, :] + side[Z_W : Z_W + 10, :] * col[0:10, :]
        for x in range(-2, 6):
            col[x + 2 : x + 3, :] = c2[x][y : y + 1]
        mid = line[s, 1:9, :]
        line3[s, 0:8, :] = (
            KEEP * mid
            + side[Z_Q : Z_Q + 8, :]
            + side[Z_W + 1 : Z_W + 9, :]
            * (line[s, 0:8, :] + line[s, 2:10, :] + beside_z(mid) + col[0:8, :])
        )
    c3 = {}
    for x in range(-2, 6):
        c = c2[x]
        c3[x] = KEEP * c + a.first(x) + a.w(x) * (
            c2[x - 1]
            + c2[x + 1]
            + beside_z(c)
            + beside_y(c, line[0, x + 3 : x + 4, :], line[1, x + 3 : x + 4, :])
        )
    for x in range(-1, 5):
        c = c3[x]
        c4 = KEEP * c + a.first(x) + a.w(x) * (
            c3[x - 1]
            + c3[x + 1]
            + beside_z(c)
            + beside_y(c, line3[0, x + 2 : x + 3, :], line3[1, x + 2 : x + 3, :])
        )
        fine[pl.ds((x + 1) * BY, CY, stride=2), :] = c4
        fine[pl.ds((x + 1) * BY + 1, CY, stride=2), :] = c4
    for s, (side, y) in enumerate(sides):
        for x in range(-1, 5):
            col[x + 1 : x + 2, :] = c3[x][y : y + 1]
        mid = line3[s, 1:7, :]
        third = side[Z_R : Z_R + 6, :] + side[Z_V : Z_V + 6, :] * line[s, 2:8, :]
        fine[6 * BY + 8 * s : 6 * BY + 8 * s + 6, :] = (
            KEEP * mid
            + side[Z_C + 2 : Z_C + 8, :]
            + side[Z_W + 2 : Z_W + 8, :]
            * (line3[s, 0:6, :] + line3[s, 2:8, :] + beside_z(mid) + third + col[0:6, :])
        )
        fine[6 * BY + 8 * s + 6 : 6 * BY + 8 * s + 8, :] = jnp.zeros((2, CZ), F32)
    corr[...] = lax.dot_general(
        fine[...],
        halved(CZ, NZ),
        (((1,), (0,)), ((), ())),
        precision=lax.Precision.HIGHEST,
        preferred_element_type=F32,
    )
    g0 = {}
    for x in range(-2, 10):
        if x == -2:
            f = slab(cleft, 2)
        elif x == 9:
            f = slab(a.right, 2)
        else:
            f = slab(f2, x + 1)
        g0[x] = f + slab(corr, (x + 2) // 2)
    for s, (cside, side, y, f2side) in enumerate(((clow, low, 0, f2low), (chigh, high, BY - 1, f2high))):
        base = 6 * BY + 8 * s
        for x in range(-1, 9):
            k = base + (x + 2) // 2
            col2[x + 1 : x + 2, :] = corr[k : k + 1, :]
        gline[s, 1:9, :] = f2side[...] + col2[1:9, :]
        for j, x in enumerate((-1, 8)):
            k = Z_K + 2 * j
            gline[s, x + 1 : x + 2, 0:CZ] = row(cside, k) + col2[x + 1 : x + 2, 0:CZ]
            gline[s, x + 1 : x + 2, CZ:] = row(cside, k + 1) + col2[x + 1 : x + 2, CZ:]
        for x in range(BX):
            k = Z_S + 2 * x
            s1[x : x + 1, 0:CZ] = row(cside, k)
            s1[x : x + 1, CZ:] = row(cside, k + 1)
        moved = col2[1:9, :]
        for x in range(BX):
            col2[x : x + 1, :] = g0[x][y : y + 1]
        mid = gline[s, 1:9, :]
        g1line[s, 0:8, :] = (
            KEEP * mid
            + s1[0:8, :]
            + side[Y_W + 1 : Y_W + 9, :]
            * (moved + gline[s, 0:8, :] + gline[s, 2:10, :] + beside_z(mid) + col2[0:8, :])
        )
    g1 = {}
    for x in range(-1, 9):
        f = g0[x]
        g1[x] = KEEP * f + wide.w(x) * (
            wide.rhs(x)
            + g0[x - 1]
            + g0[x + 1]
            + beside_z(f)
            + beside_y(f, gline[0, x + 1 : x + 2, :], gline[1, x + 1 : x + 2, :])
        )
    for x in range(BX):
        f = g1[x]
        out[place(x)] = KEEP * f + wide.w(x) * (
            wide.rhs(x)
            + g1[x - 1]
            + g1[x + 1]
            + beside_z(f)
            + beside_y(f, g1line[0, x : x + 1, :], g1line[1, x : x + 1, :])
        )


def swap(v, axis, start):
    pairs = [(i, i + 1) for i in range(start, lax.axis_size(axis) - 1, 2)]
    return lax.ppermute(v, axis, pairs + [(j, i) for i, j in pairs])


def exchange_group(cross, chip):
    groups = [[i, i + 1] for i in range(0, lax.axis_size("group"), 2)]
    return swap(cross, "group", 1), lax.all_gather(chip, "group", axis_index_groups=groups)


def exchange_dev(even, odd):
    n = lax.axis_size("dev")
    groups = [[i, (i + 1) % n] for i in range(1, n, 2)]
    return swap(even, "dev", 0), lax.all_gather(odd, "dev", axis_index_groups=groups)


def body(g, b, n):
    block = (BX, BY, NZ)
    cross, chip, g, b, w, d = call(
        load_kernel,
        [(7 * BY, NZ)] * 2 + [block] * 4,
        g, b, n,
        hbm=3,
        vmem=None,
        scratch=[pltpu.VMEM(block, jnp.int32), pltpu.SemaphoreType.DMA((3,))],
    )
    left, right = exchange_group(cross, chip)
    first, second, f1z = call(
        pack_y_kernel,
        [(Y_ROWS, NZ)] * 2 + [(12 * BY, NZ)],
        g, b, w, left, right,
        scratch=[(2, Y_ROWS, NZ)],
    )
    first, second = exchange_dev(first, second)
    f2, f2low, f2high, c1, wc, cross, chip = call(
        middle_kernel,
        [(10 * BY, NZ), (BX, NZ), (BX, NZ), (CX * CY, CZ), (CX * CY, CZ), (X2_ROWS, NZ), (X2_ROWS, NZ)],
        g, b, w, d, left, right, f1z, first, second,
        scratch=[(2, Y_ROWS, NZ), (16, NZ), (2, 16, NZ), (8 * BY, CZ)],
    )
    cleft, cright = exchange_group(cross, chip)
    one, two, c2z = call(
        pack_c_kernel,
        [(Z_ROWS, CZ)] * 2 + [(10 * CY, CZ)],
        b, w, f2, c1, wc, cleft, cright,
        scratch=[(2, Z_ROWS, CZ)],
    )
    one, two = exchange_dev(one, two)
    (out,) = call(
        last_kernel,
        [block],
        b, w, left, right, first, second, f2, f2low, f2high, c1, wc, cleft, cright, c2z, one, two,
        scratch=[
            (2, Y_ROWS, NZ), (2, Z_ROWS, CZ),
            (16, CZ), (2, 16, CZ), (2, 8, CZ), (6 * BY + 16, CZ), (6 * BY + 16, NZ), (16, NZ), (8, NZ), (2, 16, NZ), (2, 8, NZ),
        ],
        hbm_out=True,
    )
    return out


def solution(mesh):
    s = P("group", "dev", None)
    return jax.shard_map(body, mesh=mesh, in_specs=(s, s, s), out_specs=s, check_vma=False)
```

```python
import jax
import jax.numpy as jnp
from jax import lax
from jax.sharding import PartitionSpec as P
from jax.experimental import pallas as pl
from jax.experimental.pallas import tpu as pltpu

OMEGA = 0.8
KEEP = 1.0 - OMEGA
VM = pl.BlockSpec(memory_space=pltpu.VMEM)
F32 = jnp.float32
BX, BY, NZ = 8, 16, 256
CX, CY, CZ = 4, 8, 128
RUN = 32


def call(kernel, outs, *args, scratch=(), hbm=0, hbm_out=False, vmem=8 * 2**20, cost=None):
    make = jax.ShapeDtypeStruct if hbm_out else pltpu.VMEM
    return pl.pallas_call(
        kernel,
        out_shape=[make(s, F32) for s in outs],
        in_specs=[pl.BlockSpec(memory_space=pltpu.HBM)] * hbm + [VM] * (len(args) - hbm),
        out_specs=[VM] * len(outs),
        scratch_shapes=[pltpu.VMEM(s, F32) if isinstance(s, tuple) else s for s in scratch],
        compiler_params=pltpu.CompilerParams(vmem_limit_bytes=vmem),
        cost_estimate=cost,
    )(*args)


def beside_z(v):
    lane = lax.broadcasted_iota(jnp.int32, v.shape, 1)
    last = v.shape[1] - 1
    below = jnp.where(lane == 0, 0.0, pltpu.roll(v, 1, 1))
    above = jnp.where(lane == last, 0.0, pltpu.roll(v, last, 1))
    return below + above


def shift_y(v, low, high):
    row = lax.broadcasted_iota(jnp.int32, v.shape, 0)
    last = v.shape[0] - 1
    below = jnp.where(row == 0, low, pltpu.roll(v, 1, 0))
    above = jnp.where(row == last, high, pltpu.roll(v, last, 0))
    return below, above


def beside_y(v, low, high):
    below, above = shift_y(v, low, high)
    return below + above


def slab(ref, k, rows=BY):
    return ref[k * rows : (k + 1) * rows, :]


def row(ref, k):
    return ref[k : k + 1, :]


def halved(n, m):
    a = lax.broadcasted_iota(jnp.int32, (n, m), 0)
    b = lax.broadcasted_iota(jnp.int32, (n, m), 1)
    return jnp.where((a // 2 == b) if n > m else (a == b // 2), 1.0, 0.0).astype(F32)


def lanes(v, index):
    return jnp.take_along_axis(v, index, axis=1)


def pair_z(v):
    lane = lax.broadcasted_iota(jnp.int32, (v.shape[0], CZ), 1)
    low, high = v[:, :CZ], v[:, CZ:]
    low = low + pltpu.roll(low, CZ - 1, 1)
    high = high + pltpu.roll(high, CZ - 1, 1)
    index = (2 * lane) % CZ
    return jnp.where(lane < CZ // 2, lanes(low, index), lanes(high, index))


def diag_of(n):
    return 6.0 + 0.25 * n.astype(F32)


def place(x):
    odd = lax.axis_index("group") % 2
    return x + odd * (BX - 1 - 2 * x)


def partner(ref):
    return ref.at[1 - lax.axis_index("group") % 2]


def side_of_dev():
    return lax.axis_index("dev") % 2


Y_G, Y_P, Y_W, Y_Q, Y_G2, Y_W2 = 0, 8, 16, 24, 32, 34
Y_ROWS = 40
X_ROWS = 7 * BY


def load_kernel(g_hbm, b_hbm, n_hbm, cross, cross2, chip, even, even2, odd, f1z, g, b, w, d, n, both, sems):
    copies = [
        pltpu.make_async_copy(src, dst, sems.at[k])
        for k, (src, dst) in enumerate(((g_hbm, g), (b_hbm, b), (n_hbm, n)))
    ]
    for c in copies:
        c.start()
    for c in copies:
        c.wait()
    for x in range(BX):
        diag = diag_of(n[x])
        d[x] = diag
        w[x] = OMEGA / diag
    for out, layers in ((cross, (0, 1, 2)), (chip, (7, 6, 5))):
        for k in range(3):
            out[k * BY : (k + 1) * BY, :] = g[place(layers[k])]
        for k in range(2):
            out[(3 + k) * BY : (4 + k) * BY, :] = w[place(layers[k])]
            out[(5 + k) * BY : (6 + k) * BY, :] = b[place(layers[k])]
    zero = jnp.zeros((BY, NZ), F32)
    for x in range(BX):
        at = place(x)
        here, wx, bx = g[at], w[at], b[at]
        before = g[place(x - 1)] if x else zero
        after = g[place(x + 1)] if x < BX - 1 else zero
        f = KEEP * here + wx * (bx + before + after + beside_z(here) + beside_y(here, 0.0, 0.0))
        f1z[x * BY : (x + 1) * BY, :] = f
        for s, (y, inner) in enumerate(((0, 1), (BY - 1, BY - 2))):
            rows = [
                (Y_G + x, here[y : y + 1]),
                (Y_P + x, f[y : y + 1]),
                (Y_W + x, wx[y : y + 1]),
                (Y_Q + x, wx[y : y + 1] * (bx[y : y + 1] + f[inner : inner + 1])),
            ]
            if x in (0, 7):
                rows += [(Y_G2 + x // 7, here[inner : inner + 1]), (Y_W2 + x // 7, wx[inner : inner + 1])]
            for k, v in rows:
                both[s, k : k + 1, :] = v
    p = side_of_dev()
    cross2[...] = cross[...]
    even[...] = both[1 - p]
    even2[...] = both[1 - p]
    odd[...] = both[p]


class Wide:
    def __init__(self, g, b, w, left, right):
        self.own, self.left, self.right = (g, w, b), left, partner(right)

    def _get(self, which, base, x, y):
        if 0 <= x < BX:
            v = self.own[which]
            return v[place(x)] if y is None else v[place(x), y : y + 1, :]
        ref, k = (self.left, -1 - x) if x < 0 else (self.right, x - BX)
        return slab(ref, base + k) if y is None else row(ref, (base + k) * BY + y)

    def guess(self, x, y=None):
        return self._get(0, 0, x, y)

    def w(self, x, y=None):
        return self._get(1, 3, x, y)

    def rhs(self, x, y=None):
        return self._get(2, 5, x, y)


def take(both, even, odd):
    p = side_of_dev()
    both[1 - p] = even
    both[p] = odd


def gather_kernel(cross, even, odd, left, both):
    left[...] = cross[...]
    take(both, even[...], odd[...])


X2_D = 3 * BY
X2_ROWS = X2_D + 16


def diagonal_rows(edge):
    at, inner = (0, 1) if edge == 0 else (7, 6)
    return (Y_G + at, Y_G2 + edge, Y_G + inner, Y_P + at, Y_W + at, Y_W2 + edge, Y_W + inner)


def middle_kernel(
    g, b, w, d, left1, cross2, chip, f1z, both1, even2,
    f2, f2low, f2high, c1, wc, left, both, lo, hi, col, line, sums,
):
    left[...] = left1[...] + cross2[...]
    a = Wide(g, b, w, left, chip)
    p = side_of_dev()
    both[p] = both1[p]
    both[1 - p] = both1[1 - p] + even2[...]
    low, high = both.at[0], both.at[1]
    rows = lax.broadcasted_iota(jnp.int32, (BY, NZ), 0)
    f1 = {}
    for x in range(-2, 10):
        if 0 <= x < BX:
            k = Y_G + x
            beyond = jnp.where(rows == 0, row(low, k), jnp.where(rows == BY - 1, row(high, k), 0.0))
            if x == 0:
                beyond = beyond + a.guess(-1)
            if x == BX - 1:
                beyond = beyond + a.guess(BX)
            f1[x] = slab(f1z, x) + a.w(x) * beyond
        else:
            here = a.guess(x)
            f1[x] = KEEP * here + a.w(x) * (
                a.rhs(x) + a.guess(x - 1) + a.guess(x + 1) + beside_z(here) + beside_y(here, 0.0, 0.0)
            )
    for s, (side, y, out) in enumerate(((low, 0, f2low), (high, BY - 1, f2high))):
        for x in range(BX):
            col[x : x + 1, :] = a.guess(x, y)
        line[s, 0:16, :] = jnp.zeros((16, NZ), F32)
        line[s, 1:9, :] = side[Y_P : Y_P + 8, :] + side[Y_W : Y_W + 8, :] * col[0:8, :]
        for x in range(BX):
            col[x : x + 1, :] = f1[x][y : y + 1]
        mid = line[s, 1:9, :]
        out[...] = (
            KEEP * mid
            + side[Y_Q : Y_Q + 8, :]
            + side[Y_W : Y_W + 8, :] * (line[s, 0:8, :] + line[s, 2:10, :] + beside_z(mid) + col[0:8, :])
        )
        for edge, pack in enumerate((lo, hi)):
            for k, r in enumerate(diagonal_rows(edge)):
                at = X2_D + 7 * s + k
                pack[at : at + 1, :] = row(side, r)
    for pack in (lo, hi):
        pack[X2_D + 14 :, :] = jnp.zeros((2, NZ), F32)
    sec = {}
    for x in range(-1, 9):
        f = f1[x]
        sec[x] = KEEP * f + a.w(x) * (
            a.rhs(x)
            + f1[x - 1]
            + f1[x + 1]
            + beside_z(f)
            + beside_y(f, line[0, x + 1 : x + 2, :], line[1, x + 1 : x + 2, :])
        )
        f2[(x + 1) * BY : (x + 2) * BY, :] = sec[x]
    lo[2 * BY : X2_D, :] = sec[1]
    hi[2 * BY : X2_D, :] = sec[6]
    pairs, points = [], []
    for x in range(0, 8):
        f = sec[x]
        r = (
            a.rhs(x)
            - d[place(x)] * f
            + sec[x - 1]
            + sec[x + 1]
            + beside_z(f)
            + beside_y(f, row(f2low, x), row(f2high, x))
        )
        if x % 2:
            pairs[-1] = pairs[-1] + r
            points[-1] = points[-1] + d[place(x)]
        else:
            pairs.append(r)
            points.append(d[place(x)])
    sums[...] = lax.dot_general(
        jnp.concatenate(pairs + points, axis=0),
        halved(NZ, CZ),
        (((1,), (0,)), ((), ())),
        precision=lax.Precision.HIGHEST,
        preferred_element_type=F32,
    )
    for x in range(CX):
        at = x * BY
        total = sums[pl.ds(at, CY, stride=2), :] + sums[pl.ds(at + 1, CY, stride=2), :]
        at = (CX + x) * BY
        diags = sums[pl.ds(at, CY, stride=2), :] + sums[pl.ds(at + 1, CY, stride=2), :]
        weight = OMEGA / (0.5 * diags - 18.0)
        first = weight * (0.5 * total)
        c1[x * CY : (x + 1) * CY, :] = first
        wc[x * CY : (x + 1) * CY, :] = weight
        for out, k in ((lo, x), (hi, CX - 1 - x)):
            out[k * CY : (k + 1) * CY, 0:CZ] = first
            out[k * CY : (k + 1) * CY, CZ:] = weight


class Coarse:
    def __init__(self, c1x, wc, left, right):
        self.c1x, self.wc, self.left, self.right = c1x, wc, left, right

    def first(self, x):
        return slab(self.c1x, x + CX, CY)

    def w(self, x):
        if 0 <= x < CX:
            return slab(self.wc, x, CY)
        ref, k = (self.left, -1 - x) if x < 0 else (self.right, x - CX)
        return ref[k * CY : (k + 1) * CY, CZ:]


def corner_terms(a, low, high, relays, put):
    for e, (xe, xi, xn, xm) in enumerate(((0, 1, -1, -2), (7, 6, 8, 9))):
        for s, (side, y, yi) in enumerate(((low, 0, 1), (high, BY - 1, BY - 2))):
            own = [row(side, r) for r in diagonal_rows(e)]
            far = [row(relays[e], X2_D + 7 * s + k) for k in range(7)]
            corner, beside = a.guess(xe, y), a.guess(xn, y)
            w_corner, w_beside = a.w(xe, y), a.w(xn, y)
            put(2 * e + s, far[:5] + [beside + own[0], w_beside, a.w(xm, y), a.w(xn, yi), own[4], own[5], own[6], w_corner])
            put(4 + 2 * e + s, own[:5] + [corner + far[0], w_corner, a.w(xi, y), a.w(xe, yi), far[4], far[5], far[6], w_beside])


def corner_sums(t):
    g1, g2, g3, part, wd, near, wx, wx2, wxs, wy, wy2, wys, wq = (t[k] for k in range(13))
    dq = jnp.where(wq > 0.0, OMEGA / jnp.where(wq > 0.0, wq, 1.0), 0.0)
    by_y = wy * g1
    by_x = wx * g1
    diagonal = part + wd * near
    at_q = wq * (by_x + by_y)
    at_y = KEEP * by_y + wy * (beside_z(by_y) + diagonal + wy2 * g2)
    at_x = KEEP * by_x + wx * (beside_z(by_x) + diagonal + wx2 * g3)
    at_ys = wys * by_y
    at_xs = wxs * by_x
    total = at_y + at_x + beside_z(at_q) - dq * at_q + 2.0 * at_q + at_ys + at_xs
    return at_q, at_y, at_x, at_ys, at_xs, 0.5 * pair_z(total)


Z_C, Z_P, Z_W, Z_Q, Z_R, Z_V, Z_S, Z_K = 0, 10, 20, 30, 38, 44, 50, 66
Z_ROWS = 72


def pack_c_kernel(
    g, b, w, left, chip, both, f2in, f2lowin, f2highin, c1, wc, cleft, cchip,
    even, even2, odd, f2, f2low, f2high, c1x, c2z, table, terms, rows, sides,
):
    fine = Wide(g, b, w, left, chip)
    cright = partner(cchip)

    def put(i, values):
        for k, v in enumerate(values):
            table[k, i : i + 1, :] = v

    corner_terms(fine, both.at[0], both.at[1], (cleft, cright), put)
    *parts, share = corner_sums(table)
    for k, v in enumerate(parts):
        terms[k] = v
    rows[...] = share
    a = Coarse(c1x, wc, cleft, cright)
    for x in range(CX):
        c1x[(x + CX) * CY : (x + CX + 1) * CY, :] = slab(c1, x, CY)
        c1x[(CX - 1 - x) * CY : (CX - x) * CY, :] = cleft[x * CY : (x + 1) * CY, 0:CZ]
        c1x[(x + 2 * CX) * CY : (x + 2 * CX + 1) * CY, :] = cright[x * CY : (x + 1) * CY, 0:CZ]
    f2[...] = f2in[...]
    f2low[...] = f2lowin[...]
    f2high[...] = f2highin[...]

    def add(ref, k, v):
        ref[k : k + 1, :] = ref[k : k + 1, :] + v

    for e, (xe, xi, xn, cxe, cxn) in enumerate(((0, 1, -1, 0, -1), (7, 6, 8, 3, 4))):
        for s, (side, y, yi, cy) in enumerate(((f2low, 0, 1, 0), (f2high, BY - 1, BY - 2, CY - 1))):
            i = 2 * e + s
            add(f2, (xe + 1) * BY + y, terms[0, i : i + 1, :])
            add(side, xe, terms[1, i : i + 1, :])
            add(f2, (xn + 1) * BY + y, terms[2, i : i + 1, :])
            add(side, xi, terms[3, i : i + 1, :])
            add(f2, (xn + 1) * BY + yi, terms[4, i : i + 1, :])
            add(c1x, (cxe + CX) * CY + cy, a.w(cxe)[cy : cy + 1] * rows[i : i + 1, :])
            add(c1x, (cxn + CX) * CY + cy, a.w(cxn)[cy : cy + 1] * rows[i + 4 : i + 5, :])
    lo, hi = sides.at[0], sides.at[1]
    second = {}
    for x in range(-3, 7):
        c, cw = a.first(x), a.w(x)
        second[x] = (1.0 + KEEP) * c + cw * (
            a.first(x - 1) + a.first(x + 1) + beside_z(c) + beside_y(c, 0.0, 0.0)
        )
        c2z[(x + 3) * CY : (x + 4) * CY, :] = second[x]
        for out, y in ((lo, 0), (hi, CY - 1)):
            for base, v in ((Z_C, c), (Z_P, second[x]), (Z_W, cw)):
                k = base + x + 3
                out[k : k + 1, :] = v[y : y + 1]
    for x in range(-2, 6):
        s, c, cw = second[x], a.first(x), a.w(x)
        below, above = shift_y(s, 0.0, 0.0)
        inner = {0: above, 1: below}
        for side, (out, y, y2) in enumerate(((lo, 0, 1), (hi, CY - 1, CY - 2))):
            k = Z_Q + x + 2
            out[k : k + 1, :] = (c + cw * inner[side])[y : y + 1]
        if -1 <= x <= 4:
            part = KEEP * s + c + cw * (second[x - 1] + second[x + 1] + beside_z(s))
            for side, (out, y, y2) in enumerate(((lo, 0, 1), (hi, CY - 1, CY - 2))):
                k = Z_R + x + 1
                out[k : k + 1, :] = (part + cw * inner[side])[y2 : y2 + 1]
                k = Z_V + x + 1
                out[k : k + 1, :] = cw[y2 : y2 + 1]
    for out, y, inner in ((lo, 0, 1), (hi, BY - 1, BY - 2)):
        for x in range(BX):
            at = (x + 1) * BY
            v = fine.w(x, y) * (fine.rhs(x, y) + row(f2, at + inner))
            for half in range(2):
                k = Z_S + 2 * x + half
                out[k : k + 1, :] = v[:, half * CZ : (half + 1) * CZ]
        for j, x in enumerate((-1, 8)):
            at = (x + 1) * BY + y
            v = f2[at : at + 1, :]
            for half in range(2):
                k = Z_K + 2 * j + half
                out[k : k + 1, :] = v[:, half * CZ : (half + 1) * CZ]
    p = side_of_dev()
    even[...] = sides[1 - p]
    even2[...] = sides[1 - p]
    odd[...] = sides[p]


def last_kernel(
    g, b, w, left, chip, both, f2, f2low, f2high, c1x, wc, cleft, cchip, c2z, even1, odd, even2,
    out, cboth, col, line, line3, fine, corr, col2, s1, gline, g1line,
):
    wide = Wide(g, b, w, left, chip)
    a = Coarse(c1x, wc, cleft, partner(cchip))
    take(cboth, even1[...] + even2[...], odd[...])
    low, high, clow, chigh = both.at[0], both.at[1], cboth.at[0], cboth.at[1]
    crow = lax.broadcasted_iota(jnp.int32, (CY, CZ), 0)
    c2 = {}
    for x in range(-3, 7):
        k = Z_C + x + 3
        beyond = jnp.where(crow == 0, row(clow, k), jnp.where(crow == CY - 1, row(chigh, k), 0.0))
        c2[x] = slab(c2z, x + 3, CY) + a.w(x) * beyond
    sides = ((clow, 0), (chigh, CY - 1))
    for s, (side, y) in enumerate(sides):
        for x in range(-3, 7):
            col[x + 3 : x + 4, :] = a.first(x)[y : y + 1]
        line[s, 0:10, :] = side[Z_P : Z_P + 10, :] + side[Z_W : Z_W + 10, :] * col[0:10, :]
        for x in range(-2, 6):
            col[x + 2 : x + 3, :] = c2[x][y : y + 1]
        mid = line[s, 1:9, :]
        line3[s, 0:8, :] = (
            KEEP * mid
            + side[Z_Q : Z_Q + 8, :]
            + side[Z_W + 1 : Z_W + 9, :]
            * (line[s, 0:8, :] + line[s, 2:10, :] + beside_z(mid) + col[0:8, :])
        )
    c3 = {}
    for x in range(-2, 6):
        c = c2[x]
        c3[x] = KEEP * c + a.first(x) + a.w(x) * (
            c2[x - 1]
            + c2[x + 1]
            + beside_z(c)
            + beside_y(c, line[0, x + 3 : x + 4, :], line[1, x + 3 : x + 4, :])
        )
    for x in range(-1, 5):
        c = c3[x]
        c4 = KEEP * c + a.first(x) + a.w(x) * (
            c3[x - 1]
            + c3[x + 1]
            + beside_z(c)
            + beside_y(c, line3[0, x + 2 : x + 3, :], line3[1, x + 2 : x + 3, :])
        )
        fine[pl.ds((x + 1) * BY, CY, stride=2), :] = c4
        fine[pl.ds((x + 1) * BY + 1, CY, stride=2), :] = c4
    for s, (side, y) in enumerate(sides):
        for x in range(-1, 5):
            col[x + 1 : x + 2, :] = c3[x][y : y + 1]
        mid = line3[s, 1:7, :]
        third = side[Z_R : Z_R + 6, :] + side[Z_V : Z_V + 6, :] * line[s, 2:8, :]
        fine[6 * BY + 8 * s : 6 * BY + 8 * s + 6, :] = (
            KEEP * mid
            + side[Z_C + 2 : Z_C + 8, :]
            + side[Z_W + 2 : Z_W + 8, :]
            * (line3[s, 0:6, :] + line3[s, 2:8, :] + beside_z(mid) + third + col[0:6, :])
        )
        fine[6 * BY + 8 * s + 6 : 6 * BY + 8 * s + 8, :] = jnp.zeros((2, CZ), F32)
    corr[...] = lax.dot_general(
        fine[...],
        halved(CZ, NZ),
        (((1,), (0,)), ((), ())),
        precision=lax.Precision.HIGHEST,
        preferred_element_type=F32,
    )
    g0 = {}
    for x in range(-2, 10):
        if x == -2:
            f = slab(cleft, 2)
        elif x == 9:
            f = slab(a.right, 2)
        else:
            f = slab(f2, x + 1)
        g0[x] = f + slab(corr, (x + 2) // 2)
    for s, (cside, side, y, f2side) in enumerate(((clow, low, 0, f2low), (chigh, high, BY - 1, f2high))):
        base = 6 * BY + 8 * s
        for x in range(-1, 9):
            k = base + (x + 2) // 2
            col2[x + 1 : x + 2, :] = corr[k : k + 1, :]
        gline[s, 1:9, :] = f2side[...] + col2[1:9, :]
        for j, x in enumerate((-1, 8)):
            k = Z_K + 2 * j
            gline[s, x + 1 : x + 2, 0:CZ] = row(cside, k) + col2[x + 1 : x + 2, 0:CZ]
            gline[s, x + 1 : x + 2, CZ:] = row(cside, k + 1) + col2[x + 1 : x + 2, CZ:]
        for x in range(BX):
            k = Z_S + 2 * x
            s1[x : x + 1, 0:CZ] = row(cside, k)
            s1[x : x + 1, CZ:] = row(cside, k + 1)
        moved = col2[1:9, :]
        for x in range(BX):
            col2[x : x + 1, :] = g0[x][y : y + 1]
        mid = gline[s, 1:9, :]
        g1line[s, 0:8, :] = (
            KEEP * mid
            + s1[0:8, :]
            + side[Y_W : Y_W + 8, :]
            * (moved + gline[s, 0:8, :] + gline[s, 2:10, :] + beside_z(mid) + col2[0:8, :])
        )
    g1 = {}
    for x in range(-1, 9):
        f = g0[x]
        g1[x] = KEEP * f + wide.w(x) * (
            wide.rhs(x)
            + g0[x - 1]
            + g0[x + 1]
            + beside_z(f)
            + beside_y(f, gline[0, x + 1 : x + 2, :], gline[1, x + 1 : x + 2, :])
        )
    for x in range(BX):
        f = g1[x]
        out[place(x)] = KEEP * f + wide.w(x) * (
            wide.rhs(x)
            + g1[x - 1]
            + g1[x + 1]
            + beside_z(f)
            + beside_y(f, g1line[0, x : x + 1, :], g1line[1, x : x + 1, :])
        )


def swap(v, pairs):
    n = lax.axis_size("dev")
    links = [(i * n + j, k * n + l) for (i, j), (k, l) in pairs]
    return lax.ppermute(v, ("group", "dev"), links + [(j, i) for i, j in links])


def share_chip(v):
    groups = [[i, i + 1] for i in range(0, lax.axis_size("group"), 2)]
    return lax.all_gather(v, "group", axis_index_groups=groups)


def cross_pairs(keep):
    devs = [d for d in range(lax.axis_size("dev")) if keep(d)]
    return [((i, d), (i + 1, d)) for i in range(1, lax.axis_size("group") - 1, 2) for d in devs]


def dev_pairs(start, keep):
    devs = [d for d in range(start, lax.axis_size("dev") - 1, 2) if keep(d)]
    return [((i, d), (i, d + 1)) for i in range(lax.axis_size("group")) for d in devs]


def is_end(d):
    return d % RUN == RUN - 1


def before_end(d):
    return d % RUN == RUN - 2


def body(g, b, n):
    block = (BX, BY, NZ)
    cross, cross2, chip, even, even2, odd, f1z, g, b, w, d = call(
        load_kernel,
        [(X_ROWS, NZ)] * 3 + [(Y_ROWS, NZ)] * 3 + [(BX * BY, NZ)] + [block] * 4,
        g, b, n,
        hbm=3,
        vmem=None,
        scratch=[pltpu.VMEM(block, jnp.int32), (2, Y_ROWS, NZ), pltpu.SemaphoreType.DMA((3,))],
    )
    cross1 = swap(cross, cross_pairs(lambda d: not is_end(d)))
    even1 = swap(even, dev_pairs(0, lambda d: not before_end(d)))
    odd = swap(odd, dev_pairs(1, lambda d: True))
    cross2 = swap(cross2, cross_pairs(is_end))
    even2 = swap(even2, dev_pairs(0, before_end))
    chip = share_chip(chip)
    left, both = call(
        gather_kernel,
        [(X_ROWS, NZ), (2, Y_ROWS, NZ)],
        cross1, even1, odd,
        cost=pl.CostEstimate(flops=2**34, bytes_accessed=2**28, transcendentals=0),
    )
    f2, f2low, f2high, c1, wc, left, both, cross, near = call(
        middle_kernel,
        [(10 * BY, NZ), (BX, NZ), (BX, NZ), (CX * CY, CZ), (CX * CY, CZ), (X_ROWS, NZ), (2, Y_ROWS, NZ)] + [(X2_ROWS, NZ)] * 2,
        g, b, w, d, left, cross2, chip, f1z, both, even2,
        scratch=[(16, NZ), (2, 16, NZ), (8 * BY, CZ)],
    )
    cleft = swap(cross, cross_pairs(lambda d: True))
    cchip = share_chip(near)
    even, even2, odd, f2, f2low, f2high, c1x, c2z = call(
        pack_c_kernel,
        [(Z_ROWS, CZ)] * 3 + [(10 * BY, NZ), (BX, NZ), (BX, NZ), (3 * CX * CY, CZ), (10 * CY, CZ)],
        g, b, w, left, chip, both, f2, f2low, f2high, c1, wc, cleft, cchip,
        scratch=[(13, 8, NZ), (5, 8, NZ), (8, CZ), (2, Z_ROWS, CZ)],
    )
    even1 = swap(even, dev_pairs(0, lambda d: not before_end(d)))
    odd = swap(odd, dev_pairs(1, lambda d: True))
    even2 = swap(even2, dev_pairs(0, before_end))
    (out,) = call(
        last_kernel,
        [block],
        g, b, w, left, chip, both, f2, f2low, f2high, c1x, wc, cleft, cchip, c2z, even1, odd, even2,
        scratch=[
            (2, Z_ROWS, CZ),
            (16, CZ), (2, 16, CZ), (2, 8, CZ), (6 * BY + 16, CZ), (6 * BY + 16, NZ), (16, NZ), (8, NZ), (2, 16, NZ), (2, 8, NZ),
        ],
        hbm_out=True,
    )
    return out


def solution(mesh):
    s = P("group", "dev", None)
    return jax.shard_map(body, mesh=mesh, in_specs=(s, s, s), out_specs=s, check_vma=False)
```

```python
import jax
import jax.numpy as jnp
from jax import lax
from jax.sharding import PartitionSpec as P
from jax.experimental import pallas as pl
from jax.experimental.pallas import tpu as pltpu

OMEGA = 0.8
KEEP = 1.0 - OMEGA
VM = pl.BlockSpec(memory_space=pltpu.VMEM)
F32 = jnp.float32
BX, BY, NZ = 8, 16, 256
CX, CY, CZ = 4, 8, 128
RUN = 32


def call(kernel, outs, *args, scratch=(), hbm=0, hbm_out=False, vmem=8 * 2**20, cost=None):
    make = jax.ShapeDtypeStruct if hbm_out else pltpu.VMEM
    return pl.pallas_call(
        kernel,
        out_shape=[make(s, F32) for s in outs],
        in_specs=[pl.BlockSpec(memory_space=pltpu.HBM)] * hbm + [VM] * (len(args) - hbm),
        out_specs=[VM] * len(outs),
        scratch_shapes=[pltpu.VMEM(s, F32) if isinstance(s, tuple) else s for s in scratch],
        compiler_params=pltpu.CompilerParams(vmem_limit_bytes=vmem),
        cost_estimate=cost,
    )(*args)


def beside_z(v):
    lane = lax.broadcasted_iota(jnp.int32, v.shape, 1)
    last = v.shape[1] - 1
    below = jnp.where(lane == 0, 0.0, pltpu.roll(v, 1, 1))
    above = jnp.where(lane == last, 0.0, pltpu.roll(v, last, 1))
    return below + above


def shift_y(v, low, high):
    row = lax.broadcasted_iota(jnp.int32, v.shape, 0)
    last = v.shape[0] - 1
    below = jnp.where(row == 0, low, pltpu.roll(v, 1, 0))
    above = jnp.where(row == last, high, pltpu.roll(v, last, 0))
    return below, above


def beside_y(v, low, high):
    below, above = shift_y(v, low, high)
    return below + above


def slab(ref, k, rows=BY):
    return ref[k * rows : (k + 1) * rows, :]


def row(ref, k):
    return ref[k : k + 1, :]


def halved(n, m):
    a = lax.broadcasted_iota(jnp.int32, (n, m), 0)
    b = lax.broadcasted_iota(jnp.int32, (n, m), 1)
    return jnp.where((a // 2 == b) if n > m else (a == b // 2), 1.0, 0.0).astype(F32)


def lanes(v, index):
    return jnp.take_along_axis(v, index, axis=1)


def pair_z(v):
    lane = lax.broadcasted_iota(jnp.int32, (v.shape[0], CZ), 1)
    low, high = v[:, :CZ], v[:, CZ:]
    low = low + pltpu.roll(low, CZ - 1, 1)
    high = high + pltpu.roll(high, CZ - 1, 1)
    index = (2 * lane) % CZ
    return jnp.where(lane < CZ // 2, lanes(low, index), lanes(high, index))


def diag_of(n):
    return 6.0 + 0.25 * n.astype(F32)


def place(x):
    odd = lax.axis_index("group") % 2
    return x + odd * (BX - 1 - 2 * x)


def partner(ref):
    return ref.at[1 - lax.axis_index("group") % 2]


def inner_pair():
    at = lax.axis_index("dev") % RUN
    return (at == RUN - 3) | (at == RUN - 2)


def side_of_dev():
    return lax.axis_index("dev") % 2


Y_G, Y_P, Y_W, Y_Q, Y_G2, Y_W2 = 0, 8, 16, 24, 32, 34
Y_ROWS = 40
X_ROWS = 7 * BY


def load_kernel(
    g_hbm, b_hbm, n_hbm, cross, mixed, chip, even, even2, odd, f1z, g, b, w, d, n, both, sems
):
    copies = [
        pltpu.make_async_copy(src, dst, sems.at[k])
        for k, (src, dst) in enumerate(((g_hbm, g), (b_hbm, b), (n_hbm, n)))
    ]
    for c in copies:
        c.start()
    for c in copies:
        c.wait()
    for x in range(BX):
        diag = diag_of(n[x])
        d[x] = diag
        w[x] = OMEGA / diag
    for out, layers in ((cross, (0, 1, 2)), (chip, (7, 6, 5))):
        for k in range(3):
            out[k * BY : (k + 1) * BY, :] = g[place(layers[k])]
        for k in range(2):
            out[(3 + k) * BY : (4 + k) * BY, :] = w[place(layers[k])]
            out[(5 + k) * BY : (6 + k) * BY, :] = b[place(layers[k])]
    zero = jnp.zeros((BY, NZ), F32)
    for x in range(BX):
        at = place(x)
        here, wx, bx = g[at], w[at], b[at]
        before = g[place(x - 1)] if x else zero
        after = g[place(x + 1)] if x < BX - 1 else zero
        f = KEEP * here + wx * (bx + before + after + beside_z(here) + beside_y(here, 0.0, 0.0))
        f1z[x * BY : (x + 1) * BY, :] = f
        for s, (y, inner) in enumerate(((0, 1), (BY - 1, BY - 2))):
            rows = [
                (Y_G + x, here[y : y + 1]),
                (Y_P + x, f[y : y + 1]),
                (Y_W + x, wx[y : y + 1]),
                (Y_Q + x, wx[y : y + 1] * (bx[y : y + 1] + f[inner : inner + 1])),
            ]
            if x in (0, 7):
                rows += [(Y_G2 + x // 7, here[inner : inner + 1]), (Y_W2 + x // 7, wx[inner : inner + 1])]
            for k, v in rows:
                both[s, k : k + 1, :] = v
    p = side_of_dev()
    even[...] = both[1 - p]
    even2[...] = both[1 - p]
    odd[...] = both[p]
    mixed[...] = cross[...]

    @pl.when(inner_pair())
    def _():
        mixed[0:Y_ROWS, :] = both[p]


class Wide:
    def __init__(self, g, b, w, left, right):
        self.own, self.left, self.right = (g, w, b), left, partner(right)

    def _get(self, which, base, x, y):
        if 0 <= x < BX:
            v = self.own[which]
            return v[place(x)] if y is None else v[place(x), y : y + 1, :]
        ref, k = (self.left, -1 - x) if x < 0 else (self.right, x - BX)
        return slab(ref, base + k) if y is None else row(ref, (base + k) * BY + y)

    def guess(self, x, y=None):
        return self._get(0, 0, x, y)

    def w(self, x, y=None):
        return self._get(1, 3, x, y)

    def rhs(self, x, y=None):
        return self._get(2, 5, x, y)


def take(both, even, odd):
    p = side_of_dev()
    both[1 - p] = even
    both[p] = odd


def gather_kernel(cross, even, odd, left, both):
    left[...] = cross[...]
    take(both, even[...], odd[...])


X2_D = 3 * BY
X2_ROWS = X2_D + 16


def diagonal_rows(edge):
    at, inner = (0, 1) if edge == 0 else (7, 6)
    return (Y_G + at, Y_G2 + edge, Y_G + inner, Y_P + at, Y_W + at, Y_W2 + edge, Y_W + inner)


def middle_kernel(
    g, b, w, d, left1, mixed, chip, f1z, both1, even2,
    f2, f2low, f2high, c1, wc, left, both, lo, hi, col, line, sums,
):
    inner = inner_pair()
    left[...] = left1[...] + jnp.where(inner, 0.0, mixed[...])
    a = Wide(g, b, w, left, chip)
    p = side_of_dev()
    both[p] = both1[p] + jnp.where(inner, mixed[0:Y_ROWS, :], 0.0)
    both[1 - p] = both1[1 - p] + even2[...]
    low, high = both.at[0], both.at[1]
    rows = lax.broadcasted_iota(jnp.int32, (BY, NZ), 0)
    f1 = {}
    for x in range(-2, 10):
        if 0 <= x < BX:
            k = Y_G + x
            beyond = jnp.where(rows == 0, row(low, k), jnp.where(rows == BY - 1, row(high, k), 0.0))
            if x == 0:
                beyond = beyond + a.guess(-1)
            if x == BX - 1:
                beyond = beyond + a.guess(BX)
            f1[x] = slab(f1z, x) + a.w(x) * beyond
        else:
            here = a.guess(x)
            f1[x] = KEEP * here + a.w(x) * (
                a.rhs(x) + a.guess(x - 1) + a.guess(x + 1) + beside_z(here) + beside_y(here, 0.0, 0.0)
            )
    for s, (side, y, out) in enumerate(((low, 0, f2low), (high, BY - 1, f2high))):
        for x in range(BX):
            col[x : x + 1, :] = a.guess(x, y)
        line[s, 0:16, :] = jnp.zeros((16, NZ), F32)
        line[s, 1:9, :] = side[Y_P : Y_P + 8, :] + side[Y_W : Y_W + 8, :] * col[0:8, :]
        for x in range(BX):
            col[x : x + 1, :] = f1[x][y : y + 1]
        mid = line[s, 1:9, :]
        out[...] = (
            KEEP * mid
            + side[Y_Q : Y_Q + 8, :]
            + side[Y_W : Y_W + 8, :] * (line[s, 0:8, :] + line[s, 2:10, :] + beside_z(mid) + col[0:8, :])
        )
        for edge, pack in enumerate((lo, hi)):
            for k, r in enumerate(diagonal_rows(edge)):
                at = X2_D + 7 * s + k
                pack[at : at + 1, :] = row(side, r)
    for pack in (lo, hi):
        pack[X2_D + 14 :, :] = jnp.zeros((2, NZ), F32)
    sec = {}
    for x in range(-1, 9):
        f = f1[x]
        sec[x] = KEEP * f + a.w(x) * (
            a.rhs(x)
            + f1[x - 1]
            + f1[x + 1]
            + beside_z(f)
            + beside_y(f, line[0, x + 1 : x + 2, :], line[1, x + 1 : x + 2, :])
        )
        f2[(x + 1) * BY : (x + 2) * BY, :] = sec[x]
    lo[2 * BY : X2_D, :] = sec[1]
    hi[2 * BY : X2_D, :] = sec[6]
    pairs, points = [], []
    for x in range(0, 8):
        f = sec[x]
        r = (
            a.rhs(x)
            - d[place(x)] * f
            + sec[x - 1]
            + sec[x + 1]
            + beside_z(f)
            + beside_y(f, row(f2low, x), row(f2high, x))
        )
        if x % 2:
            pairs[-1] = pairs[-1] + r
            points[-1] = points[-1] + d[place(x)]
        else:
            pairs.append(r)
            points.append(d[place(x)])
    sums[...] = lax.dot_general(
        jnp.concatenate(pairs + points, axis=0),
        halved(NZ, CZ),
        (((1,), (0,)), ((), ())),
        precision=lax.Precision.HIGHEST,
        preferred_element_type=F32,
    )
    for x in range(CX):
        at = x * BY
        total = sums[pl.ds(at, CY, stride=2), :] + sums[pl.ds(at + 1, CY, stride=2), :]
        at = (CX + x) * BY
        diags = sums[pl.ds(at, CY, stride=2), :] + sums[pl.ds(at + 1, CY, stride=2), :]
        weight = OMEGA / (0.5 * diags - 18.0)
        first = weight * (0.5 * total)
        c1[x * CY : (x + 1) * CY, :] = first
        wc[x * CY : (x + 1) * CY, :] = weight
        for out, k in ((lo, x), (hi, CX - 1 - x)):
            out[k * CY : (k + 1) * CY, 0:CZ] = first
            out[k * CY : (k + 1) * CY, CZ:] = weight


class Coarse:
    def __init__(self, c1x, wc, left, right):
        self.c1x, self.wc, self.left, self.right = c1x, wc, left, right

    def first(self, x):
        return slab(self.c1x, x + CX, CY)

    def w(self, x):
        if 0 <= x < CX:
            return slab(self.wc, x, CY)
        ref, k = (self.left, -1 - x) if x < 0 else (self.right, x - CX)
        return ref[k * CY : (k + 1) * CY, CZ:]


def corner_terms(a, low, high, relays, put):
    for e, (xe, xi, xn, xm) in enumerate(((0, 1, -1, -2), (7, 6, 8, 9))):
        for s, (side, y, yi) in enumerate(((low, 0, 1), (high, BY - 1, BY - 2))):
            own = [row(side, r) for r in diagonal_rows(e)]
            far = [row(relays[e], X2_D + 7 * s + k) for k in range(7)]
            corner, beside = a.guess(xe, y), a.guess(xn, y)
            w_corner, w_beside = a.w(xe, y), a.w(xn, y)
            put(2 * e + s, far[:5] + [beside + own[0], w_beside, a.w(xm, y), a.w(xn, yi), own[4], own[5], own[6], w_corner])
            put(4 + 2 * e + s, own[:5] + [corner + far[0], w_corner, a.w(xi, y), a.w(xe, yi), far[4], far[5], far[6], w_beside])


def corner_sums(t):
    g1, g2, g3, part, wd, near, wx, wx2, wxs, wy, wy2, wys, wq = (t[k] for k in range(13))
    dq = jnp.where(wq > 0.0, OMEGA / jnp.where(wq > 0.0, wq, 1.0), 0.0)
    by_y = wy * g1
    by_x = wx * g1
    diagonal = part + wd * near
    at_q = wq * (by_x + by_y)
    at_y = KEEP * by_y + wy * (beside_z(by_y) + diagonal + wy2 * g2)
    at_x = KEEP * by_x + wx * (beside_z(by_x) + diagonal + wx2 * g3)
    at_ys = wys * by_y
    at_xs = wxs * by_x
    total = at_y + at_x + beside_z(at_q) - dq * at_q + 2.0 * at_q + at_ys + at_xs
    return at_q, at_y, at_x, at_ys, at_xs, 0.5 * pair_z(total)


Z_C, Z_P, Z_W, Z_Q, Z_R, Z_V, Z_S, Z_K = 0, 10, 20, 30, 38, 44, 50, 66
Z_ROWS = 72


def pack_c_kernel(
    g, b, w, left, chip, both, f2in, f2lowin, f2highin, c1, wc, cleft, cchip,
    even, even2, odd, f2, f2low, f2high, c1x, c2z, table, terms, rows, sides,
):
    fine = Wide(g, b, w, left, chip)
    cright = partner(cchip)

    def put(i, values):
        for k, v in enumerate(values):
            table[k, i : i + 1, :] = v

    corner_terms(fine, both.at[0], both.at[1], (cleft, cright), put)
    *parts, share = corner_sums(table)
    for k, v in enumerate(parts):
        terms[k] = v
    rows[...] = share
    a = Coarse(c1x, wc, cleft, cright)
    for x in range(CX):
        c1x[(x + CX) * CY : (x + CX + 1) * CY, :] = slab(c1, x, CY)
        c1x[(CX - 1 - x) * CY : (CX - x) * CY, :] = cleft[x * CY : (x + 1) * CY, 0:CZ]
        c1x[(x + 2 * CX) * CY : (x + 2 * CX + 1) * CY, :] = cright[x * CY : (x + 1) * CY, 0:CZ]
    f2[...] = f2in[...]
    f2low[...] = f2lowin[...]
    f2high[...] = f2highin[...]

    def add(ref, k, v):
        ref[k : k + 1, :] = ref[k : k + 1, :] + v

    for e, (xe, xi, xn, cxe, cxn) in enumerate(((0, 1, -1, 0, -1), (7, 6, 8, 3, 4))):
        for s, (side, y, yi, cy) in enumerate(((f2low, 0, 1, 0), (f2high, BY - 1, BY - 2, CY - 1))):
            i = 2 * e + s
            add(f2, (xe + 1) * BY + y, terms[0, i : i + 1, :])
            add(side, xe, terms[1, i : i + 1, :])
            add(f2, (xn + 1) * BY + y, terms[2, i : i + 1, :])
            add(side, xi, terms[3, i : i + 1, :])
            add(f2, (xn + 1) * BY + yi, terms[4, i : i + 1, :])
            add(c1x, (cxe + CX) * CY + cy, a.w(cxe)[cy : cy + 1] * rows[i : i + 1, :])
            add(c1x, (cxn + CX) * CY + cy, a.w(cxn)[cy : cy + 1] * rows[i + 4 : i + 5, :])
    lo, hi = sides.at[0], sides.at[1]
    second = {}
    for x in range(-3, 7):
        c, cw = a.first(x), a.w(x)
        second[x] = (1.0 + KEEP) * c + cw * (
            a.first(x - 1) + a.first(x + 1) + beside_z(c) + beside_y(c, 0.0, 0.0)
        )
        c2z[(x + 3) * CY : (x + 4) * CY, :] = second[x]
        for out, y in ((lo, 0), (hi, CY - 1)):
            for base, v in ((Z_C, c), (Z_P, second[x]), (Z_W, cw)):
                k = base + x + 3
                out[k : k + 1, :] = v[y : y + 1]
    for x in range(-2, 6):
        s, c, cw = second[x], a.first(x), a.w(x)
        below, above = shift_y(s, 0.0, 0.0)
        inner = {0: above, 1: below}
        for side, (out, y, y2) in enumerate(((lo, 0, 1), (hi, CY - 1, CY - 2))):
            k = Z_Q + x + 2
            out[k : k + 1, :] = (c + cw * inner[side])[y : y + 1]
        if -1 <= x <= 4:
            part = KEEP * s + c + cw * (second[x - 1] + second[x + 1] + beside_z(s))
            for side, (out, y, y2) in enumerate(((lo, 0, 1), (hi, CY - 1, CY - 2))):
                k = Z_R + x + 1
                out[k : k + 1, :] = (part + cw * inner[side])[y2 : y2 + 1]
                k = Z_V + x + 1
                out[k : k + 1, :] = cw[y2 : y2 + 1]
    for out, y, inner in ((lo, 0, 1), (hi, BY - 1, BY - 2)):
        for x in range(BX):
            at = (x + 1) * BY
            v = fine.w(x, y) * (fine.rhs(x, y) + row(f2, at + inner))
            for half in range(2):
                k = Z_S + 2 * x + half
                out[k : k + 1, :] = v[:, half * CZ : (half + 1) * CZ]
        for j, x in enumerate((-1, 8)):
            at = (x + 1) * BY + y
            v = f2[at : at + 1, :]
            for half in range(2):
                k = Z_K + 2 * j + half
                out[k : k + 1, :] = v[:, half * CZ : (half + 1) * CZ]
    p = side_of_dev()
    even[...] = sides[1 - p]
    even2[...] = sides[1 - p]
    odd[...] = sides[p]


def last_kernel(
    g, b, w, left, chip, both, f2, f2low, f2high, c1x, wc, cleft, cchip, c2z, even1, odd, even2,
    out, cboth, col, line, line3, fine, corr, col2, s1, gline, g1line,
):
    wide = Wide(g, b, w, left, chip)
    a = Coarse(c1x, wc, cleft, partner(cchip))
    take(cboth, even1[...] + even2[...], odd[...])
    low, high, clow, chigh = both.at[0], both.at[1], cboth.at[0], cboth.at[1]
    crow = lax.broadcasted_iota(jnp.int32, (CY, CZ), 0)
    c2 = {}
    for x in range(-3, 7):
        k = Z_C + x + 3
        beyond = jnp.where(crow == 0, row(clow, k), jnp.where(crow == CY - 1, row(chigh, k), 0.0))
        c2[x] = slab(c2z, x + 3, CY) + a.w(x) * beyond
    sides = ((clow, 0), (chigh, CY - 1))
    for s, (side, y) in enumerate(sides):
        for x in range(-3, 7):
            col[x + 3 : x + 4, :] = a.first(x)[y : y + 1]
        line[s, 0:10, :] = side[Z_P : Z_P + 10, :] + side[Z_W : Z_W + 10, :] * col[0:10, :]
        for x in range(-2, 6):
            col[x + 2 : x + 3, :] = c2[x][y : y + 1]
        mid = line[s, 1:9, :]
        line3[s, 0:8, :] = (
            KEEP * mid
            + side[Z_Q : Z_Q + 8, :]
            + side[Z_W + 1 : Z_W + 9, :]
            * (line[s, 0:8, :] + line[s, 2:10, :] + beside_z(mid) + col[0:8, :])
        )
    c3 = {}
    for x in range(-2, 6):
        c = c2[x]
        c3[x] = KEEP * c + a.first(x) + a.w(x) * (
            c2[x - 1]
            + c2[x + 1]
            + beside_z(c)
            + beside_y(c, line[0, x + 3 : x + 4, :], line[1, x + 3 : x + 4, :])
        )
    for x in range(-1, 5):
        c = c3[x]
        c4 = KEEP * c + a.first(x) + a.w(x) * (
            c3[x - 1]
            + c3[x + 1]
            + beside_z(c)
            + beside_y(c, line3[0, x + 2 : x + 3, :], line3[1, x + 2 : x + 3, :])
        )
        fine[pl.ds((x + 1) * BY, CY, stride=2), :] = c4
        fine[pl.ds((x + 1) * BY + 1, CY, stride=2), :] = c4
    for s, (side, y) in enumerate(sides):
        for x in range(-1, 5):
            col[x + 1 : x + 2, :] = c3[x][y : y + 1]
        mid = line3[s, 1:7, :]
        third = side[Z_R : Z_R + 6, :] + side[Z_V : Z_V + 6, :] * line[s, 2:8, :]
        fine[6 * BY + 8 * s : 6 * BY + 8 * s + 6, :] = (
            KEEP * mid
            + side[Z_C + 2 : Z_C + 8, :]
            + side[Z_W + 2 : Z_W + 8, :]
            * (line3[s, 0:6, :] + line3[s, 2:8, :] + beside_z(mid) + third + col[0:6, :])
        )
        fine[6 * BY + 8 * s + 6 : 6 * BY + 8 * s + 8, :] = jnp.zeros((2, CZ), F32)
    corr[...] = lax.dot_general(
        fine[...],
        halved(CZ, NZ),
        (((1,), (0,)), ((), ())),
        precision=lax.Precision.HIGHEST,
        preferred_element_type=F32,
    )
    g0 = {}
    for x in range(-2, 10):
        if x == -2:
            f = slab(cleft, 2)
        elif x == 9:
            f = slab(a.right, 2)
        else:
            f = slab(f2, x + 1)
        g0[x] = f + slab(corr, (x + 2) // 2)
    for s, (cside, side, y, f2side) in enumerate(((clow, low, 0, f2low), (chigh, high, BY - 1, f2high))):
        base = 6 * BY + 8 * s
        for x in range(-1, 9):
            k = base + (x + 2) // 2
            col2[x + 1 : x + 2, :] = corr[k : k + 1, :]
        gline[s, 1:9, :] = f2side[...] + col2[1:9, :]
        for j, x in enumerate((-1, 8)):
            k = Z_K + 2 * j
            gline[s, x + 1 : x + 2, 0:CZ] = row(cside, k) + col2[x + 1 : x + 2, 0:CZ]
            gline[s, x + 1 : x + 2, CZ:] = row(cside, k + 1) + col2[x + 1 : x + 2, CZ:]
        for x in range(BX):
            k = Z_S + 2 * x
            s1[x : x + 1, 0:CZ] = row(cside, k)
            s1[x : x + 1, CZ:] = row(cside, k + 1)
        moved = col2[1:9, :]
        for x in range(BX):
            col2[x : x + 1, :] = g0[x][y : y + 1]
        mid = gline[s, 1:9, :]
        g1line[s, 0:8, :] = (
            KEEP * mid
            + s1[0:8, :]
            + side[Y_W : Y_W + 8, :]
            * (moved + gline[s, 0:8, :] + gline[s, 2:10, :] + beside_z(mid) + col2[0:8, :])
        )
    g1 = {}
    for x in range(-1, 9):
        f = g0[x]
        g1[x] = KEEP * f + wide.w(x) * (
            wide.rhs(x)
            + g0[x - 1]
            + g0[x + 1]
            + beside_z(f)
            + beside_y(f, gline[0, x + 1 : x + 2, :], gline[1, x + 1 : x + 2, :])
        )
    for x in range(BX):
        f = g1[x]
        out[place(x)] = KEEP * f + wide.w(x) * (
            wide.rhs(x)
            + g1[x - 1]
            + g1[x + 1]
            + beside_z(f)
            + beside_y(f, g1line[0, x : x + 1, :], g1line[1, x : x + 1, :])
        )


def swap(v, pairs):
    n = lax.axis_size("dev")
    links = [(i * n + j, k * n + l) for (i, j), (k, l) in pairs]
    return lax.ppermute(v, ("group", "dev"), links + [(j, i) for i, j in links])


def share_chip(v):
    groups = [[i, i + 1] for i in range(0, lax.axis_size("group"), 2)]
    return lax.all_gather(v, "group", axis_index_groups=groups)


def cross_pairs(keep):
    devs = [d for d in range(lax.axis_size("dev")) if keep(d)]
    return [((i, d), (i + 1, d)) for i in range(1, lax.axis_size("group") - 1, 2) for d in devs]


def dev_pairs(start, keep):
    devs = [d for d in range(start, lax.axis_size("dev") - 1, 2) if keep(d)]
    return [((i, d), (i, d + 1)) for i in range(lax.axis_size("group")) for d in devs]


def is_end(d):
    return d % RUN == RUN - 1


def before_end(d):
    return d % RUN == RUN - 2


def body(g, b, n):
    block = (BX, BY, NZ)
    cross, mixed, chip, even, even2, odd, f1z, g, b, w, d = call(
        load_kernel,
        [(X_ROWS, NZ)] * 3 + [(Y_ROWS, NZ)] * 3 + [(BX * BY, NZ)] + [block] * 4,
        g, b, n,
        hbm=3,
        vmem=None,
        scratch=[pltpu.VMEM(block, jnp.int32), (2, Y_ROWS, NZ), pltpu.SemaphoreType.DMA((3,))],
    )
    cross1 = swap(cross, cross_pairs(lambda d: not is_end(d)))
    even1 = swap(even, dev_pairs(0, lambda d: not before_end(d)))
    odd1 = swap(odd, dev_pairs(1, lambda d: not before_end(d + 1)))
    even2 = swap(even2, dev_pairs(0, before_end))
    mixed = swap(mixed, dev_pairs(1, lambda d: before_end(d + 1)) + cross_pairs(is_end))
    chip = share_chip(chip)
    left, both = call(
        gather_kernel,
        [(X_ROWS, NZ), (2, Y_ROWS, NZ)],
        cross1, even1, odd1,
        cost=pl.CostEstimate(flops=2**34, bytes_accessed=2**28, transcendentals=0),
    )
    f2, f2low, f2high, c1, wc, left, both, cross, near = call(
        middle_kernel,
        [(10 * BY, NZ), (BX, NZ), (BX, NZ), (CX * CY, CZ), (CX * CY, CZ), (X_ROWS, NZ), (2, Y_ROWS, NZ)] + [(X2_ROWS, NZ)] * 2,
        g, b, w, d, left, mixed, chip, f1z, both, even2,
        scratch=[(16, NZ), (2, 16, NZ), (8 * BY, CZ)],
    )
    cleft = swap(cross, cross_pairs(lambda d: True))
    cchip = share_chip(near)
    even, even2, odd, f2, f2low, f2high, c1x, c2z = call(
        pack_c_kernel,
        [(Z_ROWS, CZ)] * 3 + [(10 * BY, NZ), (BX, NZ), (BX, NZ), (3 * CX * CY, CZ), (10 * CY, CZ)],
        g, b, w, left, chip, both, f2, f2low, f2high, c1, wc, cleft, cchip,
        scratch=[(13, 8, NZ), (5, 8, NZ), (8, CZ), (2, Z_ROWS, CZ)],
    )
    even1 = swap(even, dev_pairs(0, lambda d: not before_end(d)))
    odd = swap(odd, dev_pairs(1, lambda d: True))
    even2 = swap(even2, dev_pairs(0, before_end))
    (out,) = call(
        last_kernel,
        [block],
        g, b, w, left, chip, both, f2, f2low, f2high, c1x, wc, cleft, cchip, c2z, even1, odd, even2,
        scratch=[
            (2, Z_ROWS, CZ),
            (16, CZ), (2, 16, CZ), (2, 8, CZ), (6 * BY + 16, CZ), (6 * BY + 16, NZ), (16, NZ), (8, NZ), (2, 16, NZ), (2, 8, NZ),
        ],
        hbm_out=True,
    )
    return out


def solution(mesh):
    s = P("group", "dev", None)
    return jax.shard_map(body, mesh=mesh, in_specs=(s, s, s), out_specs=s, check_vma=False)
```

```python
import jax
import jax.numpy as jnp
from jax import lax
from jax.sharding import PartitionSpec as P
from jax.experimental import pallas as pl
from jax.experimental.pallas import tpu as pltpu

OMEGA = 0.8
KEEP = 1.0 - OMEGA
VM = pl.BlockSpec(memory_space=pltpu.VMEM)
F32 = jnp.float32
BX, BY, NZ = 8, 16, 256
CX, CY, CZ = 4, 8, 128
RUN = 32


def call(kernel, outs, *args, scratch=(), hbm=0, hbm_out=False, vmem=8 * 2**20, cost=None):
    make = jax.ShapeDtypeStruct if hbm_out else pltpu.VMEM
    return pl.pallas_call(
        kernel,
        out_shape=[make(s, F32) for s in outs],
        in_specs=[pl.BlockSpec(memory_space=pltpu.HBM)] * hbm + [VM] * (len(args) - hbm),
        out_specs=[VM] * len(outs),
        scratch_shapes=[pltpu.VMEM(s, F32) if isinstance(s, tuple) else s for s in scratch],
        compiler_params=pltpu.CompilerParams(vmem_limit_bytes=vmem),
        cost_estimate=cost,
    )(*args)


def beside_z(v):
    lane = lax.broadcasted_iota(jnp.int32, v.shape, 1)
    last = v.shape[1] - 1
    below = jnp.where(lane == 0, 0.0, pltpu.roll(v, 1, 1))
    above = jnp.where(lane == last, 0.0, pltpu.roll(v, last, 1))
    return below + above


def shift_y(v, low, high):
    row = lax.broadcasted_iota(jnp.int32, v.shape, 0)
    last = v.shape[0] - 1
    below = jnp.where(row == 0, low, pltpu.roll(v, 1, 0))
    above = jnp.where(row == last, high, pltpu.roll(v, last, 0))
    return below, above


def beside_y(v, low, high):
    below, above = shift_y(v, low, high)
    return below + above


def slab(ref, k, rows=BY):
    return ref[k * rows : (k + 1) * rows, :]


def row(ref, k):
    return ref[k : k + 1, :]


def halved(n, m):
    a = lax.broadcasted_iota(jnp.int32, (n, m), 0)
    b = lax.broadcasted_iota(jnp.int32, (n, m), 1)
    return jnp.where((a // 2 == b) if n > m else (a == b // 2), 1.0, 0.0).astype(F32)


def lanes(v, index):
    return jnp.take_along_axis(v, index, axis=1)


def pair_z(v):
    lane = lax.broadcasted_iota(jnp.int32, (v.shape[0], CZ), 1)
    low, high = v[:, :CZ], v[:, CZ:]
    low = low + pltpu.roll(low, CZ - 1, 1)
    high = high + pltpu.roll(high, CZ - 1, 1)
    index = (2 * lane) % CZ
    return jnp.where(lane < CZ // 2, lanes(low, index), lanes(high, index))


def diag_of(n):
    return 6.0 + 0.25 * n.astype(F32)


def place(x):
    odd = lax.axis_index("group") % 2
    return x + odd * (BX - 1 - 2 * x)


def partner(ref):
    return ref.at[1 - lax.axis_index("group") % 2]


def side_of_dev():
    return lax.axis_index("dev") % 2


Y_G, Y_P, Y_W, Y_Q, Y_G2, Y_W2 = 0, 8, 16, 24, 32, 34
Y_ROWS = 40
X_ROWS = 7 * BY


def load_kernel(
    g_hbm, b_hbm, n_hbm, cross, cross2, chip, even, odd, f1z, g, b, w, d, n, both, sems
):
    copies = [
        pltpu.make_async_copy(src, dst, sems.at[k])
        for k, (src, dst) in enumerate(((g_hbm, g), (b_hbm, b), (n_hbm, n)))
    ]
    for c in copies:
        c.start()
    for c in copies:
        c.wait()
    for x in range(BX):
        diag = diag_of(n[x])
        d[x] = diag
        w[x] = OMEGA / diag
    for out, layers in ((cross, (0, 1, 2)), (chip, (7, 6, 5))):
        for k in range(3):
            out[k * BY : (k + 1) * BY, :] = g[place(layers[k])]
        for k in range(2):
            out[(3 + k) * BY : (4 + k) * BY, :] = w[place(layers[k])]
            out[(5 + k) * BY : (6 + k) * BY, :] = b[place(layers[k])]
    zero = jnp.zeros((BY, NZ), F32)
    for x in range(BX):
        at = place(x)
        here, wx, bx = g[at], w[at], b[at]
        before = g[place(x - 1)] if x else zero
        after = g[place(x + 1)] if x < BX - 1 else zero
        f = KEEP * here + wx * (bx + before + after + beside_z(here) + beside_y(here, 0.0, 0.0))
        f1z[x * BY : (x + 1) * BY, :] = f
        for s, (y, inner) in enumerate(((0, 1), (BY - 1, BY - 2))):
            rows = [
                (Y_G + x, here[y : y + 1]),
                (Y_P + x, f[y : y + 1]),
                (Y_W + x, wx[y : y + 1]),
                (Y_Q + x, wx[y : y + 1] * (bx[y : y + 1] + f[inner : inner + 1])),
            ]
            if x in (0, 7):
                rows += [(Y_G2 + x // 7, here[inner : inner + 1]), (Y_W2 + x // 7, wx[inner : inner + 1])]
            for k, v in rows:
                both[s, k : k + 1, :] = v
    p = side_of_dev()
    even[...] = both[1 - p]
    odd[...] = both[p]
    cross2[...] = cross[...]


class Wide:
    def __init__(self, g, b, w, left, right):
        self.own, self.left, self.right = (g, w, b), left, partner(right)

    def _get(self, which, base, x, y):
        if 0 <= x < BX:
            v = self.own[which]
            return v[place(x)] if y is None else v[place(x), y : y + 1, :]
        ref, k = (self.left, -1 - x) if x < 0 else (self.right, x - BX)
        return slab(ref, base + k) if y is None else row(ref, (base + k) * BY + y)

    def guess(self, x, y=None):
        return self._get(0, 0, x, y)

    def w(self, x, y=None):
        return self._get(1, 3, x, y)

    def rhs(self, x, y=None):
        return self._get(2, 5, x, y)


def take(both, even, odd):
    p = side_of_dev()
    both[1 - p] = even
    both[p] = odd


def again_kernel(even, odd, chip, met, even2, odd2, chip2):
    chip2[...] = chip[...]
    even2[...] = even[...]
    odd2[...] = odd[...]


def gather_kernel(cross, even, odd, left, both):
    left[...] = cross[...]
    take(both, even[...], odd[...])


X2_D = 3 * BY
X2_ROWS = X2_D + 16


def diagonal_rows(edge):
    at, inner = (0, 1) if edge == 0 else (7, 6)
    return (Y_G + at, Y_G2 + edge, Y_G + inner, Y_P + at, Y_W + at, Y_W2 + edge, Y_W + inner)


def middle_kernel(
    g, b, w, d, left1, cross2, chip, f1z, both1, even2, odd2,
    f2, f2low, f2high, c1, wc, left, both, lo, hi, col, line, sums,
):
    left[...] = left1[...] + cross2[...]
    a = Wide(g, b, w, left, chip)
    p = side_of_dev()
    both[p] = both1[p] + odd2[...]
    both[1 - p] = both1[1 - p] + even2[...]
    low, high = both.at[0], both.at[1]
    rows = lax.broadcasted_iota(jnp.int32, (BY, NZ), 0)
    f1 = {}
    for x in range(-2, 10):
        if 0 <= x < BX:
            k = Y_G + x
            beyond = jnp.where(rows == 0, row(low, k), jnp.where(rows == BY - 1, row(high, k), 0.0))
            if x == 0:
                beyond = beyond + a.guess(-1)
            if x == BX - 1:
                beyond = beyond + a.guess(BX)
            f1[x] = slab(f1z, x) + a.w(x) * beyond
        else:
            here = a.guess(x)
            f1[x] = KEEP * here + a.w(x) * (
                a.rhs(x) + a.guess(x - 1) + a.guess(x + 1) + beside_z(here) + beside_y(here, 0.0, 0.0)
            )
    for s, (side, y, out) in enumerate(((low, 0, f2low), (high, BY - 1, f2high))):
        for x in range(BX):
            col[x : x + 1, :] = a.guess(x, y)
        line[s, 0:16, :] = jnp.zeros((16, NZ), F32)
        line[s, 1:9, :] = side[Y_P : Y_P + 8, :] + side[Y_W : Y_W + 8, :] * col[0:8, :]
        for x in range(BX):
            col[x : x + 1, :] = f1[x][y : y + 1]
        mid = line[s, 1:9, :]
        out[...] = (
            KEEP * mid
            + side[Y_Q : Y_Q + 8, :]
            + side[Y_W : Y_W + 8, :] * (line[s, 0:8, :] + line[s, 2:10, :] + beside_z(mid) + col[0:8, :])
        )
        for edge, pack in enumerate((lo, hi)):
            for k, r in enumerate(diagonal_rows(edge)):
                at = X2_D + 7 * s + k
                pack[at : at + 1, :] = row(side, r)
    for pack in (lo, hi):
        pack[X2_D + 14 :, :] = jnp.zeros((2, NZ), F32)
    sec = {}
    for x in range(-1, 9):
        f = f1[x]
        sec[x] = KEEP * f + a.w(x) * (
            a.rhs(x)
            + f1[x - 1]
            + f1[x + 1]
            + beside_z(f)
            + beside_y(f, line[0, x + 1 : x + 2, :], line[1, x + 1 : x + 2, :])
        )
        f2[(x + 1) * BY : (x + 2) * BY, :] = sec[x]
    lo[2 * BY : X2_D, :] = sec[1]
    hi[2 * BY : X2_D, :] = sec[6]
    pairs, points = [], []
    for x in range(0, 8):
        f = sec[x]
        r = (
            a.rhs(x)
            - d[place(x)] * f
            + sec[x - 1]
            + sec[x + 1]
            + beside_z(f)
            + beside_y(f, row(f2low, x), row(f2high, x))
        )
        if x % 2:
            pairs[-1] = pairs[-1] + r
            points[-1] = points[-1] + d[place(x)]
        else:
            pairs.append(r)
            points.append(d[place(x)])
    sums[...] = lax.dot_general(
        jnp.concatenate(pairs + points, axis=0),
        halved(NZ, CZ),
        (((1,), (0,)), ((), ())),
        precision=lax.Precision.HIGHEST,
        preferred_element_type=F32,
    )
    for x in range(CX):
        at = x * BY
        total = sums[pl.ds(at, CY, stride=2), :] + sums[pl.ds(at + 1, CY, stride=2), :]
        at = (CX + x) * BY
        diags = sums[pl.ds(at, CY, stride=2), :] + sums[pl.ds(at + 1, CY, stride=2), :]
        weight = OMEGA / (0.5 * diags - 18.0)
        first = weight * (0.5 * total)
        c1[x * CY : (x + 1) * CY, :] = first
        wc[x * CY : (x + 1) * CY, :] = weight
        for out, k in ((lo, x), (hi, CX - 1 - x)):
            out[k * CY : (k + 1) * CY, 0:CZ] = first
            out[k * CY : (k + 1) * CY, CZ:] = weight


class Coarse:
    def __init__(self, c1x, wc, left, right):
        self.c1x, self.wc, self.left, self.right = c1x, wc, left, right

    def first(self, x):
        return slab(self.c1x, x + CX, CY)

    def w(self, x):
        if 0 <= x < CX:
            return slab(self.wc, x, CY)
        ref, k = (self.left, -1 - x) if x < 0 else (self.right, x - CX)
        return ref[k * CY : (k + 1) * CY, CZ:]


def corner_terms(a, low, high, relays, put):
    for e, (xe, xi, xn, xm) in enumerate(((0, 1, -1, -2), (7, 6, 8, 9))):
        for s, (side, y, yi) in enumerate(((low, 0, 1), (high, BY - 1, BY - 2))):
            own = [row(side, r) for r in diagonal_rows(e)]
            far = [row(relays[e], X2_D + 7 * s + k) for k in range(7)]
            corner, beside = a.guess(xe, y), a.guess(xn, y)
            w_corner, w_beside = a.w(xe, y), a.w(xn, y)
            put(2 * e + s, far[:5] + [beside + own[0], w_beside, a.w(xm, y), a.w(xn, yi), own[4], own[5], own[6], w_corner])
            put(4 + 2 * e + s, own[:5] + [corner + far[0], w_corner, a.w(xi, y), a.w(xe, yi), far[4], far[5], far[6], w_beside])


def corner_sums(t):
    g1, g2, g3, part, wd, near, wx, wx2, wxs, wy, wy2, wys, wq = (t[k] for k in range(13))
    dq = jnp.where(wq > 0.0, OMEGA / jnp.where(wq > 0.0, wq, 1.0), 0.0)
    by_y = wy * g1
    by_x = wx * g1
    diagonal = part + wd * near
    at_q = wq * (by_x + by_y)
    at_y = KEEP * by_y + wy * (beside_z(by_y) + diagonal + wy2 * g2)
    at_x = KEEP * by_x + wx * (beside_z(by_x) + diagonal + wx2 * g3)
    at_ys = wys * by_y
    at_xs = wxs * by_x
    total = at_y + at_x + beside_z(at_q) - dq * at_q + 2.0 * at_q + at_ys + at_xs
    return at_q, at_y, at_x, at_ys, at_xs, 0.5 * pair_z(total)


Z_C, Z_P, Z_W, Z_Q, Z_R, Z_V, Z_S, Z_K = 0, 10, 20, 30, 38, 44, 50, 66
Z_ROWS = 72


def pack_c_kernel(
    g, b, w, left, chip, both, f2in, f2lowin, f2highin, c1, wc, cleft, cchip,
    even, even2, odd, f2, f2low, f2high, c1x, c2z, table, terms, rows, sides,
):
    fine = Wide(g, b, w, left, chip)
    cright = partner(cchip)

    def put(i, values):
        for k, v in enumerate(values):
            table[k, i : i + 1, :] = v

    corner_terms(fine, both.at[0], both.at[1], (cleft, cright), put)
    *parts, share = corner_sums(table)
    for k, v in enumerate(parts):
        terms[k] = v
    rows[...] = share
    a = Coarse(c1x, wc, cleft, cright)
    for x in range(CX):
        c1x[(x + CX) * CY : (x + CX + 1) * CY, :] = slab(c1, x, CY)
        c1x[(CX - 1 - x) * CY : (CX - x) * CY, :] = cleft[x * CY : (x + 1) * CY, 0:CZ]
        c1x[(x + 2 * CX) * CY : (x + 2 * CX + 1) * CY, :] = cright[x * CY : (x + 1) * CY, 0:CZ]
    f2[...] = f2in[...]
    f2low[...] = f2lowin[...]
    f2high[...] = f2highin[...]

    def add(ref, k, v):
        ref[k : k + 1, :] = ref[k : k + 1, :] + v

    for e, (xe, xi, xn, cxe, cxn) in enumerate(((0, 1, -1, 0, -1), (7, 6, 8, 3, 4))):
        for s, (side, y, yi, cy) in enumerate(((f2low, 0, 1, 0), (f2high, BY - 1, BY - 2, CY - 1))):
            i = 2 * e + s
            add(f2, (xe + 1) * BY + y, terms[0, i : i + 1, :])
            add(side, xe, terms[1, i : i + 1, :])
            add(f2, (xn + 1) * BY + y, terms[2, i : i + 1, :])
            add(side, xi, terms[3, i : i + 1, :])
            add(f2, (xn + 1) * BY + yi, terms[4, i : i + 1, :])
            add(c1x, (cxe + CX) * CY + cy, a.w(cxe)[cy : cy + 1] * rows[i : i + 1, :])
            add(c1x, (cxn + CX) * CY + cy, a.w(cxn)[cy : cy + 1] * rows[i + 4 : i + 5, :])
    lo, hi = sides.at[0], sides.at[1]
    second = {}
    for x in range(-3, 7):
        c, cw = a.first(x), a.w(x)
        second[x] = (1.0 + KEEP) * c + cw * (
            a.first(x - 1) + a.first(x + 1) + beside_z(c) + beside_y(c, 0.0, 0.0)
        )
        c2z[(x + 3) * CY : (x + 4) * CY, :] = second[x]
        for out, y in ((lo, 0), (hi, CY - 1)):
            for base, v in ((Z_C, c), (Z_P, second[x]), (Z_W, cw)):
                k = base + x + 3
                out[k : k + 1, :] = v[y : y + 1]
    for x in range(-2, 6):
        s, c, cw = second[x], a.first(x), a.w(x)
        below, above = shift_y(s, 0.0, 0.0)
        inner = {0: above, 1: below}
        for side, (out, y, y2) in enumerate(((lo, 0, 1), (hi, CY - 1, CY - 2))):
            k = Z_Q + x + 2
            out[k : k + 1, :] = (c + cw * inner[side])[y : y + 1]
        if -1 <= x <= 4:
            part = KEEP * s + c + cw * (second[x - 1] + second[x + 1] + beside_z(s))
            for side, (out, y, y2) in enumerate(((lo, 0, 1), (hi, CY - 1, CY - 2))):
                k = Z_R + x + 1
                out[k : k + 1, :] = (part + cw * inner[side])[y2 : y2 + 1]
                k = Z_V + x + 1
                out[k : k + 1, :] = cw[y2 : y2 + 1]
    for out, y, inner in ((lo, 0, 1), (hi, BY - 1, BY - 2)):
        for x in range(BX):
            at = (x + 1) * BY
            v = fine.w(x, y) * (fine.rhs(x, y) + row(f2, at + inner))
            for half in range(2):
                k = Z_S + 2 * x + half
                out[k : k + 1, :] = v[:, half * CZ : (half + 1) * CZ]
        for j, x in enumerate((-1, 8)):
            at = (x + 1) * BY + y
            v = f2[at : at + 1, :]
            for half in range(2):
                k = Z_K + 2 * j + half
                out[k : k + 1, :] = v[:, half * CZ : (half + 1) * CZ]
    p = side_of_dev()
    even[...] = sides[1 - p]
    even2[...] = sides[1 - p]
    odd[...] = sides[p]


def last_kernel(
    g, b, w, left, chip, both, f2, f2low, f2high, c1x, wc, cleft, cchip, c2z, even1, odd, even2,
    out, cboth, col, line, line3, fine, corr, col2, s1, gline, g1line,
):
    wide = Wide(g, b, w, left, chip)
    a = Coarse(c1x, wc, cleft, partner(cchip))
    take(cboth, even1[...] + even2[...], odd[...])
    low, high, clow, chigh = both.at[0], both.at[1], cboth.at[0], cboth.at[1]
    crow = lax.broadcasted_iota(jnp.int32, (CY, CZ), 0)
    c2 = {}
    for x in range(-3, 7):
        k = Z_C + x + 3
        beyond = jnp.where(crow == 0, row(clow, k), jnp.where(crow == CY - 1, row(chigh, k), 0.0))
        c2[x] = slab(c2z, x + 3, CY) + a.w(x) * beyond
    sides = ((clow, 0), (chigh, CY - 1))
    for s, (side, y) in enumerate(sides):
        for x in range(-3, 7):
            col[x + 3 : x + 4, :] = a.first(x)[y : y + 1]
        line[s, 0:10, :] = side[Z_P : Z_P + 10, :] + side[Z_W : Z_W + 10, :] * col[0:10, :]
        for x in range(-2, 6):
            col[x + 2 : x + 3, :] = c2[x][y : y + 1]
        mid = line[s, 1:9, :]
        line3[s, 0:8, :] = (
            KEEP * mid
            + side[Z_Q : Z_Q + 8, :]
            + side[Z_W + 1 : Z_W + 9, :]
            * (line[s, 0:8, :] + line[s, 2:10, :] + beside_z(mid) + col[0:8, :])
        )
    c3 = {}
    for x in range(-2, 6):
        c = c2[x]
        c3[x] = KEEP * c + a.first(x) + a.w(x) * (
            c2[x - 1]
            + c2[x + 1]
            + beside_z(c)
            + beside_y(c, line[0, x + 3 : x + 4, :], line[1, x + 3 : x + 4, :])
        )
    for x in range(-1, 5):
        c = c3[x]
        c4 = KEEP * c + a.first(x) + a.w(x) * (
            c3[x - 1]
            + c3[x + 1]
            + beside_z(c)
            + beside_y(c, line3[0, x + 2 : x + 3, :], line3[1, x + 2 : x + 3, :])
        )
        fine[pl.ds((x + 1) * BY, CY, stride=2), :] = c4
        fine[pl.ds((x + 1) * BY + 1, CY, stride=2), :] = c4
    for s, (side, y) in enumerate(sides):
        for x in range(-1, 5):
            col[x + 1 : x + 2, :] = c3[x][y : y + 1]
        mid = line3[s, 1:7, :]
        third = side[Z_R : Z_R + 6, :] + side[Z_V : Z_V + 6, :] * line[s, 2:8, :]
        fine[6 * BY + 8 * s : 6 * BY + 8 * s + 6, :] = (
            KEEP * mid
            + side[Z_C + 2 : Z_C + 8, :]
            + side[Z_W + 2 : Z_W + 8, :]
            * (line3[s, 0:6, :] + line3[s, 2:8, :] + beside_z(mid) + third + col[0:6, :])
        )
        fine[6 * BY + 8 * s + 6 : 6 * BY + 8 * s + 8, :] = jnp.zeros((2, CZ), F32)
    corr[...] = lax.dot_general(
        fine[...],
        halved(CZ, NZ),
        (((1,), (0,)), ((), ())),
        precision=lax.Precision.HIGHEST,
        preferred_element_type=F32,
    )
    g0 = {}
    for x in range(-2, 10):
        if x == -2:
            f = slab(cleft, 2)
        elif x == 9:
            f = slab(a.right, 2)
        else:
            f = slab(f2, x + 1)
        g0[x] = f + slab(corr, (x + 2) // 2)
    for s, (cside, side, y, f2side) in enumerate(((clow, low, 0, f2low), (chigh, high, BY - 1, f2high))):
        base = 6 * BY + 8 * s
        for x in range(-1, 9):
            k = base + (x + 2) // 2
            col2[x + 1 : x + 2, :] = corr[k : k + 1, :]
        gline[s, 1:9, :] = f2side[...] + col2[1:9, :]
        for j, x in enumerate((-1, 8)):
            k = Z_K + 2 * j
            gline[s, x + 1 : x + 2, 0:CZ] = row(cside, k) + col2[x + 1 : x + 2, 0:CZ]
            gline[s, x + 1 : x + 2, CZ:] = row(cside, k + 1) + col2[x + 1 : x + 2, CZ:]
        for x in range(BX):
            k = Z_S + 2 * x
            s1[x : x + 1, 0:CZ] = row(cside, k)
            s1[x : x + 1, CZ:] = row(cside, k + 1)
        moved = col2[1:9, :]
        for x in range(BX):
            col2[x : x + 1, :] = g0[x][y : y + 1]
        mid = gline[s, 1:9, :]
        g1line[s, 0:8, :] = (
            KEEP * mid
            + s1[0:8, :]
            + side[Y_W : Y_W + 8, :]
            * (moved + gline[s, 0:8, :] + gline[s, 2:10, :] + beside_z(mid) + col2[0:8, :])
        )
    g1 = {}
    for x in range(-1, 9):
        f = g0[x]
        g1[x] = KEEP * f + wide.w(x) * (
            wide.rhs(x)
            + g0[x - 1]
            + g0[x + 1]
            + beside_z(f)
            + beside_y(f, gline[0, x + 1 : x + 2, :], gline[1, x + 1 : x + 2, :])
        )
    for x in range(BX):
        f = g1[x]
        out[place(x)] = KEEP * f + wide.w(x) * (
            wide.rhs(x)
            + g1[x - 1]
            + g1[x + 1]
            + beside_z(f)
            + beside_y(f, g1line[0, x : x + 1, :], g1line[1, x : x + 1, :])
        )


def swap(v, pairs):
    n = lax.axis_size("dev")
    links = [(i * n + j, k * n + l) for (i, j), (k, l) in pairs]
    return lax.ppermute(v, ("group", "dev"), links + [(j, i) for i, j in links])


def share_chip(v):
    groups = [[i, i + 1] for i in range(0, lax.axis_size("group"), 2)]
    return lax.all_gather(v, "group", axis_index_groups=groups)


def cross_pairs(keep):
    devs = [d for d in range(lax.axis_size("dev")) if keep(d)]
    return [((i, d), (i + 1, d)) for i in range(1, lax.axis_size("group") - 1, 2) for d in devs]


def dev_pairs(start, keep):
    devs = [d for d in range(start, lax.axis_size("dev") - 1, 2) if keep(d)]
    return [((i, d), (i, d + 1)) for i in range(lax.axis_size("group")) for d in devs]


def is_end(d):
    return d % RUN == RUN - 1


def before_end(d):
    return d % RUN == RUN - 2


def body(g, b, n):
    block = (BX, BY, NZ)
    cross, cross2, chip, even, odd, f1z, g, b, w, d = call(
        load_kernel,
        [(X_ROWS, NZ)] * 3 + [(Y_ROWS, NZ)] * 2 + [(BX * BY, NZ)] + [block] * 4,
        g, b, n,
        hbm=3,
        vmem=None,
        scratch=[pltpu.VMEM(block, jnp.int32), (2, Y_ROWS, NZ), pltpu.SemaphoreType.DMA((3,))],
    )
    cross1 = swap(cross, cross_pairs(lambda d: not is_end(d)))
    even1 = swap(even, dev_pairs(0, lambda d: not before_end(d)))
    odd1 = swap(odd, dev_pairs(1, lambda d: not before_end(d + 1)))
    cross2 = swap(cross2, cross_pairs(is_end))
    even2, odd2, chip = call(again_kernel, [(Y_ROWS, NZ)] * 2 + [(X_ROWS, NZ)], even, odd, chip, even1)
    even2 = swap(even2, dev_pairs(0, before_end))
    odd2 = swap(odd2, dev_pairs(1, lambda d: before_end(d + 1)))
    chip = share_chip(chip)
    left, both = call(
        gather_kernel,
        [(X_ROWS, NZ), (2, Y_ROWS, NZ)],
        cross1, even1, odd1,
        cost=pl.CostEstimate(flops=2**34, bytes_accessed=0, transcendentals=0),
    )
    f2, f2low, f2high, c1, wc, left, both, cross, near = call(
        middle_kernel,
        [(10 * BY, NZ), (BX, NZ), (BX, NZ), (CX * CY, CZ), (CX * CY, CZ), (X_ROWS, NZ), (2, Y_ROWS, NZ)] + [(X2_ROWS, NZ)] * 2,
        g, b, w, d, left, cross2, chip, f1z, both, even2, odd2,
        scratch=[(16, NZ), (2, 16, NZ), (8 * BY, CZ)],
    )
    cleft = swap(cross, cross_pairs(lambda d: True))
    cchip = share_chip(near)
    even, even2, odd, f2, f2low, f2high, c1x, c2z = call(
        pack_c_kernel,
        [(Z_ROWS, CZ)] * 3 + [(10 * BY, NZ), (BX, NZ), (BX, NZ), (3 * CX * CY, CZ), (10 * CY, CZ)],
        g, b, w, left, chip, both, f2, f2low, f2high, c1, wc, cleft, cchip,
        scratch=[(13, 8, NZ), (5, 8, NZ), (8, CZ), (2, Z_ROWS, CZ)],
    )
    even1 = swap(even, dev_pairs(0, lambda d: not before_end(d)))
    odd = swap(odd, dev_pairs(1, lambda d: True))
    even2 = swap(even2, dev_pairs(0, before_end))
    (out,) = call(
        last_kernel,
        [block],
        g, b, w, left, chip, both, f2, f2low, f2high, c1x, wc, cleft, cchip, c2z, even1, odd, even2,
        scratch=[
            (2, Z_ROWS, CZ),
            (16, CZ), (2, 16, CZ), (2, 8, CZ), (6 * BY + 16, CZ), (6 * BY + 16, NZ), (16, NZ), (8, NZ), (2, 16, NZ), (2, 8, NZ),
        ],
        hbm_out=True,
    )
    return out


def solution(mesh):
    s = P("group", "dev", None)
    return jax.shard_map(body, mesh=mesh, in_specs=(s, s, s), out_specs=s, check_vma=False)
```

```python
import jax
import jax.numpy as jnp
from jax import lax
from jax.sharding import PartitionSpec as P
from jax.experimental import pallas as pl
from jax.experimental.pallas import tpu as pltpu

OMEGA = 0.8
KEEP = 1.0 - OMEGA
VM = pl.BlockSpec(memory_space=pltpu.VMEM)
F32 = jnp.float32
BX, BY, NZ = 8, 16, 256
CX, CY, CZ = 4, 8, 128
RUN = 32


def call(kernel, outs, *args, scratch=(), hbm=0, hbm_out=False, vmem=8 * 2**20, cost=None):
    make = jax.ShapeDtypeStruct if hbm_out else pltpu.VMEM
    return pl.pallas_call(
        kernel,
        out_shape=[make(s, F32) for s in outs],
        in_specs=[pl.BlockSpec(memory_space=pltpu.HBM)] * hbm + [VM] * (len(args) - hbm),
        out_specs=[VM] * len(outs),
        scratch_shapes=[pltpu.VMEM(s, F32) if isinstance(s, tuple) else s for s in scratch],
        compiler_params=pltpu.CompilerParams(vmem_limit_bytes=vmem),
        cost_estimate=cost,
    )(*args)


def beside_z(v):
    lane = lax.broadcasted_iota(jnp.int32, v.shape, 1)
    last = v.shape[1] - 1
    below = jnp.where(lane == 0, 0.0, pltpu.roll(v, 1, 1))
    above = jnp.where(lane == last, 0.0, pltpu.roll(v, last, 1))
    return below + above


def shift_y(v, low, high):
    row = lax.broadcasted_iota(jnp.int32, v.shape, 0)
    last = v.shape[0] - 1
    below = jnp.where(row == 0, low, pltpu.roll(v, 1, 0))
    above = jnp.where(row == last, high, pltpu.roll(v, last, 0))
    return below, above


def beside_y(v, low, high):
    below, above = shift_y(v, low, high)
    return below + above


def slab(ref, k, rows=BY):
    return ref[k * rows : (k + 1) * rows, :]


def by_row(n, rows):
    total = 0.0
    for k, v in rows.items():
        at = lax.broadcasted_iota(jnp.int32, (n, v.shape[1]), 0)
        total = jnp.where(at == k, v, total)
    return total


def row(ref, k):
    return ref[k : k + 1, :]


def lanes(v, index):
    return jnp.take_along_axis(v, index, axis=1)


def pair_z(low, high):
    lane = lax.broadcasted_iota(jnp.int32, low.shape, 1)
    low = low + pltpu.roll(low, CZ - 1, 1)
    high = high + pltpu.roll(high, CZ - 1, 1)
    index = (2 * lane) % CZ
    return jnp.where(lane < CZ // 2, lanes(low, index), lanes(high, index))


def spread_z(v, out):
    half = lax.broadcasted_iota(jnp.int32, v.shape, 1) // 2
    out[:, :CZ] = lanes(v, half)
    out[:, CZ:] = lanes(v, half + CZ // 2)


def diag_of(n):
    return 6.0 + 0.25 * n.astype(F32)


def place(x):
    odd = lax.axis_index("group") % 2
    return x + odd * (BX - 1 - 2 * x)


def partner(ref):
    return ref.at[1 - lax.axis_index("group") % 2]


def side_of_dev():
    return lax.axis_index("dev") % 2


Y_G, Y_P, Y_W, Y_Q, Y_G2, Y_W2 = 0, 8, 16, 24, 32, 34
Y_ROWS = 40
X_ROWS = 7 * BY


def load_kernel(
    g_hbm, b_hbm, n_hbm, cross, chip, even, odd, f1z, g, b, w, d, n, both, sems
):
    copies = [
        pltpu.make_async_copy(src, dst, sems.at[k])
        for k, (src, dst) in enumerate(((g_hbm, g), (b_hbm, b), (n_hbm, n)))
    ]
    for c in copies:
        c.start()
    for c in copies:
        c.wait()
    for x in range(BX):
        diag = diag_of(n[x])
        d[x] = diag
        w[x] = OMEGA / diag
    for out, layers in ((cross, (0, 1, 2)), (chip, (7, 6, 5))):
        for k in range(3):
            out[k * BY : (k + 1) * BY, :] = g[place(layers[k])]
        for k in range(2):
            out[(3 + k) * BY : (4 + k) * BY, :] = w[place(layers[k])]
            out[(5 + k) * BY : (6 + k) * BY, :] = b[place(layers[k])]
    zero = jnp.zeros((BY, NZ), F32)
    for x in range(BX):
        at = place(x)
        here, wx, bx = g[at], w[at], b[at]
        before = g[place(x - 1)] if x else zero
        after = g[place(x + 1)] if x < BX - 1 else zero
        f = KEEP * here + wx * (bx + before + after + beside_z(here) + beside_y(here, 0.0, 0.0))
        f1z[x * BY : (x + 1) * BY, :] = f
        for s, (y, inner) in enumerate(((0, 1), (BY - 1, BY - 2))):
            rows = [
                (Y_G + x, here[y : y + 1]),
                (Y_P + x, f[y : y + 1]),
                (Y_W + x, wx[y : y + 1]),
                (Y_Q + x, wx[y : y + 1] * (bx[y : y + 1] + f[inner : inner + 1])),
            ]
            if x in (0, 7):
                rows += [(Y_G2 + x // 7, here[inner : inner + 1]), (Y_W2 + x // 7, wx[inner : inner + 1])]
            for k, v in rows:
                both[s, k : k + 1, :] = v
    p = side_of_dev()
    even[...] = both[1 - p]
    odd[...] = both[p]


class Wide:
    def __init__(self, g, b, w, left, right):
        self.own, self.left, self.right = (g, w, b), left, partner(right)

    def _get(self, which, base, x, y):
        if 0 <= x < BX:
            v = self.own[which]
            return v[place(x)] if y is None else v[place(x), y : y + 1, :]
        ref, k = (self.left, -1 - x) if x < 0 else (self.right, x - BX)
        return slab(ref, base + k) if y is None else row(ref, (base + k) * BY + y)

    def guess(self, x, y=None):
        return self._get(0, 0, x, y)

    def w(self, x, y=None):
        return self._get(1, 3, x, y)

    def rhs(self, x, y=None):
        return self._get(2, 5, x, y)


def take(both, even, odd):
    p = side_of_dev()
    both[1 - p] = even
    both[p] = odd


def again_kernel(cross, even, odd, chip, met, cross2, even2, odd2, chip2):
    even2[...] = even[...]
    cross2[...] = cross[...]
    odd2[...] = odd[...]
    chip2[...] = chip[...]


def gather_kernel(cross, even, odd, left, both):
    left[...] = cross[...]
    take(both, even[...], odd[...])


X2_D = 3 * BY
X2_ROWS = X2_D + 16


def diagonal_rows(edge):
    at, inner = (0, 1) if edge == 0 else (7, 6)
    return (Y_G + at, Y_G2 + edge, Y_G + inner, Y_P + at, Y_W + at, Y_W2 + edge, Y_W + inner)


def middle_kernel(
    g, b, w, d, left1, cross2, chip, f1z, both1, even2, odd2,
    f2, f2low, f2high, c1, wc, left, both, lo, hi, col, line, sums,
):
    left[...] = left1[...] + cross2[...]
    a = Wide(g, b, w, left, chip)
    p = side_of_dev()
    both[p] = both1[p] + odd2[...]
    both[1 - p] = both1[1 - p] + even2[...]
    low, high = both.at[0], both.at[1]
    rows = lax.broadcasted_iota(jnp.int32, (BY, NZ), 0)
    f1 = {}
    for x in range(-2, 10):
        if 0 <= x < BX:
            k = Y_G + x
            beyond = jnp.where(rows == 0, row(low, k), jnp.where(rows == BY - 1, row(high, k), 0.0))
            if x == 0:
                beyond = beyond + a.guess(-1)
            if x == BX - 1:
                beyond = beyond + a.guess(BX)
            f1[x] = slab(f1z, x) + a.w(x) * beyond
        else:
            here = a.guess(x)
            f1[x] = KEEP * here + a.w(x) * (
                a.rhs(x) + a.guess(x - 1) + a.guess(x + 1) + beside_z(here) + beside_y(here, 0.0, 0.0)
            )
    for s, (side, y, out) in enumerate(((low, 0, f2low), (high, BY - 1, f2high))):
        for x in range(BX):
            col[x : x + 1, :] = a.guess(x, y)
        line[s, 0:16, :] = jnp.zeros((16, NZ), F32)
        line[s, 1:9, :] = side[Y_P : Y_P + 8, :] + side[Y_W : Y_W + 8, :] * col[0:8, :]
        for x in range(BX):
            col[x : x + 1, :] = f1[x][y : y + 1]
        mid = line[s, 1:9, :]
        out[...] = (
            KEEP * mid
            + side[Y_Q : Y_Q + 8, :]
            + side[Y_W : Y_W + 8, :] * (line[s, 0:8, :] + line[s, 2:10, :] + beside_z(mid) + col[0:8, :])
        )
        for edge, pack in enumerate((lo, hi)):
            for k, r in enumerate(diagonal_rows(edge)):
                at = X2_D + 7 * s + k
                pack[at : at + 1, :] = row(side, r)
    for pack in (lo, hi):
        pack[X2_D + 14 :, :] = jnp.zeros((2, NZ), F32)
    sec = {}
    for x in range(-1, 9):
        f = f1[x]
        sec[x] = KEEP * f + a.w(x) * (
            a.rhs(x)
            + f1[x - 1]
            + f1[x + 1]
            + beside_z(f)
            + beside_y(f, line[0, x + 1 : x + 2, :], line[1, x + 1 : x + 2, :])
        )
        f2[(x + 1) * BY : (x + 2) * BY, :] = sec[x]
    lo[2 * BY : X2_D, :] = sec[1]
    hi[2 * BY : X2_D, :] = sec[6]
    for x in range(0, 8):
        f = sec[x]
        r = (
            a.rhs(x)
            - d[place(x)] * f
            + sec[x - 1]
            + sec[x + 1]
            + beside_z(f)
            + beside_y(f, row(f2low, x), row(f2high, x))
        )
        if x % 2:
            pairs = pairs + r
            points = points + d[place(x)]
            at = (x // 2) * BY
            for half in range(2):
                sums[half, at : at + BY, :] = pairs[:, half * CZ : (half + 1) * CZ]
                sums[2 + half, at : at + BY, :] = points[:, half * CZ : (half + 1) * CZ]
        else:
            pairs, points = r, d[place(x)]
    doubled = [
        sums[k, pl.ds(0, CX * CY, stride=2), :] + sums[k, pl.ds(1, CX * CY, stride=2), :] for k in range(4)
    ]
    total = pair_z(doubled[0], doubled[1])
    diags = pair_z(doubled[2], doubled[3])
    weight = OMEGA / (0.5 * diags - 18.0)
    first = weight * (0.5 * total)
    c1[...] = first
    wc[...] = weight
    for x in range(CX):
        for out, k in ((lo, x), (hi, CX - 1 - x)):
            out[k * CY : (k + 1) * CY, 0:CZ] = first[x * CY : (x + 1) * CY]
            out[k * CY : (k + 1) * CY, CZ:] = weight[x * CY : (x + 1) * CY]


class Coarse:
    def __init__(self, c1x, wc, left, right):
        self.c1x, self.wc, self.left, self.right = c1x, wc, left, right

    def first(self, x):
        return slab(self.c1x, x + CX, CY)

    def w(self, x):
        if 0 <= x < CX:
            return slab(self.wc, x, CY)
        ref, k = (self.left, -1 - x) if x < 0 else (self.right, x - CX)
        return ref[k * CY : (k + 1) * CY, CZ:]


def corner_terms(a, low, high, relays, put):
    for e, (xe, xi, xn, xm) in enumerate(((0, 1, -1, -2), (7, 6, 8, 9))):
        for s, (side, y, yi) in enumerate(((low, 0, 1), (high, BY - 1, BY - 2))):
            own = [row(side, r) for r in diagonal_rows(e)]
            far = [row(relays[e], X2_D + 7 * s + k) for k in range(7)]
            corner, beside = a.guess(xe, y), a.guess(xn, y)
            w_corner, w_beside = a.w(xe, y), a.w(xn, y)
            put(2 * e + s, far[:5] + [beside + own[0], w_beside, a.w(xm, y), a.w(xn, yi), own[4], own[5], own[6], w_corner])
            put(4 + 2 * e + s, own[:5] + [corner + far[0], w_corner, a.w(xi, y), a.w(xe, yi), far[4], far[5], far[6], w_beside])


def corner_sums(t):
    g1, g2, g3, part, wd, near, wx, wx2, wxs, wy, wy2, wys, wq = (t[k] for k in range(13))
    dq = jnp.where(wq > 0.0, OMEGA / jnp.where(wq > 0.0, wq, 1.0), 0.0)
    by_y = wy * g1
    by_x = wx * g1
    diagonal = part + wd * near
    at_q = wq * (by_x + by_y)
    at_y = KEEP * by_y + wy * (beside_z(by_y) + diagonal + wy2 * g2)
    at_x = KEEP * by_x + wx * (beside_z(by_x) + diagonal + wx2 * g3)
    at_ys = wys * by_y
    at_xs = wxs * by_x
    total = at_y + at_x + beside_z(at_q) - dq * at_q + 2.0 * at_q + at_ys + at_xs
    return at_q, at_y, at_x, at_ys, at_xs, 0.5 * pair_z(total[:, :CZ], total[:, CZ:])


Z_C, Z_P, Z_W, Z_Q, Z_R, Z_V, Z_S, Z_K = 0, 10, 20, 30, 38, 44, 50, 66
Z_ROWS = 72


def pack_c_kernel(
    g, b, w, left, chip, both, f2in, f2lowin, f2highin, c1, wc, cleft, cchip,
    even, even2, odd, f2, f2low, f2high, c1x, c2z, table, terms, rows, sides,
):
    fine = Wide(g, b, w, left, chip)
    cright = partner(cchip)

    def put(i, values):
        for k, v in enumerate(values):
            table[k, i : i + 1, :] = v

    corner_terms(fine, both.at[0], both.at[1], (cleft, cright), put)
    *parts, share = corner_sums(table)
    for k, v in enumerate(parts):
        terms[k] = v
    rows[...] = share
    a = Coarse(c1x, wc, cleft, cright)
    for x in range(1, CX):
        c1x[(CX - 1 - x) * CY : (CX - x) * CY, :] = cleft[x * CY : (x + 1) * CY, 0:CZ]
        c1x[(x + 2 * CX) * CY : (x + 2 * CX + 1) * CY, :] = cright[x * CY : (x + 1) * CY, 0:CZ]
    for x in range(1, CX - 1):
        c1x[(x + CX) * CY : (x + CX + 1) * CY, :] = slab(c1, x, CY)
    term = lambda k, e, s: terms[k, 2 * e + s : 2 * e + s + 1, :]
    for e, (xe, xn, cxe, cxn) in enumerate(((0, -1, 0, -1), (7, 8, 3, 4))):
        at = (xe + 1) * BY
        f2[at : at + BY, :] = f2in[at : at + BY, :] + by_row(BY, {0: term(0, e, 0), BY - 1: term(0, e, 1)})
        at = (xn + 1) * BY
        f2[at : at + BY, :] = f2in[at : at + BY, :] + by_row(
            BY, {0: term(2, e, 0), 1: term(4, e, 0), BY - 2: term(4, e, 1), BY - 1: term(2, e, 1)}
        )
        for i, cx in ((2 * e, cxe), (2 * e + 4, cxn)):
            at = (cx + CX) * CY
            given = slab(c1, cx, CY) if 0 <= cx < CX else (cleft if cx < 0 else cright)[0:CY, 0:CZ]
            c1x[at : at + CY, :] = given + a.w(cx) * by_row(CY, {0: row(rows, i), CY - 1: row(rows, i + 1)})
    f2[2 * BY : 8 * BY, :] = f2in[2 * BY : 8 * BY, :]
    for s, (side, sidein) in enumerate(((f2low, f2lowin), (f2high, f2highin))):
        side[...] = sidein[...] + by_row(
            BX, {0: term(1, 0, s), 1: term(3, 0, s), BX - 2: term(3, 1, s), BX - 1: term(1, 1, s)}
        )
    lo, hi = sides.at[0], sides.at[1]
    second = {}
    for x in range(-3, 7):
        c, cw = a.first(x), a.w(x)
        second[x] = (1.0 + KEEP) * c + cw * (
            a.first(x - 1) + a.first(x + 1) + beside_z(c) + beside_y(c, 0.0, 0.0)
        )
        c2z[(x + 3) * CY : (x + 4) * CY, :] = second[x]
        for out, y in ((lo, 0), (hi, CY - 1)):
            for base, v in ((Z_C, c), (Z_P, second[x]), (Z_W, cw)):
                k = base + x + 3
                out[k : k + 1, :] = v[y : y + 1]
    for x in range(-2, 6):
        s, c, cw = second[x], a.first(x), a.w(x)
        below, above = shift_y(s, 0.0, 0.0)
        inner = {0: above, 1: below}
        for side, (out, y, y2) in enumerate(((lo, 0, 1), (hi, CY - 1, CY - 2))):
            k = Z_Q + x + 2
            out[k : k + 1, :] = (c + cw * inner[side])[y : y + 1]
        if -1 <= x <= 4:
            part = KEEP * s + c + cw * (second[x - 1] + second[x + 1] + beside_z(s))
            for side, (out, y, y2) in enumerate(((lo, 0, 1), (hi, CY - 1, CY - 2))):
                k = Z_R + x + 1
                out[k : k + 1, :] = (part + cw * inner[side])[y2 : y2 + 1]
                k = Z_V + x + 1
                out[k : k + 1, :] = cw[y2 : y2 + 1]
    for out, y, inner in ((lo, 0, 1), (hi, BY - 1, BY - 2)):
        for x in range(BX):
            at = (x + 1) * BY
            v = fine.w(x, y) * (fine.rhs(x, y) + row(f2, at + inner))
            for half in range(2):
                k = Z_S + 2 * x + half
                out[k : k + 1, :] = v[:, half * CZ : (half + 1) * CZ]
        for j, x in enumerate((-1, 8)):
            at = (x + 1) * BY + y
            v = f2[at : at + 1, :]
            for half in range(2):
                k = Z_K + 2 * j + half
                out[k : k + 1, :] = v[:, half * CZ : (half + 1) * CZ]
    p = side_of_dev()
    even[...] = sides[1 - p]
    even2[...] = sides[1 - p]
    odd[...] = sides[p]


def last_kernel(
    g, b, w, left, chip, both, f2, f2low, f2high, c1x, wc, cleft, cchip, c2z, even1, odd, even2,
    out, cboth, col, line, line3, fine, corr, col2, s1, gline, g1line,
):
    wide = Wide(g, b, w, left, chip)
    a = Coarse(c1x, wc, cleft, partner(cchip))
    take(cboth, even1[...] + even2[...], odd[...])
    low, high, clow, chigh = both.at[0], both.at[1], cboth.at[0], cboth.at[1]
    crow = lax.broadcasted_iota(jnp.int32, (CY, CZ), 0)
    c2 = {}
    for x in range(-3, 7):
        k = Z_C + x + 3
        beyond = jnp.where(crow == 0, row(clow, k), jnp.where(crow == CY - 1, row(chigh, k), 0.0))
        c2[x] = slab(c2z, x + 3, CY) + a.w(x) * beyond
    sides = ((clow, 0), (chigh, CY - 1))
    for s, (side, y) in enumerate(sides):
        for x in range(-3, 7):
            col[x + 3 : x + 4, :] = a.first(x)[y : y + 1]
        line[s, 0:10, :] = side[Z_P : Z_P + 10, :] + side[Z_W : Z_W + 10, :] * col[0:10, :]
        for x in range(-2, 6):
            col[x + 2 : x + 3, :] = c2[x][y : y + 1]
        mid = line[s, 1:9, :]
        line3[s, 0:8, :] = (
            KEEP * mid
            + side[Z_Q : Z_Q + 8, :]
            + side[Z_W + 1 : Z_W + 9, :]
            * (line[s, 0:8, :] + line[s, 2:10, :] + beside_z(mid) + col[0:8, :])
        )
    c3 = {}
    for x in range(-2, 6):
        c = c2[x]
        c3[x] = KEEP * c + a.first(x) + a.w(x) * (
            c2[x - 1]
            + c2[x + 1]
            + beside_z(c)
            + beside_y(c, line[0, x + 3 : x + 4, :], line[1, x + 3 : x + 4, :])
        )
    for x in range(-1, 5):
        c = c3[x]
        c4 = KEEP * c + a.first(x) + a.w(x) * (
            c3[x - 1]
            + c3[x + 1]
            + beside_z(c)
            + beside_y(c, line3[0, x + 2 : x + 3, :], line3[1, x + 2 : x + 3, :])
        )
        fine[pl.ds((x + 1) * BY, CY, stride=2), :] = c4
        fine[pl.ds((x + 1) * BY + 1, CY, stride=2), :] = c4
    for s, (side, y) in enumerate(sides):
        for x in range(-1, 5):
            col[x + 1 : x + 2, :] = c3[x][y : y + 1]
        mid = line3[s, 1:7, :]
        third = side[Z_R : Z_R + 6, :] + side[Z_V : Z_V + 6, :] * line[s, 2:8, :]
        fine[6 * BY + 8 * s : 6 * BY + 8 * s + 6, :] = (
            KEEP * mid
            + side[Z_C + 2 : Z_C + 8, :]
            + side[Z_W + 2 : Z_W + 8, :]
            * (line3[s, 0:6, :] + line3[s, 2:8, :] + beside_z(mid) + third + col[0:6, :])
        )
        fine[6 * BY + 8 * s + 6 : 6 * BY + 8 * s + 8, :] = jnp.zeros((2, CZ), F32)
    spread_z(fine[...], corr)
    g0 = {}
    for x in range(-2, 10):
        if x == -2:
            f = slab(cleft, 2)
        elif x == 9:
            f = slab(a.right, 2)
        else:
            f = slab(f2, x + 1)
        g0[x] = f + slab(corr, (x + 2) // 2)
    for s, (cside, side, y, f2side) in enumerate(((clow, low, 0, f2low), (chigh, high, BY - 1, f2high))):
        base = 6 * BY + 8 * s
        for x in range(-1, 9):
            k = base + (x + 2) // 2
            col2[x + 1 : x + 2, :] = corr[k : k + 1, :]
        gline[s, 1:9, :] = f2side[...] + col2[1:9, :]
        for j, x in enumerate((-1, 8)):
            k = Z_K + 2 * j
            gline[s, x + 1 : x + 2, 0:CZ] = row(cside, k) + col2[x + 1 : x + 2, 0:CZ]
            gline[s, x + 1 : x + 2, CZ:] = row(cside, k + 1) + col2[x + 1 : x + 2, CZ:]
        for x in range(BX):
            k = Z_S + 2 * x
            s1[x : x + 1, 0:CZ] = row(cside, k)
            s1[x : x + 1, CZ:] = row(cside, k + 1)
        moved = col2[1:9, :]
        for x in range(BX):
            col2[x : x + 1, :] = g0[x][y : y + 1]
        mid = gline[s, 1:9, :]
        g1line[s, 0:8, :] = (
            KEEP * mid
            + s1[0:8, :]
            + side[Y_W : Y_W + 8, :]
            * (moved + gline[s, 0:8, :] + gline[s, 2:10, :] + beside_z(mid) + col2[0:8, :])
        )
    g1 = {}
    for x in range(-1, 9):
        f = g0[x]
        g1[x] = KEEP * f + wide.w(x) * (
            wide.rhs(x)
            + g0[x - 1]
            + g0[x + 1]
            + beside_z(f)
            + beside_y(f, gline[0, x + 1 : x + 2, :], gline[1, x + 1 : x + 2, :])
        )
    for x in range(BX):
        f = g1[x]
        out[place(x)] = KEEP * f + wide.w(x) * (
            wide.rhs(x)
            + g1[x - 1]
            + g1[x + 1]
            + beside_z(f)
            + beside_y(f, g1line[0, x : x + 1, :], g1line[1, x : x + 1, :])
        )


def swap(v, links):
    n = lax.axis_size("dev")
    return lax.ppermute(v, ("group", "dev"), [(i * n + j, k * n + l) for (i, j), (k, l) in links])


def both_ways(pairs):
    return pairs + one_way_back(pairs)


def one_way_back(pairs):
    return [(j, i) for i, j in pairs]


def share_chip(v):
    groups = [[i, i + 1] for i in range(0, lax.axis_size("group"), 2)]
    return lax.all_gather(v, "group", axis_index_groups=groups)


def cross_pairs(keep):
    devs = [d for d in range(lax.axis_size("dev")) if keep(d)]
    return [((i, d), (i + 1, d)) for i in range(1, lax.axis_size("group") - 1, 2) for d in devs]


def dev_pairs(start, keep):
    devs = [d for d in range(start, lax.axis_size("dev") - 1, 2) if keep(d)]
    return [((i, d), (i, d + 1)) for i in range(lax.axis_size("group")) for d in devs]


def is_start(d):
    return d % RUN == 0


def is_end(d):
    return d % RUN == RUN - 1


def near_end(d):
    return is_end(d) or before_end(d)


def before_end(d):
    return d % RUN == RUN - 2


def body(g, b, n):
    block = (BX, BY, NZ)
    cross, chip, even, odd, f1z, g, b, w, d = call(
        load_kernel,
        [(X_ROWS, NZ)] * 2 + [(Y_ROWS, NZ)] * 2 + [(BX * BY, NZ)] + [block] * 4,
        g, b, n,
        hbm=3,
        vmem=None,
        scratch=[pltpu.VMEM(block, jnp.int32), (2, Y_ROWS, NZ), pltpu.SemaphoreType.DMA((3,))],
    )
    cross1 = swap(cross, both_ways(cross_pairs(lambda d: not near_end(d))))
    even1 = swap(even, both_ways(dev_pairs(0, lambda d: not before_end(d))))
    odd1 = swap(odd, both_ways(dev_pairs(1, lambda d: not before_end(d + 1))))
    cross2, even2, odd2, chip = call(
        again_kernel, [(X_ROWS, NZ), (Y_ROWS, NZ), (Y_ROWS, NZ), (X_ROWS, NZ)], cross, even, odd, chip, even1
    )
    even2 = swap(even2, both_ways(dev_pairs(0, before_end)))
    odd2 = swap(odd2, both_ways(dev_pairs(1, lambda d: before_end(d + 1))))
    cross2 = swap(cross2, both_ways(cross_pairs(near_end)))
    chip = share_chip(chip)
    left, both = call(
        gather_kernel,
        [(X_ROWS, NZ), (2, Y_ROWS, NZ)],
        cross1, even1, odd1,
        cost=pl.CostEstimate(flops=2**34, bytes_accessed=0, transcendentals=0),
    )
    f2, f2low, f2high, c1, wc, left, both, cross, near = call(
        middle_kernel,
        [(10 * BY, NZ), (BX, NZ), (BX, NZ), (CX * CY, CZ), (CX * CY, CZ), (X_ROWS, NZ), (2, Y_ROWS, NZ)] + [(X2_ROWS, NZ)] * 2,
        g, b, w, d, left, cross2, chip, f1z, both, even2, odd2,
        scratch=[(16, NZ), (2, 16, NZ), (4, CX * BY, CZ)],
    )
    cleft = swap(cross, both_ways(cross_pairs(lambda d: True)))
    cchip = share_chip(near)
    even, even2, odd, f2, f2low, f2high, c1x, c2z = call(
        pack_c_kernel,
        [(Z_ROWS, CZ)] * 3 + [(10 * BY, NZ), (BX, NZ), (BX, NZ), (3 * CX * CY, CZ), (10 * CY, CZ)],
        g, b, w, left, chip, both, f2, f2low, f2high, c1, wc, cleft, cchip,
        scratch=[(13, 8, NZ), (5, 8, NZ), (8, CZ), (2, Z_ROWS, CZ)],
    )
    first = dev_pairs(0, is_start)
    even1 = swap(even, both_ways(dev_pairs(0, lambda d: not (is_start(d) or before_end(d)))) + one_way_back(first))
    odd = swap(odd, both_ways(dev_pairs(1, lambda d: True)))
    even2 = swap(even2, both_ways(dev_pairs(0, before_end)) + first)
    (out,) = call(
        last_kernel,
        [block],
        g, b, w, left, chip, both, f2, f2low, f2high, c1x, wc, cleft, cchip, c2z, even1, odd, even2,
        scratch=[
            (2, Z_ROWS, CZ),
            (16, CZ), (2, 16, CZ), (2, 8, CZ), (6 * BY + 16, CZ), (6 * BY + 16, NZ), (16, NZ), (8, NZ), (2, 16, NZ), (2, 8, NZ),
        ],
        hbm_out=True,
    )
    return out


def solution(mesh):
    s = P("group", "dev", None)
    return jax.shard_map(body, mesh=mesh, in_specs=(s, s, s), out_specs=s, check_vma=False)
```

```python
import jax
import jax.numpy as jnp
from jax import lax
from jax.sharding import PartitionSpec as P
from jax.experimental import pallas as pl
from jax.experimental.pallas import tpu as pltpu

OMEGA = 0.8
KEEP = 1.0 - OMEGA
VM = pl.BlockSpec(memory_space=pltpu.VMEM)
F32 = jnp.float32
BX, BY, NZ = 8, 16, 256
CX, CY, CZ = 4, 8, 128
RUN = 32


def call(kernel, outs, *args, scratch=(), hbm=0, hbm_out=False, vmem=8 * 2**20, cost=None):
    make = jax.ShapeDtypeStruct if hbm_out else pltpu.VMEM
    return pl.pallas_call(
        kernel,
        out_shape=[make(s, F32) for s in outs],
        in_specs=[pl.BlockSpec(memory_space=pltpu.HBM)] * hbm + [VM] * (len(args) - hbm),
        out_specs=[VM] * len(outs),
        scratch_shapes=[pltpu.VMEM(s, F32) if isinstance(s, tuple) else s for s in scratch],
        compiler_params=pltpu.CompilerParams(vmem_limit_bytes=vmem),
        cost_estimate=cost,
    )(*args)


def beside_z(v):
    lane = lax.broadcasted_iota(jnp.int32, v.shape, 1)
    last = v.shape[1] - 1
    below = jnp.where(lane == 0, 0.0, pltpu.roll(v, 1, 1))
    above = jnp.where(lane == last, 0.0, pltpu.roll(v, last, 1))
    return below + above


def shift_y(v, low, high):
    row = lax.broadcasted_iota(jnp.int32, v.shape, 0)
    last = v.shape[0] - 1
    below = jnp.where(row == 0, low, pltpu.roll(v, 1, 0))
    above = jnp.where(row == last, high, pltpu.roll(v, last, 0))
    return below, above


def beside_y(v, low, high):
    below, above = shift_y(v, low, high)
    return below + above


def slab(ref, k, rows=BY):
    return ref[k * rows : (k + 1) * rows, :]


def by_row(n, rows):
    total = 0.0
    for k, v in rows.items():
        at = lax.broadcasted_iota(jnp.int32, (n, v.shape[1]), 0)
        total = jnp.where(at == k, v, total)
    return total


def row(ref, k):
    return ref[k : k + 1, :]


def lanes(v, index):
    return jnp.take_along_axis(v, index, axis=1)


def pair_z(low, high):
    lane = lax.broadcasted_iota(jnp.int32, low.shape, 1)
    low = low + pltpu.roll(low, CZ - 1, 1)
    high = high + pltpu.roll(high, CZ - 1, 1)
    index = (2 * lane) % CZ
    return jnp.where(lane < CZ // 2, lanes(low, index), lanes(high, index))


def spread_z(v, out):
    half = lax.broadcasted_iota(jnp.int32, v.shape, 1) // 2
    out[:, :CZ] = lanes(v, half)
    out[:, CZ:] = lanes(v, half + CZ // 2)


def diag_of(n):
    return 6.0 + 0.25 * n.astype(F32)


def place(x):
    odd = lax.axis_index("group") % 2
    return x + odd * (BX - 1 - 2 * x)


def partner(ref):
    return ref.at[1 - lax.axis_index("group") % 2]


def at_end_of_run():
    return lax.axis_index("dev") % RUN == RUN - 1


def side_of_dev():
    return lax.axis_index("dev") % 2


Y_G, Y_P, Y_W, Y_Q, Y_G2, Y_W2 = 0, 8, 16, 24, 32, 34
Y_ROWS = 40
X_ROWS = 7 * BY


def load_kernel(
    g_hbm, b_hbm, n_hbm, cross, fourth, last, even, odd, f1z, g, b, w, d, n, both, chip, sems
):
    copies = [
        pltpu.make_async_copy(src, dst, sems.at[k])
        for k, (src, dst) in enumerate(((g_hbm, g), (b_hbm, b), (n_hbm, n)))
    ]
    for c in copies:
        c.start()
    for c in copies:
        c.wait()
    for x in range(BX):
        diag = diag_of(n[x])
        d[x] = diag
        w[x] = OMEGA / diag
    for out, layers in ((cross, (0, 1, 2)), (chip, (7, 6, 5))):
        for k in range(3):
            out[k * BY : (k + 1) * BY, :] = g[place(layers[k])]
        for k in range(2):
            out[(3 + k) * BY : (4 + k) * BY, :] = w[place(layers[k])]
            out[(5 + k) * BY : (6 + k) * BY, :] = b[place(layers[k])]
    zero = jnp.zeros((BY, NZ), F32)
    for x in range(BX):
        at = place(x)
        here, wx, bx = g[at], w[at], b[at]
        before = g[place(x - 1)] if x else zero
        after = g[place(x + 1)] if x < BX - 1 else zero
        f = KEEP * here + wx * (bx + before + after + beside_z(here) + beside_y(here, 0.0, 0.0))
        f1z[x * BY : (x + 1) * BY, :] = f
        for s, (y, inner) in enumerate(((0, 1), (BY - 1, BY - 2))):
            rows = [
                (Y_G + x, here[y : y + 1]),
                (Y_P + x, f[y : y + 1]),
                (Y_W + x, wx[y : y + 1]),
                (Y_Q + x, wx[y : y + 1] * (bx[y : y + 1] + f[inner : inner + 1])),
            ]
            if x in (0, 7):
                rows += [(Y_G2 + x // 7, here[inner : inner + 1]), (Y_W2 + x // 7, wx[inner : inner + 1])]
            for k, v in rows:
                both[s, k : k + 1, :] = v
    p = side_of_dev()
    even[...] = both[1 - p]
    odd[...] = both[p]
    end = at_end_of_run()
    fourth[...] = jnp.where(end, cross[...], chip[...])
    last[...] = chip[...]

    @pl.when(jnp.logical_not(end))
    def _():
        last[0:Y_ROWS, :] = both[p]


class Wide:
    def __init__(self, g, b, w, left, right):
        self.own, self.left, self.right = (g, w, b), left, right

    def _get(self, which, base, x, y):
        if 0 <= x < BX:
            v = self.own[which]
            return v[place(x)] if y is None else v[place(x), y : y + 1, :]
        ref, k = (self.left, -1 - x) if x < 0 else (self.right, x - BX)
        return slab(ref, base + k) if y is None else row(ref, (base + k) * BY + y)

    def guess(self, x, y=None):
        return self._get(0, 0, x, y)

    def w(self, x, y=None):
        return self._get(1, 3, x, y)

    def rhs(self, x, y=None):
        return self._get(2, 5, x, y)


def take(both, even, odd):
    p = side_of_dev()
    both[1 - p] = even
    both[p] = odd


def again_kernel(even, last, met, even2, last2):
    even2[...] = even[...]
    last2[...] = last[...]


def gather_kernel(cross, even, odd, left, both):
    left[...] = cross[...]
    take(both, even[...], odd[...])


X2_D = 3 * BY
X2_ROWS = X2_D + 16


def diagonal_rows(edge):
    at, inner = (0, 1) if edge == 0 else (7, 6)
    return (Y_G + at, Y_G2 + edge, Y_G + inner, Y_P + at, Y_W + at, Y_W2 + edge, Y_W + inner)


def middle_kernel(
    g, b, w, d, left1, fourth, f1z, both1, even2, last,
    f2, f2low, f2high, c1, wc, left, right, both, lo, hi, col, line, sums,
):
    end = at_end_of_run()
    left[...] = left1[...] + jnp.where(end, fourth[...], 0.0)
    right[...] = jnp.where(end, last[...], fourth[...])
    a = Wide(g, b, w, left, right)
    p = side_of_dev()
    both[p] = both1[p] + jnp.where(end, 0.0, last[0:Y_ROWS, :])
    both[1 - p] = both1[1 - p] + even2[...]
    low, high = both.at[0], both.at[1]
    rows = lax.broadcasted_iota(jnp.int32, (BY, NZ), 0)
    f1 = {}
    for x in range(-2, 10):
        if 0 <= x < BX:
            k = Y_G + x
            beyond = jnp.where(rows == 0, row(low, k), jnp.where(rows == BY - 1, row(high, k), 0.0))
            if x == 0:
                beyond = beyond + a.guess(-1)
            if x == BX - 1:
                beyond = beyond + a.guess(BX)
            f1[x] = slab(f1z, x) + a.w(x) * beyond
        else:
            here = a.guess(x)
            f1[x] = KEEP * here + a.w(x) * (
                a.rhs(x) + a.guess(x - 1) + a.guess(x + 1) + beside_z(here) + beside_y(here, 0.0, 0.0)
            )
    for s, (side, y, out) in enumerate(((low, 0, f2low), (high, BY - 1, f2high))):
        for x in range(BX):
            col[x : x + 1, :] = a.guess(x, y)
        line[s, 0:16, :] = jnp.zeros((16, NZ), F32)
        line[s, 1:9, :] = side[Y_P : Y_P + 8, :] + side[Y_W : Y_W + 8, :] * col[0:8, :]
        for x in range(BX):
            col[x : x + 1, :] = f1[x][y : y + 1]
        mid = line[s, 1:9, :]
        out[...] = (
            KEEP * mid
            + side[Y_Q : Y_Q + 8, :]
            + side[Y_W : Y_W + 8, :] * (line[s, 0:8, :] + line[s, 2:10, :] + beside_z(mid) + col[0:8, :])
        )
        for edge, pack in enumerate((lo, hi)):
            for k, r in enumerate(diagonal_rows(edge)):
                at = X2_D + 7 * s + k
                pack[at : at + 1, :] = row(side, r)
    for pack in (lo, hi):
        pack[X2_D + 14 :, :] = jnp.zeros((2, NZ), F32)
    sec = {}
    for x in range(-1, 9):
        f = f1[x]
        sec[x] = KEEP * f + a.w(x) * (
            a.rhs(x)
            + f1[x - 1]
            + f1[x + 1]
            + beside_z(f)
            + beside_y(f, line[0, x + 1 : x + 2, :], line[1, x + 1 : x + 2, :])
        )
        f2[(x + 1) * BY : (x + 2) * BY, :] = sec[x]
    lo[2 * BY : X2_D, :] = sec[1]
    hi[2 * BY : X2_D, :] = sec[6]
    for x in range(0, 8):
        f = sec[x]
        r = (
            a.rhs(x)
            - d[place(x)] * f
            + sec[x - 1]
            + sec[x + 1]
            + beside_z(f)
            + beside_y(f, row(f2low, x), row(f2high, x))
        )
        if x % 2:
            pairs = pairs + r
            points = points + d[place(x)]
            at = (x // 2) * BY
            for half in range(2):
                sums[half, at : at + BY, :] = pairs[:, half * CZ : (half + 1) * CZ]
                sums[2 + half, at : at + BY, :] = points[:, half * CZ : (half + 1) * CZ]
        else:
            pairs, points = r, d[place(x)]
    doubled = [
        sums[k, pl.ds(0, CX * CY, stride=2), :] + sums[k, pl.ds(1, CX * CY, stride=2), :] for k in range(4)
    ]
    total = pair_z(doubled[0], doubled[1])
    diags = pair_z(doubled[2], doubled[3])
    weight = OMEGA / (0.5 * diags - 18.0)
    first = weight * (0.5 * total)
    c1[...] = first
    wc[...] = weight
    for x in range(CX):
        for out, k in ((lo, x), (hi, CX - 1 - x)):
            out[k * CY : (k + 1) * CY, 0:CZ] = first[x * CY : (x + 1) * CY]
            out[k * CY : (k + 1) * CY, CZ:] = weight[x * CY : (x + 1) * CY]


class Coarse:
    def __init__(self, c1x, wc, left, right):
        self.c1x, self.wc, self.left, self.right = c1x, wc, left, right

    def first(self, x):
        return slab(self.c1x, x + CX, CY)

    def w(self, x):
        if 0 <= x < CX:
            return slab(self.wc, x, CY)
        ref, k = (self.left, -1 - x) if x < 0 else (self.right, x - CX)
        return ref[k * CY : (k + 1) * CY, CZ:]


def corner_terms(a, low, high, relays, put):
    for e, (xe, xi, xn, xm) in enumerate(((0, 1, -1, -2), (7, 6, 8, 9))):
        for s, (side, y, yi) in enumerate(((low, 0, 1), (high, BY - 1, BY - 2))):
            own = [row(side, r) for r in diagonal_rows(e)]
            far = [row(relays[e], X2_D + 7 * s + k) for k in range(7)]
            corner, beside = a.guess(xe, y), a.guess(xn, y)
            w_corner, w_beside = a.w(xe, y), a.w(xn, y)
            put(2 * e + s, far[:5] + [beside + own[0], w_beside, a.w(xm, y), a.w(xn, yi), own[4], own[5], own[6], w_corner])
            put(4 + 2 * e + s, own[:5] + [corner + far[0], w_corner, a.w(xi, y), a.w(xe, yi), far[4], far[5], far[6], w_beside])


def corner_sums(t):
    g1, g2, g3, part, wd, near, wx, wx2, wxs, wy, wy2, wys, wq = (t[k] for k in range(13))
    dq = jnp.where(wq > 0.0, OMEGA / jnp.where(wq > 0.0, wq, 1.0), 0.0)
    by_y = wy * g1
    by_x = wx * g1
    diagonal = part + wd * near
    at_q = wq * (by_x + by_y)
    at_y = KEEP * by_y + wy * (beside_z(by_y) + diagonal + wy2 * g2)
    at_x = KEEP * by_x + wx * (beside_z(by_x) + diagonal + wx2 * g3)
    at_ys = wys * by_y
    at_xs = wxs * by_x
    total = at_y + at_x + beside_z(at_q) - dq * at_q + 2.0 * at_q + at_ys + at_xs
    return at_q, at_y, at_x, at_ys, at_xs, 0.5 * pair_z(total[:, :CZ], total[:, CZ:])


Z_C, Z_P, Z_W, Z_Q, Z_R, Z_V, Z_S, Z_K = 0, 10, 20, 30, 38, 44, 50, 66
Z_ROWS = 72


def pack_c_kernel(
    g, b, w, left, right, both, f2in, f2lowin, f2highin, c1, wc, cleft, cchip,
    even, even2, odd, f2, f2low, f2high, c1x, c2z, table, terms, rows, sides,
):
    fine = Wide(g, b, w, left, right)
    cright = partner(cchip)

    def put(i, values):
        for k, v in enumerate(values):
            table[k, i : i + 1, :] = v

    corner_terms(fine, both.at[0], both.at[1], (cleft, cright), put)
    *parts, share = corner_sums(table)
    for k, v in enumerate(parts):
        terms[k] = v
    rows[...] = share
    a = Coarse(c1x, wc, cleft, cright)
    for x in range(1, CX):
        c1x[(CX - 1 - x) * CY : (CX - x) * CY, :] = cleft[x * CY : (x + 1) * CY, 0:CZ]
        c1x[(x + 2 * CX) * CY : (x + 2 * CX + 1) * CY, :] = cright[x * CY : (x + 1) * CY, 0:CZ]
    for x in range(1, CX - 1):
        c1x[(x + CX) * CY : (x + CX + 1) * CY, :] = slab(c1, x, CY)
    term = lambda k, e, s: terms[k, 2 * e + s : 2 * e + s + 1, :]
    for e, (xe, xn, cxe, cxn) in enumerate(((0, -1, 0, -1), (7, 8, 3, 4))):
        at = (xe + 1) * BY
        f2[at : at + BY, :] = f2in[at : at + BY, :] + by_row(BY, {0: term(0, e, 0), BY - 1: term(0, e, 1)})
        at = (xn + 1) * BY
        f2[at : at + BY, :] = f2in[at : at + BY, :] + by_row(
            BY, {0: term(2, e, 0), 1: term(4, e, 0), BY - 2: term(4, e, 1), BY - 1: term(2, e, 1)}
        )
        for i, cx in ((2 * e, cxe), (2 * e + 4, cxn)):
            at = (cx + CX) * CY
            given = slab(c1, cx, CY) if 0 <= cx < CX else (cleft if cx < 0 else cright)[0:CY, 0:CZ]
            c1x[at : at + CY, :] = given + a.w(cx) * by_row(CY, {0: row(rows, i), CY - 1: row(rows, i + 1)})
    f2[2 * BY : 8 * BY, :] = f2in[2 * BY : 8 * BY, :]
    for s, (side, sidein) in enumerate(((f2low, f2lowin), (f2high, f2highin))):
        side[...] = sidein[...] + by_row(
            BX, {0: term(1, 0, s), 1: term(3, 0, s), BX - 2: term(3, 1, s), BX - 1: term(1, 1, s)}
        )
    lo, hi = sides.at[0], sides.at[1]
    second = {}
    for x in range(-3, 7):
        c, cw = a.first(x), a.w(x)
        second[x] = (1.0 + KEEP) * c + cw * (
            a.first(x - 1) + a.first(x + 1) + beside_z(c) + beside_y(c, 0.0, 0.0)
        )
        c2z[(x + 3) * CY : (x + 4) * CY, :] = second[x]
        for out, y in ((lo, 0), (hi, CY - 1)):
            for base, v in ((Z_C, c), (Z_P, second[x]), (Z_W, cw)):
                k = base + x + 3
                out[k : k + 1, :] = v[y : y + 1]
    for x in range(-2, 6):
        s, c, cw = second[x], a.first(x), a.w(x)
        below, above = shift_y(s, 0.0, 0.0)
        inner = {0: above, 1: below}
        for side, (out, y, y2) in enumerate(((lo, 0, 1), (hi, CY - 1, CY - 2))):
            k = Z_Q + x + 2
            out[k : k + 1, :] = (c + cw * inner[side])[y : y + 1]
        if -1 <= x <= 4:
            part = KEEP * s + c + cw * (second[x - 1] + second[x + 1] + beside_z(s))
            for side, (out, y, y2) in enumerate(((lo, 0, 1), (hi, CY - 1, CY - 2))):
                k = Z_R + x + 1
                out[k : k + 1, :] = (part + cw * inner[side])[y2 : y2 + 1]
                k = Z_V + x + 1
                out[k : k + 1, :] = cw[y2 : y2 + 1]
    for out, y, inner in ((lo, 0, 1), (hi, BY - 1, BY - 2)):
        for x in range(BX):
            at = (x + 1) * BY
            v = fine.w(x, y) * (fine.rhs(x, y) + row(f2, at + inner))
            for half in range(2):
                k = Z_S + 2 * x + half
                out[k : k + 1, :] = v[:, half * CZ : (half + 1) * CZ]
        for j, x in enumerate((-1, 8)):
            at = (x + 1) * BY + y
            v = f2[at : at + 1, :]
            for half in range(2):
                k = Z_K + 2 * j + half
                out[k : k + 1, :] = v[:, half * CZ : (half + 1) * CZ]
    p = side_of_dev()
    even[...] = sides[1 - p]
    even2[...] = sides[1 - p]
    odd[...] = sides[p]


def last_kernel(
    g, b, w, left, right, both, f2, f2low, f2high, c1x, wc, cleft, cchip, c2z, even1, odd, even2,
    out, cboth, col, line, line3, fine, corr, col2, s1, gline, g1line,
):
    wide = Wide(g, b, w, left, right)
    a = Coarse(c1x, wc, cleft, partner(cchip))
    take(cboth, even1[...] + even2[...], odd[...])
    low, high, clow, chigh = both.at[0], both.at[1], cboth.at[0], cboth.at[1]
    crow = lax.broadcasted_iota(jnp.int32, (CY, CZ), 0)
    c2 = {}
    for x in range(-3, 7):
        k = Z_C + x + 3
        beyond = jnp.where(crow == 0, row(clow, k), jnp.where(crow == CY - 1, row(chigh, k), 0.0))
        c2[x] = slab(c2z, x + 3, CY) + a.w(x) * beyond
    sides = ((clow, 0), (chigh, CY - 1))
    for s, (side, y) in enumerate(sides):
        for x in range(-3, 7):
            col[x + 3 : x + 4, :] = a.first(x)[y : y + 1]
        line[s, 0:10, :] = side[Z_P : Z_P + 10, :] + side[Z_W : Z_W + 10, :] * col[0:10, :]
        for x in range(-2, 6):
            col[x + 2 : x + 3, :] = c2[x][y : y + 1]
        mid = line[s, 1:9, :]
        line3[s, 0:8, :] = (
            KEEP * mid
            + side[Z_Q : Z_Q + 8, :]
            + side[Z_W + 1 : Z_W + 9, :]
            * (line[s, 0:8, :] + line[s, 2:10, :] + beside_z(mid) + col[0:8, :])
        )
    c3 = {}
    for x in range(-2, 6):
        c = c2[x]
        c3[x] = KEEP * c + a.first(x) + a.w(x) * (
            c2[x - 1]
            + c2[x + 1]
            + beside_z(c)
            + beside_y(c, line[0, x + 3 : x + 4, :], line[1, x + 3 : x + 4, :])
        )
    for x in range(-1, 5):
        c = c3[x]
        c4 = KEEP * c + a.first(x) + a.w(x) * (
            c3[x - 1]
            + c3[x + 1]
            + beside_z(c)
            + beside_y(c, line3[0, x + 2 : x + 3, :], line3[1, x + 2 : x + 3, :])
        )
        fine[pl.ds((x + 1) * BY, CY, stride=2), :] = c4
        fine[pl.ds((x + 1) * BY + 1, CY, stride=2), :] = c4
    for s, (side, y) in enumerate(sides):
        for x in range(-1, 5):
            col[x + 1 : x + 2, :] = c3[x][y : y + 1]
        mid = line3[s, 1:7, :]
        third = side[Z_R : Z_R + 6, :] + side[Z_V : Z_V + 6, :] * line[s, 2:8, :]
        fine[6 * BY + 8 * s : 6 * BY + 8 * s + 6, :] = (
            KEEP * mid
            + side[Z_C + 2 : Z_C + 8, :]
            + side[Z_W + 2 : Z_W + 8, :]
            * (line3[s, 0:6, :] + line3[s, 2:8, :] + beside_z(mid) + third + col[0:6, :])
        )
        fine[6 * BY + 8 * s + 6 : 6 * BY + 8 * s + 8, :] = jnp.zeros((2, CZ), F32)
    spread_z(fine[...], corr)
    g0 = {}
    for x in range(-2, 10):
        if x == -2:
            f = slab(cleft, 2)
        elif x == 9:
            f = slab(a.right, 2)
        else:
            f = slab(f2, x + 1)
        g0[x] = f + slab(corr, (x + 2) // 2)
    for s, (cside, side, y, f2side) in enumerate(((clow, low, 0, f2low), (chigh, high, BY - 1, f2high))):
        base = 6 * BY + 8 * s
        for x in range(-1, 9):
            k = base + (x + 2) // 2
            col2[x + 1 : x + 2, :] = corr[k : k + 1, :]
        gline[s, 1:9, :] = f2side[...] + col2[1:9, :]
        for j, x in enumerate((-1, 8)):
            k = Z_K + 2 * j
            gline[s, x + 1 : x + 2, 0:CZ] = row(cside, k) + col2[x + 1 : x + 2, 0:CZ]
            gline[s, x + 1 : x + 2, CZ:] = row(cside, k + 1) + col2[x + 1 : x + 2, CZ:]
        for x in range(BX):
            k = Z_S + 2 * x
            s1[x : x + 1, 0:CZ] = row(cside, k)
            s1[x : x + 1, CZ:] = row(cside, k + 1)
        moved = col2[1:9, :]
        for x in range(BX):
            col2[x : x + 1, :] = g0[x][y : y + 1]
        mid = gline[s, 1:9, :]
        g1line[s, 0:8, :] = (
            KEEP * mid
            + s1[0:8, :]
            + side[Y_W : Y_W + 8, :]
            * (moved + gline[s, 0:8, :] + gline[s, 2:10, :] + beside_z(mid) + col2[0:8, :])
        )
    g1 = {}
    for x in range(-1, 9):
        f = g0[x]
        g1[x] = KEEP * f + wide.w(x) * (
            wide.rhs(x)
            + g0[x - 1]
            + g0[x + 1]
            + beside_z(f)
            + beside_y(f, gline[0, x + 1 : x + 2, :], gline[1, x + 1 : x + 2, :])
        )
    for x in range(BX):
        f = g1[x]
        out[place(x)] = KEEP * f + wide.w(x) * (
            wide.rhs(x)
            + g1[x - 1]
            + g1[x + 1]
            + beside_z(f)
            + beside_y(f, g1line[0, x : x + 1, :], g1line[1, x : x + 1, :])
        )


def swap(v, pairs):
    n = lax.axis_size("dev")
    links = [(i * n + j, k * n + l) for (i, j), (k, l) in pairs]
    return lax.ppermute(v, ("group", "dev"), links + [(j, i) for i, j in links])


def share_chip(v):
    groups = [[i, i + 1] for i in range(0, lax.axis_size("group"), 2)]
    return lax.all_gather(v, "group", axis_index_groups=groups)


def cross_pairs(keep):
    devs = [d for d in range(lax.axis_size("dev")) if keep(d)]
    return [((i, d), (i + 1, d)) for i in range(1, lax.axis_size("group") - 1, 2) for d in devs]


def chip_pairs(keep):
    devs = [d for d in range(lax.axis_size("dev")) if keep(d)]
    return [((i, d), (i + 1, d)) for i in range(0, lax.axis_size("group"), 2) for d in devs]


def dev_pairs(start, keep):
    devs = [d for d in range(start, lax.axis_size("dev") - 1, 2) if keep(d)]
    return [((i, d), (i, d + 1)) for i in range(lax.axis_size("group")) for d in devs]


def is_end(d):
    return d % RUN == RUN - 1


def before_end(d):
    return d % RUN == RUN - 2


def body(g, b, n):
    block = (BX, BY, NZ)
    cross, fourth, last, even, odd, f1z, g, b, w, d = call(
        load_kernel,
        [(X_ROWS, NZ)] * 3 + [(Y_ROWS, NZ)] * 2 + [(BX * BY, NZ)] + [block] * 4,
        g, b, n,
        hbm=3,
        vmem=None,
        scratch=[pltpu.VMEM(block, jnp.int32), (2, Y_ROWS, NZ), (X_ROWS, NZ), pltpu.SemaphoreType.DMA((3,))],
    )
    cross1 = swap(cross, cross_pairs(lambda d: not is_end(d)))
    even1 = swap(even, dev_pairs(0, lambda d: not before_end(d)))
    odd1 = swap(odd, dev_pairs(1, lambda d: not before_end(d + 1)))
    fourth = swap(fourth, chip_pairs(lambda d: not is_end(d)) + cross_pairs(is_end))
    even2, last = call(again_kernel, [(Y_ROWS, NZ), (X_ROWS, NZ)], even, last, even1)
    even2 = swap(even2, dev_pairs(0, before_end))
    last = swap(last, dev_pairs(1, lambda d: before_end(d + 1)) + chip_pairs(is_end))
    left, both = call(
        gather_kernel,
        [(X_ROWS, NZ), (2, Y_ROWS, NZ)],
        cross1, even1, odd1,
        cost=pl.CostEstimate(flops=2**34, bytes_accessed=0, transcendentals=0),
    )
    f2, f2low, f2high, c1, wc, left, right, both, cross, near = call(
        middle_kernel,
        [(10 * BY, NZ), (BX, NZ), (BX, NZ), (CX * CY, CZ), (CX * CY, CZ), (X_ROWS, NZ), (X_ROWS, NZ), (2, Y_ROWS, NZ)] + [(X2_ROWS, NZ)] * 2,
        g, b, w, d, left, fourth, f1z, both, even2, last,
        scratch=[(16, NZ), (2, 16, NZ), (4, CX * BY, CZ)],
    )
    cleft = swap(cross, cross_pairs(lambda d: True))
    cchip = share_chip(near)
    even, even2, odd, f2, f2low, f2high, c1x, c2z = call(
        pack_c_kernel,
        [(Z_ROWS, CZ)] * 3 + [(10 * BY, NZ), (BX, NZ), (BX, NZ), (3 * CX * CY, CZ), (10 * CY, CZ)],
        g, b, w, left, right, both, f2, f2low, f2high, c1, wc, cleft, cchip,
        scratch=[(13, 8, NZ), (5, 8, NZ), (8, CZ), (2, Z_ROWS, CZ)],
    )
    even1 = swap(even, dev_pairs(0, lambda d: not before_end(d)))
    odd = swap(odd, dev_pairs(1, lambda d: True))
    even2 = swap(even2, dev_pairs(0, before_end))
    (out,) = call(
        last_kernel,
        [block],
        g, b, w, left, right, both, f2, f2low, f2high, c1x, wc, cleft, cchip, c2z, even1, odd, even2,
        scratch=[
            (2, Z_ROWS, CZ),
            (16, CZ), (2, 16, CZ), (2, 8, CZ), (6 * BY + 16, CZ), (6 * BY + 16, NZ), (16, NZ), (8, NZ), (2, 16, NZ), (2, 8, NZ),
        ],
        hbm_out=True,
    )
    return out


def solution(mesh):
    s = P("group", "dev", None)
    return jax.shard_map(body, mesh=mesh, in_specs=(s, s, s), out_specs=s, check_vma=False)
```

```python
import jax
import jax.numpy as jnp
from jax import lax
from jax.sharding import PartitionSpec as P
from jax.experimental import pallas as pl
from jax.experimental.pallas import tpu as pltpu

OMEGA = 0.8
KEEP = 1.0 - OMEGA
VM = pl.BlockSpec(memory_space=pltpu.VMEM)
F32 = jnp.float32
BX, BY, NZ = 8, 16, 256
CX, CY, CZ = 4, 8, 128
RUN = 32


def call(kernel, outs, *args, scratch=(), hbm=0, hbm_out=False, vmem=8 * 2**20, cost=None):
    make = jax.ShapeDtypeStruct if hbm_out else pltpu.VMEM
    return pl.pallas_call(
        kernel,
        out_shape=[make(s, F32) for s in outs],
        in_specs=[pl.BlockSpec(memory_space=pltpu.HBM)] * hbm + [VM] * (len(args) - hbm),
        out_specs=[VM] * len(outs),
        scratch_shapes=[pltpu.VMEM(s, F32) if isinstance(s, tuple) else s for s in scratch],
        compiler_params=pltpu.CompilerParams(vmem_limit_bytes=vmem),
        cost_estimate=cost,
    )(*args)


def beside_z(v):
    lane = lax.broadcasted_iota(jnp.int32, v.shape, 1)
    last = v.shape[1] - 1
    below = jnp.where(lane == 0, 0.0, pltpu.roll(v, 1, 1))
    above = jnp.where(lane == last, 0.0, pltpu.roll(v, last, 1))
    return below + above


def shift_y(v, low, high):
    row = lax.broadcasted_iota(jnp.int32, v.shape, 0)
    last = v.shape[0] - 1
    below = jnp.where(row == 0, low, pltpu.roll(v, 1, 0))
    above = jnp.where(row == last, high, pltpu.roll(v, last, 0))
    return below, above


def beside_y(v, low, high):
    below, above = shift_y(v, low, high)
    return below + above


def slab(ref, k, rows=BY):
    return ref[k * rows : (k + 1) * rows, :]


def by_row(n, rows):
    total = 0.0
    for k, v in rows.items():
        at = lax.broadcasted_iota(jnp.int32, (n, v.shape[1]), 0)
        total = jnp.where(at == k, v, total)
    return total


def row(ref, k):
    return ref[k : k + 1, :]


def lanes(v, index):
    return jnp.take_along_axis(v, index, axis=1)


def pair_z(low, high):
    lane = lax.broadcasted_iota(jnp.int32, low.shape, 1)
    low = low + pltpu.roll(low, CZ - 1, 1)
    high = high + pltpu.roll(high, CZ - 1, 1)
    index = (2 * lane) % CZ
    return jnp.where(lane < CZ // 2, lanes(low, index), lanes(high, index))


def spread_z(v, out):
    half = lax.broadcasted_iota(jnp.int32, v.shape, 1) // 2
    out[:, :CZ] = lanes(v, half)
    out[:, CZ:] = lanes(v, half + CZ // 2)


def diag_of(n):
    return 6.0 + 0.25 * n.astype(F32)


def place(x):
    odd = lax.axis_index("group") % 2
    return x + odd * (BX - 1 - 2 * x)


def partner(ref):
    return ref.at[1 - lax.axis_index("group") % 2]


def side_of_dev():
    return lax.axis_index("dev") % 2


Y_G, Y_P, Y_W, Y_Q, Y_G2, Y_W2 = 0, 8, 16, 24, 32, 34
Y_ROWS = 40
X_ROWS = 7 * BY


def load_kernel(
    g_hbm, b_hbm, n_hbm, cross, cross2, chip, even, odd, f1z, g, b, w, d, n, both, sems
):
    copies = [
        pltpu.make_async_copy(src, dst, sems.at[k])
        for k, (src, dst) in enumerate(((g_hbm, g), (b_hbm, b), (n_hbm, n)))
    ]
    for c in copies:
        c.start()
    for c in copies:
        c.wait()
    for x in range(BX):
        diag = diag_of(n[x])
        d[x] = diag
        w[x] = OMEGA / diag
    for out, layers in ((cross, (0, 1, 2)), (chip, (7, 6, 5))):
        for k in range(3):
            out[k * BY : (k + 1) * BY, :] = g[place(layers[k])]
        for k in range(2):
            out[(3 + k) * BY : (4 + k) * BY, :] = w[place(layers[k])]
            out[(5 + k) * BY : (6 + k) * BY, :] = b[place(layers[k])]
    zero = jnp.zeros((BY, NZ), F32)
    for x in range(BX):
        at = place(x)
        here, wx, bx = g[at], w[at], b[at]
        before = g[place(x - 1)] if x else zero
        after = g[place(x + 1)] if x < BX - 1 else zero
        f = KEEP * here + wx * (bx + before + after + beside_z(here) + beside_y(here, 0.0, 0.0))
        f1z[x * BY : (x + 1) * BY, :] = f
        for s, (y, inner) in enumerate(((0, 1), (BY - 1, BY - 2))):
            rows = [
                (Y_G + x, here[y : y + 1]),
                (Y_P + x, f[y : y + 1]),
                (Y_W + x, wx[y : y + 1]),
                (Y_Q + x, wx[y : y + 1] * (bx[y : y + 1] + f[inner : inner + 1])),
            ]
            if x in (0, 7):
                rows += [(Y_G2 + x // 7, here[inner : inner + 1]), (Y_W2 + x // 7, wx[inner : inner + 1])]
            for k, v in rows:
                both[s, k : k + 1, :] = v
    p = side_of_dev()
    even[...] = both[1 - p]
    odd[...] = both[p]
    cross2[...] = cross[...]


class Wide:
    def __init__(self, g, b, w, left, right):
        self.own, self.left, self.right = (g, w, b), left, partner(right)

    def _get(self, which, base, x, y):
        if 0 <= x < BX:
            v = self.own[which]
            return v[place(x)] if y is None else v[place(x), y : y + 1, :]
        ref, k = (self.left, -1 - x) if x < 0 else (self.right, x - BX)
        return slab(ref, base + k) if y is None else row(ref, (base + k) * BY + y)

    def guess(self, x, y=None):
        return self._get(0, 0, x, y)

    def w(self, x, y=None):
        return self._get(1, 3, x, y)

    def rhs(self, x, y=None):
        return self._get(2, 5, x, y)


def take(both, even, odd):
    p = side_of_dev()
    both[1 - p] = even
    both[p] = odd


def again_kernel(even, odd, chip, met, even2, odd2, chip2):
    chip2[...] = chip[...]
    even2[...] = even[...]
    odd2[...] = odd[...]


def gather_kernel(cross, even, odd, left, both):
    left[...] = cross[...]
    take(both, even[...], odd[...])


X2_D = 3 * BY
X2_ROWS = X2_D + 16


def diagonal_rows(edge):
    at, inner = (0, 1) if edge == 0 else (7, 6)
    return (Y_G + at, Y_G2 + edge, Y_G + inner, Y_P + at, Y_W + at, Y_W2 + edge, Y_W + inner)


def middle_kernel(
    g, b, w, d, left1, cross2, chip, f1z, both1, even2, odd2,
    f2, f2low, f2high, c1, wc, left, both, lo, hi, col, line, sums,
):
    left[...] = left1[...] + cross2[...]
    a = Wide(g, b, w, left, chip)
    p = side_of_dev()
    both[p] = both1[p] + odd2[...]
    both[1 - p] = both1[1 - p] + even2[...]
    low, high = both.at[0], both.at[1]
    rows = lax.broadcasted_iota(jnp.int32, (BY, NZ), 0)
    f1 = {}
    for x in range(-2, 10):
        if 0 <= x < BX:
            k = Y_G + x
            beyond = jnp.where(rows == 0, row(low, k), jnp.where(rows == BY - 1, row(high, k), 0.0))
            if x == 0:
                beyond = beyond + a.guess(-1)
            if x == BX - 1:
                beyond = beyond + a.guess(BX)
            f1[x] = slab(f1z, x) + a.w(x) * beyond
        else:
            here = a.guess(x)
            f1[x] = KEEP * here + a.w(x) * (
                a.rhs(x) + a.guess(x - 1) + a.guess(x + 1) + beside_z(here) + beside_y(here, 0.0, 0.0)
            )
    for s, (side, y, out) in enumerate(((low, 0, f2low), (high, BY - 1, f2high))):
        for x in range(BX):
            col[x : x + 1, :] = a.guess(x, y)
        line[s, 0:16, :] = jnp.zeros((16, NZ), F32)
        line[s, 1:9, :] = side[Y_P : Y_P + 8, :] + side[Y_W : Y_W + 8, :] * col[0:8, :]
        for x in range(BX):
            col[x : x + 1, :] = f1[x][y : y + 1]
        mid = line[s, 1:9, :]
        out[...] = (
            KEEP * mid
            + side[Y_Q : Y_Q + 8, :]
            + side[Y_W : Y_W + 8, :] * (line[s, 0:8, :] + line[s, 2:10, :] + beside_z(mid) + col[0:8, :])
        )
        for edge, pack in enumerate((lo, hi)):
            for k, r in enumerate(diagonal_rows(edge)):
                at = X2_D + 7 * s + k
                pack[at : at + 1, :] = row(side, r)
    for pack in (lo, hi):
        pack[X2_D + 14 :, :] = jnp.zeros((2, NZ), F32)
    sec = {}
    for x in range(-1, 9):
        f = f1[x]
        sec[x] = KEEP * f + a.w(x) * (
            a.rhs(x)
            + f1[x - 1]
            + f1[x + 1]
            + beside_z(f)
            + beside_y(f, line[0, x + 1 : x + 2, :], line[1, x + 1 : x + 2, :])
        )
        f2[(x + 1) * BY : (x + 2) * BY, :] = sec[x]
    lo[2 * BY : X2_D, :] = sec[1]
    hi[2 * BY : X2_D, :] = sec[6]
    for x in range(0, 8):
        f = sec[x]
        r = (
            a.rhs(x)
            - d[place(x)] * f
            + sec[x - 1]
            + sec[x + 1]
            + beside_z(f)
            + beside_y(f, row(f2low, x), row(f2high, x))
        )
        if x % 2:
            pairs = pairs + r
            points = points + d[place(x)]
            at = (x // 2) * BY
            for half in range(2):
                sums[half, at : at + BY, :] = pairs[:, half * CZ : (half + 1) * CZ]
                sums[2 + half, at : at + BY, :] = points[:, half * CZ : (half + 1) * CZ]
        else:
            pairs, points = r, d[place(x)]
    doubled = [
        sums[k, pl.ds(0, CX * CY, stride=2), :] + sums[k, pl.ds(1, CX * CY, stride=2), :] for k in range(4)
    ]
    total = pair_z(doubled[0], doubled[1])
    diags = pair_z(doubled[2], doubled[3])
    weight = OMEGA / (0.5 * diags - 18.0)
    first = weight * (0.5 * total)
    c1[...] = first
    wc[...] = weight
    for x in range(CX):
        for out, k in ((lo, x), (hi, CX - 1 - x)):
            out[k * CY : (k + 1) * CY, 0:CZ] = first[x * CY : (x + 1) * CY]
            out[k * CY : (k + 1) * CY, CZ:] = weight[x * CY : (x + 1) * CY]


class Coarse:
    def __init__(self, c1x, wc, left, right):
        self.c1x, self.wc, self.left, self.right = c1x, wc, left, right

    def first(self, x):
        return slab(self.c1x, x + CX, CY)

    def w(self, x):
        if 0 <= x < CX:
            return slab(self.wc, x, CY)
        ref, k = (self.left, -1 - x) if x < 0 else (self.right, x - CX)
        return ref[k * CY : (k + 1) * CY, CZ:]


def corner_terms(a, low, high, relays, put):
    for e, (xe, xi, xn, xm) in enumerate(((0, 1, -1, -2), (7, 6, 8, 9))):
        for s, (side, y, yi) in enumerate(((low, 0, 1), (high, BY - 1, BY - 2))):
            own = [row(side, r) for r in diagonal_rows(e)]
            far = [row(relays[e], X2_D + 7 * s + k) for k in range(7)]
            corner, beside = a.guess(xe, y), a.guess(xn, y)
            w_corner, w_beside = a.w(xe, y), a.w(xn, y)
            put(2 * e + s, far[:5] + [beside + own[0], w_beside, a.w(xm, y), a.w(xn, yi), own[4], own[5], own[6], w_corner])
            put(4 + 2 * e + s, own[:5] + [corner + far[0], w_corner, a.w(xi, y), a.w(xe, yi), far[4], far[5], far[6], w_beside])


def corner_sums(t):
    g1, g2, g3, part, wd, near, wx, wx2, wxs, wy, wy2, wys, wq = (t[k] for k in range(13))
    dq = jnp.where(wq > 0.0, OMEGA / jnp.where(wq > 0.0, wq, 1.0), 0.0)
    by_y = wy * g1
    by_x = wx * g1
    diagonal = part + wd * near
    at_q = wq * (by_x + by_y)
    at_y = KEEP * by_y + wy * (beside_z(by_y) + diagonal + wy2 * g2)
    at_x = KEEP * by_x + wx * (beside_z(by_x) + diagonal + wx2 * g3)
    at_ys = wys * by_y
    at_xs = wxs * by_x
    total = at_y + at_x + beside_z(at_q) - dq * at_q + 2.0 * at_q + at_ys + at_xs
    return at_q, at_y, at_x, at_ys, at_xs, 0.5 * pair_z(total[:, :CZ], total[:, CZ:])


Z_C, Z_P, Z_W, Z_Q, Z_R, Z_V, Z_S, Z_K = 0, 10, 20, 30, 38, 44, 50, 66
Z_ROWS = 72


def pack_c_kernel(
    g, b, w, left, chip, both, f2in, f2lowin, f2highin, c1, wc, cleft, cchip,
    even, even2, odd, f2, f2low, f2high, c1x, c2z, table, terms, rows, sides,
):
    fine = Wide(g, b, w, left, chip)
    cright = partner(cchip)

    def put(i, values):
        for k, v in enumerate(values):
            table[k, i : i + 1, :] = v

    corner_terms(fine, both.at[0], both.at[1], (cleft, cright), put)
    *parts, share = corner_sums(table)
    for k, v in enumerate(parts):
        terms[k] = v
    rows[...] = share
    a = Coarse(c1x, wc, cleft, cright)
    for x in range(1, CX):
        c1x[(CX - 1 - x) * CY : (CX - x) * CY, :] = cleft[x * CY : (x + 1) * CY, 0:CZ]
        c1x[(x + 2 * CX) * CY : (x + 2 * CX + 1) * CY, :] = cright[x * CY : (x + 1) * CY, 0:CZ]
    for x in range(1, CX - 1):
        c1x[(x + CX) * CY : (x + CX + 1) * CY, :] = slab(c1, x, CY)
    term = lambda k, e, s: terms[k, 2 * e + s : 2 * e + s + 1, :]
    for e, (xe, xn, cxe, cxn) in enumerate(((0, -1, 0, -1), (7, 8, 3, 4))):
        at = (xe + 1) * BY
        f2[at : at + BY, :] = f2in[at : at + BY, :] + by_row(BY, {0: term(0, e, 0), BY - 1: term(0, e, 1)})
        at = (xn + 1) * BY
        f2[at : at + BY, :] = f2in[at : at + BY, :] + by_row(
            BY, {0: term(2, e, 0), 1: term(4, e, 0), BY - 2: term(4, e, 1), BY - 1: term(2, e, 1)}
        )
        for i, cx in ((2 * e, cxe), (2 * e + 4, cxn)):
            at = (cx + CX) * CY
            given = slab(c1, cx, CY) if 0 <= cx < CX else (cleft if cx < 0 else cright)[0:CY, 0:CZ]
            c1x[at : at + CY, :] = given + a.w(cx) * by_row(CY, {0: row(rows, i), CY - 1: row(rows, i + 1)})
    f2[2 * BY : 8 * BY, :] = f2in[2 * BY : 8 * BY, :]
    for s, (side, sidein) in enumerate(((f2low, f2lowin), (f2high, f2highin))):
        side[...] = sidein[...] + by_row(
            BX, {0: term(1, 0, s), 1: term(3, 0, s), BX - 2: term(3, 1, s), BX - 1: term(1, 1, s)}
        )
    lo, hi = sides.at[0], sides.at[1]
    second = {}
    for x in range(-3, 7):
        c, cw = a.first(x), a.w(x)
        second[x] = (1.0 + KEEP) * c + cw * (
            a.first(x - 1) + a.first(x + 1) + beside_z(c) + beside_y(c, 0.0, 0.0)
        )
        c2z[(x + 3) * CY : (x + 4) * CY, :] = second[x]
        for out, y in ((lo, 0), (hi, CY - 1)):
            for base, v in ((Z_C, c), (Z_P, second[x]), (Z_W, cw)):
                k = base + x + 3
                out[k : k + 1, :] = v[y : y + 1]
    for x in range(-2, 6):
        s, c, cw = second[x], a.first(x), a.w(x)
        below, above = shift_y(s, 0.0, 0.0)
        inner = {0: above, 1: below}
        for side, (out, y, y2) in enumerate(((lo, 0, 1), (hi, CY - 1, CY - 2))):
            k = Z_Q + x + 2
            out[k : k + 1, :] = (c + cw * inner[side])[y : y + 1]
        if -1 <= x <= 4:
            part = KEEP * s + c + cw * (second[x - 1] + second[x + 1] + beside_z(s))
            for side, (out, y, y2) in enumerate(((lo, 0, 1), (hi, CY - 1, CY - 2))):
                k = Z_R + x + 1
                out[k : k + 1, :] = (part + cw * inner[side])[y2 : y2 + 1]
                k = Z_V + x + 1
                out[k : k + 1, :] = cw[y2 : y2 + 1]
    for out, y, inner in ((lo, 0, 1), (hi, BY - 1, BY - 2)):
        for x in range(BX):
            at = (x + 1) * BY
            v = fine.w(x, y) * (fine.rhs(x, y) + row(f2, at + inner))
            for half in range(2):
                k = Z_S + 2 * x + half
                out[k : k + 1, :] = v[:, half * CZ : (half + 1) * CZ]
        for j, x in enumerate((-1, 8)):
            at = (x + 1) * BY + y
            v = f2[at : at + 1, :]
            for half in range(2):
                k = Z_K + 2 * j + half
                out[k : k + 1, :] = v[:, half * CZ : (half + 1) * CZ]
    p = side_of_dev()
    even[...] = sides[1 - p]
    even2[...] = sides[1 - p]
    odd[...] = sides[p]


def last_kernel(
    g, b, w, left, chip, both, f2, f2low, f2high, c1x, wc, cleft, cchip, c2z, even1, odd, even2,
    out, cboth, col, line, line3, fine, corr, col2, s1, gline, g1line,
):
    wide = Wide(g, b, w, left, chip)
    a = Coarse(c1x, wc, cleft, partner(cchip))
    take(cboth, even1[...] + even2[...], odd[...])
    low, high, clow, chigh = both.at[0], both.at[1], cboth.at[0], cboth.at[1]
    crow = lax.broadcasted_iota(jnp.int32, (CY, CZ), 0)
    c2 = {}
    for x in range(-3, 7):
        k = Z_C + x + 3
        beyond = jnp.where(crow == 0, row(clow, k), jnp.where(crow == CY - 1, row(chigh, k), 0.0))
        c2[x] = slab(c2z, x + 3, CY) + a.w(x) * beyond
    sides = ((clow, 0), (chigh, CY - 1))
    for s, (side, y) in enumerate(sides):
        for x in range(-3, 7):
            col[x + 3 : x + 4, :] = a.first(x)[y : y + 1]
        line[s, 0:10, :] = side[Z_P : Z_P + 10, :] + side[Z_W : Z_W + 10, :] * col[0:10, :]
        for x in range(-2, 6):
            col[x + 2 : x + 3, :] = c2[x][y : y + 1]
        mid = line[s, 1:9, :]
        line3[s, 0:8, :] = (
            KEEP * mid
            + side[Z_Q : Z_Q + 8, :]
            + side[Z_W + 1 : Z_W + 9, :]
            * (line[s, 0:8, :] + line[s, 2:10, :] + beside_z(mid) + col[0:8, :])
        )
    c3 = {}
    for x in range(-2, 6):
        c = c2[x]
        c3[x] = KEEP * c + a.first(x) + a.w(x) * (
            c2[x - 1]
            + c2[x + 1]
            + beside_z(c)
            + beside_y(c, line[0, x + 3 : x + 4, :], line[1, x + 3 : x + 4, :])
        )
    for x in range(-1, 5):
        c = c3[x]
        c4 = KEEP * c + a.first(x) + a.w(x) * (
            c3[x - 1]
            + c3[x + 1]
            + beside_z(c)
            + beside_y(c, line3[0, x + 2 : x + 3, :], line3[1, x + 2 : x + 3, :])
        )
        fine[pl.ds((x + 1) * BY, CY, stride=2), :] = c4
        fine[pl.ds((x + 1) * BY + 1, CY, stride=2), :] = c4
    for s, (side, y) in enumerate(sides):
        for x in range(-1, 5):
            col[x + 1 : x + 2, :] = c3[x][y : y + 1]
        mid = line3[s, 1:7, :]
        third = side[Z_R : Z_R + 6, :] + side[Z_V : Z_V + 6, :] * line[s, 2:8, :]
        fine[6 * BY + 8 * s : 6 * BY + 8 * s + 6, :] = (
            KEEP * mid
            + side[Z_C + 2 : Z_C + 8, :]
            + side[Z_W + 2 : Z_W + 8, :]
            * (line3[s, 0:6, :] + line3[s, 2:8, :] + beside_z(mid) + third + col[0:6, :])
        )
        fine[6 * BY + 8 * s + 6 : 6 * BY + 8 * s + 8, :] = jnp.zeros((2, CZ), F32)
    spread_z(fine[...], corr)
    g0 = {}
    for x in range(-2, 10):
        if x == -2:
            f = slab(cleft, 2)
        elif x == 9:
            f = slab(a.right, 2)
        else:
            f = slab(f2, x + 1)
        g0[x] = f + slab(corr, (x + 2) // 2)
    for s, (cside, side, y, f2side) in enumerate(((clow, low, 0, f2low), (chigh, high, BY - 1, f2high))):
        base = 6 * BY + 8 * s
        for x in range(-1, 9):
            k = base + (x + 2) // 2
            col2[x + 1 : x + 2, :] = corr[k : k + 1, :]
        gline[s, 1:9, :] = f2side[...] + col2[1:9, :]
        for j, x in enumerate((-1, 8)):
            k = Z_K + 2 * j
            gline[s, x + 1 : x + 2, 0:CZ] = row(cside, k) + col2[x + 1 : x + 2, 0:CZ]
            gline[s, x + 1 : x + 2, CZ:] = row(cside, k + 1) + col2[x + 1 : x + 2, CZ:]
        for x in range(BX):
            k = Z_S + 2 * x
            s1[x : x + 1, 0:CZ] = row(cside, k)
            s1[x : x + 1, CZ:] = row(cside, k + 1)
        moved = col2[1:9, :]
        for x in range(BX):
            col2[x : x + 1, :] = g0[x][y : y + 1]
        mid = gline[s, 1:9, :]
        g1line[s, 0:8, :] = (
            KEEP * mid
            + s1[0:8, :]
            + side[Y_W : Y_W + 8, :]
            * (moved + gline[s, 0:8, :] + gline[s, 2:10, :] + beside_z(mid) + col2[0:8, :])
        )
    g1 = {}
    for x in range(-1, 9):
        f = g0[x]
        g1[x] = KEEP * f + wide.w(x) * (
            wide.rhs(x)
            + g0[x - 1]
            + g0[x + 1]
            + beside_z(f)
            + beside_y(f, gline[0, x + 1 : x + 2, :], gline[1, x + 1 : x + 2, :])
        )
    for x in range(BX):
        f = g1[x]
        out[place(x)] = KEEP * f + wide.w(x) * (
            wide.rhs(x)
            + g1[x - 1]
            + g1[x + 1]
            + beside_z(f)
            + beside_y(f, g1line[0, x : x + 1, :], g1line[1, x : x + 1, :])
        )


def send(v, links):
    n = lax.axis_size("dev")
    return lax.ppermute(v, ("group", "dev"), [(i * n + j, k * n + l) for (i, j), (k, l) in links])


def back(links):
    return [(j, i) for i, j in links]


def swap(v, pairs):
    return send(v, pairs + back(pairs))


def share_chip(v):
    groups = [[i, i + 1] for i in range(0, lax.axis_size("group"), 2)]
    return lax.all_gather(v, "group", axis_index_groups=groups)


def cross_pairs(keep):
    devs = [d for d in range(lax.axis_size("dev")) if keep(d)]
    return [((i, d), (i + 1, d)) for i in range(1, lax.axis_size("group") - 1, 2) for d in devs]


def dev_pairs(start, keep):
    devs = [d for d in range(start, lax.axis_size("dev") - 1, 2) if keep(d)]
    return [((i, d), (i, d + 1)) for i in range(lax.axis_size("group")) for d in devs]


def is_start(d):
    return d % RUN == 0


def in_middle(d):
    return not (is_start(d) or before_end(d))


def is_end(d):
    return d % RUN == RUN - 1


def before_end(d):
    return d % RUN == RUN - 2


def body(g, b, n):
    block = (BX, BY, NZ)
    cross, cross2, chip, even, odd, f1z, g, b, w, d = call(
        load_kernel,
        [(X_ROWS, NZ)] * 3 + [(Y_ROWS, NZ)] * 2 + [(BX * BY, NZ)] + [block] * 4,
        g, b, n,
        hbm=3,
        vmem=None,
        scratch=[pltpu.VMEM(block, jnp.int32), (2, Y_ROWS, NZ), pltpu.SemaphoreType.DMA((3,))],
    )
    cross1 = swap(cross, cross_pairs(lambda d: not is_end(d)))
    even1 = swap(even, dev_pairs(0, lambda d: not before_end(d)))
    odd1 = swap(odd, dev_pairs(1, lambda d: not before_end(d + 1)))
    cross2 = swap(cross2, cross_pairs(is_end))
    even2, odd2, chip = call(again_kernel, [(Y_ROWS, NZ)] * 2 + [(X_ROWS, NZ)], even, odd, chip, even1)
    even2 = swap(even2, dev_pairs(0, before_end))
    odd2 = swap(odd2, dev_pairs(1, lambda d: before_end(d + 1)))
    chip = share_chip(chip)
    left, both = call(
        gather_kernel,
        [(X_ROWS, NZ), (2, Y_ROWS, NZ)],
        cross1, even1, odd1,
        cost=pl.CostEstimate(flops=2**34, bytes_accessed=0, transcendentals=0),
    )
    f2, f2low, f2high, c1, wc, left, both, cross, near = call(
        middle_kernel,
        [(10 * BY, NZ), (BX, NZ), (BX, NZ), (CX * CY, CZ), (CX * CY, CZ), (X_ROWS, NZ), (2, Y_ROWS, NZ)] + [(X2_ROWS, NZ)] * 2,
        g, b, w, d, left, cross2, chip, f1z, both, even2, odd2,
        scratch=[(16, NZ), (2, 16, NZ), (4, CX * BY, CZ)],
    )
    cleft = swap(cross, cross_pairs(lambda d: True))
    cchip = share_chip(near)
    even, even2, odd, f2, f2low, f2high, c1x, c2z = call(
        pack_c_kernel,
        [(Z_ROWS, CZ)] * 3 + [(10 * BY, NZ), (BX, NZ), (BX, NZ), (3 * CX * CY, CZ), (10 * CY, CZ)],
        g, b, w, left, chip, both, f2, f2low, f2high, c1, wc, cleft, cchip,
        scratch=[(13, 8, NZ), (5, 8, NZ), (8, CZ), (2, Z_ROWS, CZ)],
    )
    inner, start, end = (dev_pairs(0, keep) for keep in (in_middle, is_start, before_end))
    even1 = send(even, inner + back(inner) + back(start))
    odd = swap(odd, dev_pairs(1, lambda d: True))
    even2 = send(even2, end + back(end) + start)
    (out,) = call(
        last_kernel,
        [block],
        g, b, w, left, chip, both, f2, f2low, f2high, c1x, wc, cleft, cchip, c2z, even1, odd, even2,
        scratch=[
            (2, Z_ROWS, CZ),
            (16, CZ), (2, 16, CZ), (2, 8, CZ), (6 * BY + 16, CZ), (6 * BY + 16, NZ), (16, NZ), (8, NZ), (2, 16, NZ), (2, 8, NZ),
        ],
        hbm_out=True,
    )
    return out


def solution(mesh):
    s = P("group", "dev", None)
    return jax.shard_map(body, mesh=mesh, in_specs=(s, s, s), out_specs=s, check_vma=False)
```

```python
import jax
import jax.numpy as jnp
from jax import lax
from jax.sharding import PartitionSpec as P
from jax.experimental import pallas as pl
from jax.experimental.pallas import tpu as pltpu

OMEGA = 0.8
KEEP = 1.0 - OMEGA
VM = pl.BlockSpec(memory_space=pltpu.VMEM)
F32 = jnp.float32
BX, BY, NZ = 8, 16, 256
CX, CY, CZ = 4, 8, 128
RUN = 32


def call(kernel, outs, *args, scratch=(), hbm=0, hbm_out=False, vmem=8 * 2**20, cost=None):
    make = jax.ShapeDtypeStruct if hbm_out else pltpu.VMEM
    return pl.pallas_call(
        kernel,
        out_shape=[make(s, F32) for s in outs],
        in_specs=[pl.BlockSpec(memory_space=pltpu.HBM)] * hbm + [VM] * (len(args) - hbm),
        out_specs=[VM] * len(outs),
        scratch_shapes=[pltpu.VMEM(s, F32) if isinstance(s, tuple) else s for s in scratch],
        compiler_params=pltpu.CompilerParams(vmem_limit_bytes=vmem),
        cost_estimate=cost,
    )(*args)


def beside_z(v):
    lane = lax.broadcasted_iota(jnp.int32, v.shape, 1)
    last = v.shape[1] - 1
    below = jnp.where(lane == 0, 0.0, pltpu.roll(v, 1, 1))
    above = jnp.where(lane == last, 0.0, pltpu.roll(v, last, 1))
    return below + above


def shift_y(v, low, high):
    row = lax.broadcasted_iota(jnp.int32, v.shape, 0)
    last = v.shape[0] - 1
    below = jnp.where(row == 0, low, pltpu.roll(v, 1, 0))
    above = jnp.where(row == last, high, pltpu.roll(v, last, 0))
    return below, above


def beside_y(v, low, high):
    below, above = shift_y(v, low, high)
    return below + above


def slab(ref, k, rows=BY):
    return ref[k * rows : (k + 1) * rows, :]


def by_row(n, rows):
    total = 0.0
    for k, v in rows.items():
        at = lax.broadcasted_iota(jnp.int32, (n, v.shape[1]), 0)
        total = jnp.where(at == k, v, total)
    return total


def row(ref, k):
    return ref[k : k + 1, :]


def lanes(v, index):
    return jnp.take_along_axis(v, index, axis=1)


def pair_z(low, high):
    lane = lax.broadcasted_iota(jnp.int32, low.shape, 1)
    low = low + pltpu.roll(low, CZ - 1, 1)
    high = high + pltpu.roll(high, CZ - 1, 1)
    index = (2 * lane) % CZ
    return jnp.where(lane < CZ // 2, lanes(low, index), lanes(high, index))


def spread_z(v, out):
    half = lax.broadcasted_iota(jnp.int32, v.shape, 1) // 2
    out[:, :CZ] = lanes(v, half)
    out[:, CZ:] = lanes(v, half + CZ // 2)


def diag_of(n):
    return 6.0 + 0.25 * n.astype(F32)


def place(x):
    odd = lax.axis_index("group") % 2
    return x + odd * (BX - 1 - 2 * x)


def partner(ref):
    return ref.at[1 - lax.axis_index("group") % 2]


def side_of_dev():
    return lax.axis_index("dev") % 2


Y_G, Y_P, Y_W, Y_Q, Y_G2, Y_W2 = 0, 8, 16, 24, 32, 34
Y_ROWS = 40
X_ROWS = 7 * BY


def load_kernel(
    g_hbm, b_hbm, n_hbm, cross, cross2, chip, even, odd, f1z, g, b, w, d, n, both, sems
):
    copies = [
        pltpu.make_async_copy(src, dst, sems.at[k])
        for k, (src, dst) in enumerate(((g_hbm, g), (b_hbm, b), (n_hbm, n)))
    ]
    for c in copies:
        c.start()
    for c in copies:
        c.wait()
    for x in range(BX):
        diag = diag_of(n[x])
        d[x] = diag
        w[x] = OMEGA / diag
    for out, layers in ((cross, (0, 1, 2)), (chip, (7, 6, 5))):
        for k in range(3):
            out[k * BY : (k + 1) * BY, :] = g[place(layers[k])]
        for k in range(2):
            out[(3 + k) * BY : (4 + k) * BY, :] = w[place(layers[k])]
            out[(5 + k) * BY : (6 + k) * BY, :] = b[place(layers[k])]
    zero = jnp.zeros((BY, NZ), F32)
    for x in range(BX):
        at = place(x)
        here, wx, bx = g[at], w[at], b[at]
        before = g[place(x - 1)] if x else zero
        after = g[place(x + 1)] if x < BX - 1 else zero
        f = KEEP * here + wx * (bx + before + after + beside_z(here) + beside_y(here, 0.0, 0.0))
        f1z[x * BY : (x + 1) * BY, :] = f
        for s, (y, inner) in enumerate(((0, 1), (BY - 1, BY - 2))):
            rows = [
                (Y_G + x, here[y : y + 1]),
                (Y_P + x, f[y : y + 1]),
                (Y_W + x, wx[y : y + 1]),
                (Y_Q + x, wx[y : y + 1] * (bx[y : y + 1] + f[inner : inner + 1])),
            ]
            if x in (0, 7):
                rows += [(Y_G2 + x // 7, here[inner : inner + 1]), (Y_W2 + x // 7, wx[inner : inner + 1])]
            for k, v in rows:
                both[s, k : k + 1, :] = v
    p = side_of_dev()
    even[...] = both[1 - p]
    odd[...] = both[p]
    cross2[...] = cross[...]


class Wide:
    def __init__(self, g, b, w, left, right):
        self.own, self.left, self.right = (g, w, b), left, partner(right)

    def _get(self, which, base, x, y):
        if 0 <= x < BX:
            v = self.own[which]
            return v[place(x)] if y is None else v[place(x), y : y + 1, :]
        ref, k = (self.left, -1 - x) if x < 0 else (self.right, x - BX)
        return slab(ref, base + k) if y is None else row(ref, (base + k) * BY + y)

    def guess(self, x, y=None):
        return self._get(0, 0, x, y)

    def w(self, x, y=None):
        return self._get(1, 3, x, y)

    def rhs(self, x, y=None):
        return self._get(2, 5, x, y)


def take(both, even, odd):
    p = side_of_dev()
    both[1 - p] = even
    both[p] = odd


def again_kernel(even, chip, met, even2, chip2):
    even2[...] = even[...]
    chip2[...] = chip[...]


def later_kernel(odd, met, odd2):
    odd2[...] = odd[...]


def gather_kernel(cross, even, odd, left, both):
    left[...] = cross[...]
    take(both, even[...], odd[...])


X2_D = 3 * BY
X2_ROWS = X2_D + 16


def diagonal_rows(edge):
    at, inner = (0, 1) if edge == 0 else (7, 6)
    return (Y_G + at, Y_G2 + edge, Y_G + inner, Y_P + at, Y_W + at, Y_W2 + edge, Y_W + inner)


def middle_kernel(
    g, b, w, d, left1, cross2, chip, f1z, both1, even2, odd2,
    f2, f2low, f2high, c1, wc, left, both, lo, hi, col, line, sums,
):
    left[...] = left1[...] + cross2[...]
    a = Wide(g, b, w, left, chip)
    p = side_of_dev()
    both[p] = both1[p] + odd2[...]
    both[1 - p] = both1[1 - p] + even2[...]
    low, high = both.at[0], both.at[1]
    rows = lax.broadcasted_iota(jnp.int32, (BY, NZ), 0)
    f1 = {}
    for x in range(-2, 10):
        if 0 <= x < BX:
            k = Y_G + x
            beyond = jnp.where(rows == 0, row(low, k), jnp.where(rows == BY - 1, row(high, k), 0.0))
            if x == 0:
                beyond = beyond + a.guess(-1)
            if x == BX - 1:
                beyond = beyond + a.guess(BX)
            f1[x] = slab(f1z, x) + a.w(x) * beyond
        else:
            here = a.guess(x)
            f1[x] = KEEP * here + a.w(x) * (
                a.rhs(x) + a.guess(x - 1) + a.guess(x + 1) + beside_z(here) + beside_y(here, 0.0, 0.0)
            )
    for s, (side, y, out) in enumerate(((low, 0, f2low), (high, BY - 1, f2high))):
        for x in range(BX):
            col[x : x + 1, :] = a.guess(x, y)
        line[s, 0:16, :] = jnp.zeros((16, NZ), F32)
        line[s, 1:9, :] = side[Y_P : Y_P + 8, :] + side[Y_W : Y_W + 8, :] * col[0:8, :]
        for x in range(BX):
            col[x : x + 1, :] = f1[x][y : y + 1]
        mid = line[s, 1:9, :]
        out[...] = (
            KEEP * mid
            + side[Y_Q : Y_Q + 8, :]
            + side[Y_W : Y_W + 8, :] * (line[s, 0:8, :] + line[s, 2:10, :] + beside_z(mid) + col[0:8, :])
        )
        for edge, pack in enumerate((lo, hi)):
            for k, r in enumerate(diagonal_rows(edge)):
                at = X2_D + 7 * s + k
                pack[at : at + 1, :] = row(side, r)
    for pack in (lo, hi):
        pack[X2_D + 14 :, :] = jnp.zeros((2, NZ), F32)
    sec = {}
    for x in range(-1, 9):
        f = f1[x]
        sec[x] = KEEP * f + a.w(x) * (
            a.rhs(x)
            + f1[x - 1]
            + f1[x + 1]
            + beside_z(f)
            + beside_y(f, line[0, x + 1 : x + 2, :], line[1, x + 1 : x + 2, :])
        )
        f2[(x + 1) * BY : (x + 2) * BY, :] = sec[x]
    lo[2 * BY : X2_D, :] = sec[1]
    hi[2 * BY : X2_D, :] = sec[6]
    for x in range(0, 8):
        f = sec[x]
        r = (
            a.rhs(x)
            - d[place(x)] * f
            + sec[x - 1]
            + sec[x + 1]
            + beside_z(f)
            + beside_y(f, row(f2low, x), row(f2high, x))
        )
        if x % 2:
            pairs = pairs + r
            points = points + d[place(x)]
            at = (x // 2) * BY
            for half in range(2):
                sums[half, at : at + BY, :] = pairs[:, half * CZ : (half + 1) * CZ]
                sums[2 + half, at : at + BY, :] = points[:, half * CZ : (half + 1) * CZ]
        else:
            pairs, points = r, d[place(x)]
    doubled = [
        sums[k, pl.ds(0, CX * CY, stride=2), :] + sums[k, pl.ds(1, CX * CY, stride=2), :] for k in range(4)
    ]
    total = pair_z(doubled[0], doubled[1])
    diags = pair_z(doubled[2], doubled[3])
    weight = OMEGA / (0.5 * diags - 18.0)
    first = weight * (0.5 * total)
    c1[...] = first
    wc[...] = weight
    for x in range(CX):
        for out, k in ((lo, x), (hi, CX - 1 - x)):
            out[k * CY : (k + 1) * CY, 0:CZ] = first[x * CY : (x + 1) * CY]
            out[k * CY : (k + 1) * CY, CZ:] = weight[x * CY : (x + 1) * CY]


class Coarse:
    def __init__(self, c1x, wc, left, right):
        self.c1x, self.wc, self.left, self.right = c1x, wc, left, right

    def first(self, x):
        return slab(self.c1x, x + CX, CY)

    def w(self, x):
        if 0 <= x < CX:
            return slab(self.wc, x, CY)
        ref, k = (self.left, -1 - x) if x < 0 else (self.right, x - CX)
        return ref[k * CY : (k + 1) * CY, CZ:]


def corner_terms(a, low, high, relays, put):
    for e, (xe, xi, xn, xm) in enumerate(((0, 1, -1, -2), (7, 6, 8, 9))):
        for s, (side, y, yi) in enumerate(((low, 0, 1), (high, BY - 1, BY - 2))):
            own = [row(side, r) for r in diagonal_rows(e)]
            far = [row(relays[e], X2_D + 7 * s + k) for k in range(7)]
            corner, beside = a.guess(xe, y), a.guess(xn, y)
            w_corner, w_beside = a.w(xe, y), a.w(xn, y)
            put(2 * e + s, far[:5] + [beside + own[0], w_beside, a.w(xm, y), a.w(xn, yi), own[4], own[5], own[6], w_corner])
            put(4 + 2 * e + s, own[:5] + [corner + far[0], w_corner, a.w(xi, y), a.w(xe, yi), far[4], far[5], far[6], w_beside])


def corner_sums(t):
    g1, g2, g3, part, wd, near, wx, wx2, wxs, wy, wy2, wys, wq = (t[k] for k in range(13))
    dq = jnp.where(wq > 0.0, OMEGA / jnp.where(wq > 0.0, wq, 1.0), 0.0)
    by_y = wy * g1
    by_x = wx * g1
    diagonal = part + wd * near
    at_q = wq * (by_x + by_y)
    at_y = KEEP * by_y + wy * (beside_z(by_y) + diagonal + wy2 * g2)
    at_x = KEEP * by_x + wx * (beside_z(by_x) + diagonal + wx2 * g3)
    at_ys = wys * by_y
    at_xs = wxs * by_x
    total = at_y + at_x + beside_z(at_q) - dq * at_q + 2.0 * at_q + at_ys + at_xs
    return at_q, at_y, at_x, at_ys, at_xs, 0.5 * pair_z(total[:, :CZ], total[:, CZ:])


Z_C, Z_P, Z_W, Z_Q, Z_R, Z_V, Z_S, Z_K = 0, 10, 20, 30, 38, 44, 50, 66
Z_ROWS = 72


def pack_c_kernel(
    g, b, w, left, chip, both, f2in, f2lowin, f2highin, c1, wc, cleft, cchip,
    even, even2, odd, f2, f2low, f2high, c1x, c2z, table, terms, rows, sides,
):
    fine = Wide(g, b, w, left, chip)
    cright = partner(cchip)

    def put(i, values):
        for k, v in enumerate(values):
            table[k, i : i + 1, :] = v

    corner_terms(fine, both.at[0], both.at[1], (cleft, cright), put)
    *parts, share = corner_sums(table)
    for k, v in enumerate(parts):
        terms[k] = v
    rows[...] = share
    a = Coarse(c1x, wc, cleft, cright)
    for x in range(1, CX):
        c1x[(CX - 1 - x) * CY : (CX - x) * CY, :] = cleft[x * CY : (x + 1) * CY, 0:CZ]
        c1x[(x + 2 * CX) * CY : (x + 2 * CX + 1) * CY, :] = cright[x * CY : (x + 1) * CY, 0:CZ]
    for x in range(1, CX - 1):
        c1x[(x + CX) * CY : (x + CX + 1) * CY, :] = slab(c1, x, CY)
    term = lambda k, e, s: terms[k, 2 * e + s : 2 * e + s + 1, :]
    for e, (xe, xn, cxe, cxn) in enumerate(((0, -1, 0, -1), (7, 8, 3, 4))):
        at = (xe + 1) * BY
        f2[at : at + BY, :] = f2in[at : at + BY, :] + by_row(BY, {0: term(0, e, 0), BY - 1: term(0, e, 1)})
        at = (xn + 1) * BY
        f2[at : at + BY, :] = f2in[at : at + BY, :] + by_row(
            BY, {0: term(2, e, 0), 1: term(4, e, 0), BY - 2: term(4, e, 1), BY - 1: term(2, e, 1)}
        )
        for i, cx in ((2 * e, cxe), (2 * e + 4, cxn)):
            at = (cx + CX) * CY
            given = slab(c1, cx, CY) if 0 <= cx < CX else (cleft if cx < 0 else cright)[0:CY, 0:CZ]
            c1x[at : at + CY, :] = given + a.w(cx) * by_row(CY, {0: row(rows, i), CY - 1: row(rows, i + 1)})
    f2[2 * BY : 8 * BY, :] = f2in[2 * BY : 8 * BY, :]
    for s, (side, sidein) in enumerate(((f2low, f2lowin), (f2high, f2highin))):
        side[...] = sidein[...] + by_row(
            BX, {0: term(1, 0, s), 1: term(3, 0, s), BX - 2: term(3, 1, s), BX - 1: term(1, 1, s)}
        )
    lo, hi = sides.at[0], sides.at[1]
    second = {}
    for x in range(-3, 7):
        c, cw = a.first(x), a.w(x)
        second[x] = (1.0 + KEEP) * c + cw * (
            a.first(x - 1) + a.first(x + 1) + beside_z(c) + beside_y(c, 0.0, 0.0)
        )
        c2z[(x + 3) * CY : (x + 4) * CY, :] = second[x]
        for out, y in ((lo, 0), (hi, CY - 1)):
            for base, v in ((Z_C, c), (Z_P, second[x]), (Z_W, cw)):
                k = base + x + 3
                out[k : k + 1, :] = v[y : y + 1]
    for x in range(-2, 6):
        s, c, cw = second[x], a.first(x), a.w(x)
        below, above = shift_y(s, 0.0, 0.0)
        inner = {0: above, 1: below}
        for side, (out, y, y2) in enumerate(((lo, 0, 1), (hi, CY - 1, CY - 2))):
            k = Z_Q + x + 2
            out[k : k + 1, :] = (c + cw * inner[side])[y : y + 1]
        if -1 <= x <= 4:
            part = KEEP * s + c + cw * (second[x - 1] + second[x + 1] + beside_z(s))
            for side, (out, y, y2) in enumerate(((lo, 0, 1), (hi, CY - 1, CY - 2))):
                k = Z_R + x + 1
                out[k : k + 1, :] = (part + cw * inner[side])[y2 : y2 + 1]
                k = Z_V + x + 1
                out[k : k + 1, :] = cw[y2 : y2 + 1]
    for out, y, inner in ((lo, 0, 1), (hi, BY - 1, BY - 2)):
        for x in range(BX):
            at = (x + 1) * BY
            v = fine.w(x, y) * (fine.rhs(x, y) + row(f2, at + inner))
            for half in range(2):
                k = Z_S + 2 * x + half
                out[k : k + 1, :] = v[:, half * CZ : (half + 1) * CZ]
        for j, x in enumerate((-1, 8)):
            at = (x + 1) * BY + y
            v = f2[at : at + 1, :]
            for half in range(2):
                k = Z_K + 2 * j + half
                out[k : k + 1, :] = v[:, half * CZ : (half + 1) * CZ]
    p = side_of_dev()
    even[...] = sides[1 - p]
    even2[...] = sides[1 - p]
    odd[...] = sides[p]


def last_kernel(
    g, b, w, left, chip, both, f2, f2low, f2high, c1x, wc, cleft, cchip, c2z, even1, odd, even2,
    out, cboth, col, line, line3, fine, corr, col2, s1, gline, g1line,
):
    wide = Wide(g, b, w, left, chip)
    a = Coarse(c1x, wc, cleft, partner(cchip))
    take(cboth, even1[...] + even2[...], odd[...])
    low, high, clow, chigh = both.at[0], both.at[1], cboth.at[0], cboth.at[1]
    crow = lax.broadcasted_iota(jnp.int32, (CY, CZ), 0)
    c2 = {}
    for x in range(-3, 7):
        k = Z_C + x + 3
        beyond = jnp.where(crow == 0, row(clow, k), jnp.where(crow == CY - 1, row(chigh, k), 0.0))
        c2[x] = slab(c2z, x + 3, CY) + a.w(x) * beyond
    sides = ((clow, 0), (chigh, CY - 1))
    for s, (side, y) in enumerate(sides):
        for x in range(-3, 7):
            col[x + 3 : x + 4, :] = a.first(x)[y : y + 1]
        line[s, 0:10, :] = side[Z_P : Z_P + 10, :] + side[Z_W : Z_W + 10, :] * col[0:10, :]
        for x in range(-2, 6):
            col[x + 2 : x + 3, :] = c2[x][y : y + 1]
        mid = line[s, 1:9, :]
        line3[s, 0:8, :] = (
            KEEP * mid
            + side[Z_Q : Z_Q + 8, :]
            + side[Z_W + 1 : Z_W + 9, :]
            * (line[s, 0:8, :] + line[s, 2:10, :] + beside_z(mid) + col[0:8, :])
        )
    c3 = {}
    for x in range(-2, 6):
        c = c2[x]
        c3[x] = KEEP * c + a.first(x) + a.w(x) * (
            c2[x - 1]
            + c2[x + 1]
            + beside_z(c)
            + beside_y(c, line[0, x + 3 : x + 4, :], line[1, x + 3 : x + 4, :])
        )
    for x in range(-1, 5):
        c = c3[x]
        c4 = KEEP * c + a.first(x) + a.w(x) * (
            c3[x - 1]
            + c3[x + 1]
            + beside_z(c)
            + beside_y(c, line3[0, x + 2 : x + 3, :], line3[1, x + 2 : x + 3, :])
        )
        fine[pl.ds((x + 1) * BY, CY, stride=2), :] = c4
        fine[pl.ds((x + 1) * BY + 1, CY, stride=2), :] = c4
    for s, (side, y) in enumerate(sides):
        for x in range(-1, 5):
            col[x + 1 : x + 2, :] = c3[x][y : y + 1]
        mid = line3[s, 1:7, :]
        third = side[Z_R : Z_R + 6, :] + side[Z_V : Z_V + 6, :] * line[s, 2:8, :]
        fine[6 * BY + 8 * s : 6 * BY + 8 * s + 6, :] = (
            KEEP * mid
            + side[Z_C + 2 : Z_C + 8, :]
            + side[Z_W + 2 : Z_W + 8, :]
            * (line3[s, 0:6, :] + line3[s, 2:8, :] + beside_z(mid) + third + col[0:6, :])
        )
        fine[6 * BY + 8 * s + 6 : 6 * BY + 8 * s + 8, :] = jnp.zeros((2, CZ), F32)
    spread_z(fine[...], corr)
    g0 = {}
    for x in range(-2, 10):
        if x == -2:
            f = slab(cleft, 2)
        elif x == 9:
            f = slab(a.right, 2)
        else:
            f = slab(f2, x + 1)
        g0[x] = f + slab(corr, (x + 2) // 2)
    for s, (cside, side, y, f2side) in enumerate(((clow, low, 0, f2low), (chigh, high, BY - 1, f2high))):
        base = 6 * BY + 8 * s
        for x in range(-1, 9):
            k = base + (x + 2) // 2
            col2[x + 1 : x + 2, :] = corr[k : k + 1, :]
        gline[s, 1:9, :] = f2side[...] + col2[1:9, :]
        for j, x in enumerate((-1, 8)):
            k = Z_K + 2 * j
            gline[s, x + 1 : x + 2, 0:CZ] = row(cside, k) + col2[x + 1 : x + 2, 0:CZ]
            gline[s, x + 1 : x + 2, CZ:] = row(cside, k + 1) + col2[x + 1 : x + 2, CZ:]
        for x in range(BX):
            k = Z_S + 2 * x
            s1[x : x + 1, 0:CZ] = row(cside, k)
            s1[x : x + 1, CZ:] = row(cside, k + 1)
        moved = col2[1:9, :]
        for x in range(BX):
            col2[x : x + 1, :] = g0[x][y : y + 1]
        mid = gline[s, 1:9, :]
        g1line[s, 0:8, :] = (
            KEEP * mid
            + s1[0:8, :]
            + side[Y_W : Y_W + 8, :]
            * (moved + gline[s, 0:8, :] + gline[s, 2:10, :] + beside_z(mid) + col2[0:8, :])
        )
    g1 = {}
    for x in range(-1, 9):
        f = g0[x]
        g1[x] = KEEP * f + wide.w(x) * (
            wide.rhs(x)
            + g0[x - 1]
            + g0[x + 1]
            + beside_z(f)
            + beside_y(f, gline[0, x + 1 : x + 2, :], gline[1, x + 1 : x + 2, :])
        )
    for x in range(BX):
        f = g1[x]
        out[place(x)] = KEEP * f + wide.w(x) * (
            wide.rhs(x)
            + g1[x - 1]
            + g1[x + 1]
            + beside_z(f)
            + beside_y(f, g1line[0, x : x + 1, :], g1line[1, x : x + 1, :])
        )


def send(v, links):
    n = lax.axis_size("dev")
    return lax.ppermute(v, ("group", "dev"), [(i * n + j, k * n + l) for (i, j), (k, l) in links])


def back(links):
    return [(j, i) for i, j in links]


def swap(v, pairs):
    return send(v, pairs + back(pairs))


def share_chip(v):
    groups = [[i, i + 1] for i in range(0, lax.axis_size("group"), 2)]
    return lax.all_gather(v, "group", axis_index_groups=groups)


def cross_pairs(keep):
    devs = [d for d in range(lax.axis_size("dev")) if keep(d)]
    return [((i, d), (i + 1, d)) for i in range(1, lax.axis_size("group") - 1, 2) for d in devs]


def dev_pairs(start, keep):
    devs = [d for d in range(start, lax.axis_size("dev") - 1, 2) if keep(d)]
    return [((i, d), (i, d + 1)) for i in range(lax.axis_size("group")) for d in devs]


def is_start(d):
    return d % RUN == 0


def in_middle(d):
    return not (is_start(d) or before_end(d))


def is_end(d):
    return d % RUN == RUN - 1


def before_end(d):
    return d % RUN == RUN - 2


def body(g, b, n):
    block = (BX, BY, NZ)
    cross, cross2, chip, even, odd, f1z, g, b, w, d = call(
        load_kernel,
        [(X_ROWS, NZ)] * 3 + [(Y_ROWS, NZ)] * 2 + [(BX * BY, NZ)] + [block] * 4,
        g, b, n,
        hbm=3,
        vmem=None,
        scratch=[pltpu.VMEM(block, jnp.int32), (2, Y_ROWS, NZ), pltpu.SemaphoreType.DMA((3,))],
    )
    cross1 = swap(cross, cross_pairs(lambda d: not is_end(d)))
    even1 = swap(even, dev_pairs(0, lambda d: not before_end(d)))
    odd1 = swap(odd, dev_pairs(1, lambda d: not before_end(d + 1)))
    cross2 = swap(cross2, cross_pairs(is_end))
    even2, chip = call(again_kernel, [(Y_ROWS, NZ), (X_ROWS, NZ)], even, chip, even1)
    even2 = swap(even2, dev_pairs(0, before_end))
    chip = share_chip(chip)
    (odd2,) = call(later_kernel, [(Y_ROWS, NZ)], odd, chip)
    odd2 = swap(odd2, dev_pairs(1, lambda d: before_end(d + 1)))
    left, both = call(
        gather_kernel,
        [(X_ROWS, NZ), (2, Y_ROWS, NZ)],
        cross1, even1, odd1,
        cost=pl.CostEstimate(flops=2**34, bytes_accessed=0, transcendentals=0),
    )
    f2, f2low, f2high, c1, wc, left, both, cross, near = call(
        middle_kernel,
        [(10 * BY, NZ), (BX, NZ), (BX, NZ), (CX * CY, CZ), (CX * CY, CZ), (X_ROWS, NZ), (2, Y_ROWS, NZ)] + [(X2_ROWS, NZ)] * 2,
        g, b, w, d, left, cross2, chip, f1z, both, even2, odd2,
        scratch=[(16, NZ), (2, 16, NZ), (4, CX * BY, CZ)],
    )
    cleft = swap(cross, cross_pairs(lambda d: True))
    cchip = share_chip(near)
    even, even2, odd, f2, f2low, f2high, c1x, c2z = call(
        pack_c_kernel,
        [(Z_ROWS, CZ)] * 3 + [(10 * BY, NZ), (BX, NZ), (BX, NZ), (3 * CX * CY, CZ), (10 * CY, CZ)],
        g, b, w, left, chip, both, f2, f2low, f2high, c1, wc, cleft, cchip,
        scratch=[(13, 8, NZ), (5, 8, NZ), (8, CZ), (2, Z_ROWS, CZ)],
    )
    inner, start, end = (dev_pairs(0, keep) for keep in (in_middle, is_start, before_end))
    even1 = send(even, inner + back(inner) + back(start))
    odd = swap(odd, dev_pairs(1, lambda d: True))
    even2 = send(even2, end + back(end) + start)
    (out,) = call(
        last_kernel,
        [block],
        g, b, w, left, chip, both, f2, f2low, f2high, c1x, wc, cleft, cchip, c2z, even1, odd, even2,
        scratch=[
            (2, Z_ROWS, CZ),
            (16, CZ), (2, 16, CZ), (2, 8, CZ), (6 * BY + 16, CZ), (6 * BY + 16, NZ), (16, NZ), (8, NZ), (2, 16, NZ), (2, 8, NZ),
        ],
        hbm_out=True,
    )
    return out


def solution(mesh):
    s = P("group", "dev", None)
    return jax.shard_map(body, mesh=mesh, in_specs=(s, s, s), out_specs=s, check_vma=False)
```

```python
import jax
import jax.numpy as jnp
from jax import lax
from jax.sharding import PartitionSpec as P
from jax.experimental import pallas as pl
from jax.experimental.pallas import tpu as pltpu

OMEGA = 0.8
KEEP = 1.0 - OMEGA
VM = pl.BlockSpec(memory_space=pltpu.VMEM)
F32 = jnp.float32
BX, BY, NZ = 8, 16, 256
CX, CY, CZ = 4, 8, 128
RUN = 32


def call(kernel, outs, *args, scratch=(), hbm=0, hbm_out=False, vmem=8 * 2**20, cost=None):
    make = jax.ShapeDtypeStruct if hbm_out else pltpu.VMEM
    return pl.pallas_call(
        kernel,
        out_shape=[make(s, F32) for s in outs],
        in_specs=[pl.BlockSpec(memory_space=pltpu.HBM)] * hbm + [VM] * (len(args) - hbm),
        out_specs=[VM] * len(outs),
        scratch_shapes=[pltpu.VMEM(s, F32) if isinstance(s, tuple) else s for s in scratch],
        compiler_params=pltpu.CompilerParams(vmem_limit_bytes=vmem),
        cost_estimate=cost,
    )(*args)


def beside_z(v):
    lane = lax.broadcasted_iota(jnp.int32, v.shape, 1)
    last = v.shape[1] - 1
    below = jnp.where(lane == 0, 0.0, pltpu.roll(v, 1, 1))
    above = jnp.where(lane == last, 0.0, pltpu.roll(v, last, 1))
    return below + above


def shift_y(v, low, high):
    row = lax.broadcasted_iota(jnp.int32, v.shape, 0)
    last = v.shape[0] - 1
    below = jnp.where(row == 0, low, pltpu.roll(v, 1, 0))
    above = jnp.where(row == last, high, pltpu.roll(v, last, 0))
    return below, above


def beside_y(v, low, high):
    below, above = shift_y(v, low, high)
    return below + above


def slab(ref, k, rows=BY):
    return ref[k * rows : (k + 1) * rows, :]


def by_row(n, rows):
    total = 0.0
    for k, v in rows.items():
        at = lax.broadcasted_iota(jnp.int32, (n, v.shape[1]), 0)
        total = jnp.where(at == k, v, total)
    return total


def row(ref, k):
    return ref[k : k + 1, :]


def lanes(v, index):
    return jnp.take_along_axis(v, index, axis=1)


def pair_z(low, high):
    lane = lax.broadcasted_iota(jnp.int32, low.shape, 1)
    index = (2 * lane) % CZ
    first = jnp.where(lane < CZ // 2, lanes(low, index), lanes(high, index))
    second = jnp.where(lane < CZ // 2, lanes(low, index + 1), lanes(high, index + 1))
    return first + second


def spread_z(v):
    half = lax.broadcasted_iota(jnp.int32, v.shape, 1) // 2
    return lanes(v, half), lanes(v, half + CZ // 2)


def diag_of(n):
    return 6.0 + 0.25 * n.astype(F32)


def place(x):
    odd = lax.axis_index("group") % 2
    return x + odd * (BX - 1 - 2 * x)


def partner(ref):
    return ref.at[1 - lax.axis_index("group") % 2]


def side_of_dev():
    return lax.axis_index("dev") % 2


Y_G, Y_P, Y_W, Y_Q, Y_G2, Y_W2 = 0, 8, 16, 24, 32, 34
Y_ROWS = 40
X_ROWS = 7 * BY


def load_kernel(
    g_hbm, b_hbm, n_hbm, cross, cross2, chip, even, odd, f1z, g, b, w, d, n, both, sems
):
    copies = [
        pltpu.make_async_copy(src, dst, sems.at[k])
        for k, (src, dst) in enumerate(((g_hbm, g), (b_hbm, b), (n_hbm, n)))
    ]
    for c in copies:
        c.start()
    for c in copies:
        c.wait()
    for x in range(BX):
        diag = diag_of(n[x])
        d[x] = diag
        w[x] = OMEGA / diag
    for out, layers in ((cross, (0, 1, 2)), (chip, (7, 6, 5))):
        for k in range(3):
            out[k * BY : (k + 1) * BY, :] = g[place(layers[k])]
        for k in range(2):
            out[(3 + k) * BY : (4 + k) * BY, :] = w[place(layers[k])]
            out[(5 + k) * BY : (6 + k) * BY, :] = b[place(layers[k])]
    zero = jnp.zeros((BY, NZ), F32)
    for x in range(BX):
        at = place(x)
        here, wx, bx = g[at], w[at], b[at]
        before = g[place(x - 1)] if x else zero
        after = g[place(x + 1)] if x < BX - 1 else zero
        f = KEEP * here + wx * (bx + before + after + beside_z(here) + beside_y(here, 0.0, 0.0))
        f1z[x * BY : (x + 1) * BY, :] = f
        for s, (y, inner) in enumerate(((0, 1), (BY - 1, BY - 2))):
            rows = [
                (Y_G + x, here[y : y + 1]),
                (Y_P + x, f[y : y + 1]),
                (Y_W + x, wx[y : y + 1]),
                (Y_Q + x, wx[y : y + 1] * (bx[y : y + 1] + f[inner : inner + 1])),
            ]
            if x in (0, 7):
                rows += [(Y_G2 + x // 7, here[inner : inner + 1]), (Y_W2 + x // 7, wx[inner : inner + 1])]
            for k, v in rows:
                both[s, k : k + 1, :] = v
    p = side_of_dev()
    even[...] = both[1 - p]
    odd[...] = both[p]
    cross2[...] = cross[...]


class Wide:
    def __init__(self, g, b, w, left, right):
        self.own, self.left, self.right = (g, w, b), left, partner(right)

    def _get(self, which, base, x, y):
        if 0 <= x < BX:
            v = self.own[which]
            return v[place(x)] if y is None else v[place(x), y : y + 1, :]
        ref, k = (self.left, -1 - x) if x < 0 else (self.right, x - BX)
        return slab(ref, base + k) if y is None else row(ref, (base + k) * BY + y)

    def guess(self, x, y=None):
        return self._get(0, 0, x, y)

    def w(self, x, y=None):
        return self._get(1, 3, x, y)

    def rhs(self, x, y=None):
        return self._get(2, 5, x, y)


def take(both, even, odd):
    p = side_of_dev()
    both[1 - p] = even
    both[p] = odd


def again_kernel(even, odd, chip, met, even2, odd2, chip2):
    chip2[...] = chip[...]
    even2[...] = even[...]
    odd2[...] = odd[...]


def gather_kernel(cross, even, odd, left, both):
    left[...] = cross[...]
    take(both, even[...], odd[...])


X2_D = 3 * BY
X2_ROWS = X2_D + 16


def diagonal_rows(edge):
    at, inner = (0, 1) if edge == 0 else (7, 6)
    return (Y_G + at, Y_G2 + edge, Y_G + inner, Y_P + at, Y_W + at, Y_W2 + edge, Y_W + inner)


def middle_kernel(
    g, b, w, d, left1, cross2, chip, f1z, both1, even2, odd2,
    f2, f2low, f2high, c1, wc, left, both, lo, hi, col, line, sums,
):
    left[...] = left1[...] + cross2[...]
    a = Wide(g, b, w, left, chip)
    p = side_of_dev()
    both[p] = both1[p] + odd2[...]
    both[1 - p] = both1[1 - p] + even2[...]
    low, high = both.at[0], both.at[1]
    rows = lax.broadcasted_iota(jnp.int32, (BY, NZ), 0)
    f1 = {}
    for x in range(-2, 10):
        if 0 <= x < BX:
            k = Y_G + x
            beyond = jnp.where(rows == 0, row(low, k), jnp.where(rows == BY - 1, row(high, k), 0.0))
            if x == 0:
                beyond = beyond + a.guess(-1)
            if x == BX - 1:
                beyond = beyond + a.guess(BX)
            f1[x] = slab(f1z, x) + a.w(x) * beyond
        else:
            here = a.guess(x)
            f1[x] = KEEP * here + a.w(x) * (
                a.rhs(x) + a.guess(x - 1) + a.guess(x + 1) + beside_z(here) + beside_y(here, 0.0, 0.0)
            )
    for s, (side, y, out) in enumerate(((low, 0, f2low), (high, BY - 1, f2high))):
        for x in range(BX):
            col[x : x + 1, :] = a.guess(x, y)
        line[s, 0:16, :] = jnp.zeros((16, NZ), F32)
        line[s, 1:9, :] = side[Y_P : Y_P + 8, :] + side[Y_W : Y_W + 8, :] * col[0:8, :]
        for x in range(BX):
            col[x : x + 1, :] = f1[x][y : y + 1]
        mid = line[s, 1:9, :]
        out[...] = (
            KEEP * mid
            + side[Y_Q : Y_Q + 8, :]
            + side[Y_W : Y_W + 8, :] * (line[s, 0:8, :] + line[s, 2:10, :] + beside_z(mid) + col[0:8, :])
        )
        for edge, pack in enumerate((lo, hi)):
            for k, r in enumerate(diagonal_rows(edge)):
                at = X2_D + 7 * s + k
                pack[at : at + 1, :] = row(side, r)
    for pack in (lo, hi):
        pack[X2_D + 14 :, :] = jnp.zeros((2, NZ), F32)
    sec = {}
    for x in range(-1, 9):
        f = f1[x]
        sec[x] = KEEP * f + a.w(x) * (
            a.rhs(x)
            + f1[x - 1]
            + f1[x + 1]
            + beside_z(f)
            + beside_y(f, line[0, x + 1 : x + 2, :], line[1, x + 1 : x + 2, :])
        )
        f2[(x + 1) * BY : (x + 2) * BY, :] = sec[x]
    lo[2 * BY : X2_D, :] = sec[1]
    hi[2 * BY : X2_D, :] = sec[6]
    for x in range(0, 8):
        f = sec[x]
        r = (
            a.rhs(x)
            - d[place(x)] * f
            + sec[x - 1]
            + sec[x + 1]
            + beside_z(f)
            + beside_y(f, row(f2low, x), row(f2high, x))
        )
        if x % 2:
            pairs = pairs + r
            points = points + d[place(x)]
            at = (x // 2) * BY
            for half in range(2):
                sums[half, at : at + BY, :] = pairs[:, half * CZ : (half + 1) * CZ]
                sums[2 + half, at : at + BY, :] = points[:, half * CZ : (half + 1) * CZ]
        else:
            pairs, points = r, d[place(x)]
    doubled = [
        sums[k, pl.ds(0, CX * CY, stride=2), :] + sums[k, pl.ds(1, CX * CY, stride=2), :] for k in range(4)
    ]
    total = pair_z(doubled[0], doubled[1])
    diags = pair_z(doubled[2], doubled[3])
    weight = OMEGA / (0.5 * diags - 18.0)
    first = weight * (0.5 * total)
    c1[...] = first
    wc[...] = weight
    for x in range(CX):
        for out, k in ((lo, x), (hi, CX - 1 - x)):
            out[k * CY : (k + 1) * CY, 0:CZ] = first[x * CY : (x + 1) * CY]
            out[k * CY : (k + 1) * CY, CZ:] = weight[x * CY : (x + 1) * CY]


class Coarse:
    def __init__(self, c1x, wc, left, right):
        self.c1x, self.wc, self.left, self.right = c1x, wc, left, right

    def first(self, x):
        return slab(self.c1x, x + CX, CY)

    def w(self, x):
        if 0 <= x < CX:
            return slab(self.wc, x, CY)
        ref, k = (self.left, -1 - x) if x < 0 else (self.right, x - CX)
        return ref[k * CY : (k + 1) * CY, CZ:]


def corner_terms(a, low, high, relays, put):
    for e, (xe, xi, xn, xm) in enumerate(((0, 1, -1, -2), (7, 6, 8, 9))):
        for s, (side, y, yi) in enumerate(((low, 0, 1), (high, BY - 1, BY - 2))):
            own = [row(side, r) for r in diagonal_rows(e)]
            far = [row(relays[e], X2_D + 7 * s + k) for k in range(7)]
            corner, beside = a.guess(xe, y), a.guess(xn, y)
            w_corner, w_beside = a.w(xe, y), a.w(xn, y)
            put(2 * e + s, far[:5] + [beside + own[0], w_beside, a.w(xm, y), a.w(xn, yi), own[4], own[5], own[6], w_corner])
            put(4 + 2 * e + s, own[:5] + [corner + far[0], w_corner, a.w(xi, y), a.w(xe, yi), far[4], far[5], far[6], w_beside])


def corner_sums(t):
    g1, g2, g3, part, wd, near, wx, wx2, wxs, wy, wy2, wys, wq = (t[k] for k in range(13))
    dq = jnp.where(wq > 0.0, OMEGA / jnp.where(wq > 0.0, wq, 1.0), 0.0)
    by_y = wy * g1
    by_x = wx * g1
    diagonal = part + wd * near
    at_q = wq * (by_x + by_y)
    at_y = KEEP * by_y + wy * (beside_z(by_y) + diagonal + wy2 * g2)
    at_x = KEEP * by_x + wx * (beside_z(by_x) + diagonal + wx2 * g3)
    at_ys = wys * by_y
    at_xs = wxs * by_x
    total = at_y + at_x + beside_z(at_q) - dq * at_q + 2.0 * at_q + at_ys + at_xs
    return at_q, at_y, at_x, at_ys, at_xs, 0.5 * pair_z(total[:, :CZ], total[:, CZ:])


Z_C, Z_P, Z_W, Z_Q, Z_R, Z_V, Z_S, Z_K = 0, 10, 20, 30, 38, 44, 50, 66
Z_ROWS = 72


def pack_c_kernel(
    g, b, w, left, chip, both, f2in, f2lowin, f2highin, c1, wc, cleft, cchip,
    even, even2, odd, f2, f2low, f2high, c1x, c2z, table, terms, rows, sides,
):
    fine = Wide(g, b, w, left, chip)
    cright = partner(cchip)

    def put(i, values):
        for k, v in enumerate(values):
            table[k, i : i + 1, :] = v

    corner_terms(fine, both.at[0], both.at[1], (cleft, cright), put)
    *parts, share = corner_sums(table)
    for k, v in enumerate(parts):
        terms[k] = v
    rows[...] = share
    a = Coarse(c1x, wc, cleft, cright)
    for x in range(1, CX):
        c1x[(CX - 1 - x) * CY : (CX - x) * CY, :] = cleft[x * CY : (x + 1) * CY, 0:CZ]
        c1x[(x + 2 * CX) * CY : (x + 2 * CX + 1) * CY, :] = cright[x * CY : (x + 1) * CY, 0:CZ]
    for x in range(1, CX - 1):
        c1x[(x + CX) * CY : (x + CX + 1) * CY, :] = slab(c1, x, CY)
    term = lambda k, e, s: terms[k, 2 * e + s : 2 * e + s + 1, :]
    for e, (xe, xn, cxe, cxn) in enumerate(((0, -1, 0, -1), (7, 8, 3, 4))):
        at = (xe + 1) * BY
        f2[at : at + BY, :] = f2in[at : at + BY, :] + by_row(BY, {0: term(0, e, 0), BY - 1: term(0, e, 1)})
        at = (xn + 1) * BY
        f2[at : at + BY, :] = f2in[at : at + BY, :] + by_row(
            BY, {0: term(2, e, 0), 1: term(4, e, 0), BY - 2: term(4, e, 1), BY - 1: term(2, e, 1)}
        )
        for i, cx in ((2 * e, cxe), (2 * e + 4, cxn)):
            at = (cx + CX) * CY
            given = slab(c1, cx, CY) if 0 <= cx < CX else (cleft if cx < 0 else cright)[0:CY, 0:CZ]
            c1x[at : at + CY, :] = given + a.w(cx) * by_row(CY, {0: row(rows, i), CY - 1: row(rows, i + 1)})
    f2[2 * BY : 8 * BY, :] = f2in[2 * BY : 8 * BY, :]
    for s, (side, sidein) in enumerate(((f2low, f2lowin), (f2high, f2highin))):
        side[...] = sidein[...] + by_row(
            BX, {0: term(1, 0, s), 1: term(3, 0, s), BX - 2: term(3, 1, s), BX - 1: term(1, 1, s)}
        )
    lo, hi = sides.at[0], sides.at[1]
    second = {}
    for x in range(-3, 7):
        c, cw = a.first(x), a.w(x)
        second[x] = (1.0 + KEEP) * c + cw * (
            a.first(x - 1) + a.first(x + 1) + beside_z(c) + beside_y(c, 0.0, 0.0)
        )
        c2z[(x + 3) * CY : (x + 4) * CY, :] = second[x]
        for out, y in ((lo, 0), (hi, CY - 1)):
            for base, v in ((Z_C, c), (Z_P, second[x]), (Z_W, cw)):
                k = base + x + 3
                out[k : k + 1, :] = v[y : y + 1]
    for x in range(-2, 6):
        s, c, cw = second[x], a.first(x), a.w(x)
        below, above = shift_y(s, 0.0, 0.0)
        inner = {0: above, 1: below}
        for side, (out, y, y2) in enumerate(((lo, 0, 1), (hi, CY - 1, CY - 2))):
            k = Z_Q + x + 2
            out[k : k + 1, :] = (c + cw * inner[side])[y : y + 1]
        if -1 <= x <= 4:
            part = KEEP * s + c + cw * (second[x - 1] + second[x + 1] + beside_z(s))
            for side, (out, y, y2) in enumerate(((lo, 0, 1), (hi, CY - 1, CY - 2))):
                k = Z_R + x + 1
                out[k : k + 1, :] = (part + cw * inner[side])[y2 : y2 + 1]
                k = Z_V + x + 1
                out[k : k + 1, :] = cw[y2 : y2 + 1]
    for out, y, inner in ((lo, 0, 1), (hi, BY - 1, BY - 2)):
        for x in range(BX):
            at = (x + 1) * BY
            v = fine.w(x, y) * (fine.rhs(x, y) + row(f2, at + inner))
            for half in range(2):
                k = Z_S + 2 * x + half
                out[k : k + 1, :] = v[:, half * CZ : (half + 1) * CZ]
        for j, x in enumerate((-1, 8)):
            at = (x + 1) * BY + y
            v = f2[at : at + 1, :]
            for half in range(2):
                k = Z_K + 2 * j + half
                out[k : k + 1, :] = v[:, half * CZ : (half + 1) * CZ]
    p = side_of_dev()
    even[...] = sides[1 - p]
    even2[...] = sides[1 - p]
    odd[...] = sides[p]


def last_kernel(
    g, b, w, left, chip, both, f2, f2low, f2high, c1x, wc, cleft, cchip, c2z, even1, odd, even2,
    out, cboth, col, line, line3, corr, col2, s1, gline, g1line,
):
    wide = Wide(g, b, w, left, chip)
    a = Coarse(c1x, wc, cleft, partner(cchip))
    take(cboth, even1[...] + even2[...], odd[...])
    low, high, clow, chigh = both.at[0], both.at[1], cboth.at[0], cboth.at[1]
    crow = lax.broadcasted_iota(jnp.int32, (CY, CZ), 0)
    c2 = {}
    for x in range(-3, 7):
        k = Z_C + x + 3
        beyond = jnp.where(crow == 0, row(clow, k), jnp.where(crow == CY - 1, row(chigh, k), 0.0))
        c2[x] = slab(c2z, x + 3, CY) + a.w(x) * beyond
    sides = ((clow, 0), (chigh, CY - 1))
    for s, (side, y) in enumerate(sides):
        for x in range(-3, 7):
            col[x + 3 : x + 4, :] = a.first(x)[y : y + 1]
        line[s, 0:10, :] = side[Z_P : Z_P + 10, :] + side[Z_W : Z_W + 10, :] * col[0:10, :]
        for x in range(-2, 6):
            col[x + 2 : x + 3, :] = c2[x][y : y + 1]
        mid = line[s, 1:9, :]
        line3[s, 0:8, :] = (
            KEEP * mid
            + side[Z_Q : Z_Q + 8, :]
            + side[Z_W + 1 : Z_W + 9, :]
            * (line[s, 0:8, :] + line[s, 2:10, :] + beside_z(mid) + col[0:8, :])
        )
    c3 = {}
    for x in range(-2, 6):
        c = c2[x]
        c3[x] = KEEP * c + a.first(x) + a.w(x) * (
            c2[x - 1]
            + c2[x + 1]
            + beside_z(c)
            + beside_y(c, line[0, x + 3 : x + 4, :], line[1, x + 3 : x + 4, :])
        )
    for x in range(-1, 5):
        c = c3[x]
        c4 = KEEP * c + a.first(x) + a.w(x) * (
            c3[x - 1]
            + c3[x + 1]
            + beside_z(c)
            + beside_y(c, line3[0, x + 2 : x + 3, :], line3[1, x + 2 : x + 3, :])
        )
        for half, v in enumerate(spread_z(c4)):
            corr[half, pl.ds((x + 1) * BY, CY, stride=2), :] = v
            corr[half, pl.ds((x + 1) * BY + 1, CY, stride=2), :] = v
    for s, (side, y) in enumerate(sides):
        for x in range(-1, 5):
            col[x + 1 : x + 2, :] = c3[x][y : y + 1]
        mid = line3[s, 1:7, :]
        third = side[Z_R : Z_R + 6, :] + side[Z_V : Z_V + 6, :] * line[s, 2:8, :]
        fourth = (
            KEEP * mid
            + side[Z_C + 2 : Z_C + 8, :]
            + side[Z_W + 2 : Z_W + 8, :]
            * (line3[s, 0:6, :] + line3[s, 2:8, :] + beside_z(mid) + third + col[0:6, :])
        )
        for half, v in enumerate(spread_z(fourth)):
            corr[half, 6 * BY + 8 * s : 6 * BY + 8 * s + 6, :] = v

    def corr_at(k, n):
        return jnp.concatenate([corr[0, k : k + n, :], corr[1, k : k + n, :]], axis=1)

    g0 = {}
    for x in range(-2, 10):
        if x == -2:
            f = slab(cleft, 2)
        elif x == 9:
            f = slab(a.right, 2)
        else:
            f = slab(f2, x + 1)
        g0[x] = f + corr_at((x + 2) // 2 * BY, BY)
    for s, (cside, side, y, f2side) in enumerate(((clow, low, 0, f2low), (chigh, high, BY - 1, f2high))):
        base = 6 * BY + 8 * s
        for x in range(-1, 9):
            k = base + (x + 2) // 2
            col2[x + 1 : x + 2, :] = corr_at(k, 1)
        gline[s, 1:9, :] = f2side[...] + col2[1:9, :]
        for j, x in enumerate((-1, 8)):
            k = Z_K + 2 * j
            gline[s, x + 1 : x + 2, 0:CZ] = row(cside, k) + col2[x + 1 : x + 2, 0:CZ]
            gline[s, x + 1 : x + 2, CZ:] = row(cside, k + 1) + col2[x + 1 : x + 2, CZ:]
        for x in range(BX):
            k = Z_S + 2 * x
            s1[x : x + 1, 0:CZ] = row(cside, k)
            s1[x : x + 1, CZ:] = row(cside, k + 1)
        moved = col2[1:9, :]
        for x in range(BX):
            col2[x : x + 1, :] = g0[x][y : y + 1]
        mid = gline[s, 1:9, :]
        g1line[s, 0:8, :] = (
            KEEP * mid
            + s1[0:8, :]
            + side[Y_W : Y_W + 8, :]
            * (moved + gline[s, 0:8, :] + gline[s, 2:10, :] + beside_z(mid) + col2[0:8, :])
        )
    g1 = {}
    for x in range(-1, 9):
        f = g0[x]
        g1[x] = KEEP * f + wide.w(x) * (
            wide.rhs(x)
            + g0[x - 1]
            + g0[x + 1]
            + beside_z(f)
            + beside_y(f, gline[0, x + 1 : x + 2, :], gline[1, x + 1 : x + 2, :])
        )
    for x in range(BX):
        f = g1[x]
        out[place(x)] = KEEP * f + wide.w(x) * (
            wide.rhs(x)
            + g1[x - 1]
            + g1[x + 1]
            + beside_z(f)
            + beside_y(f, g1line[0, x : x + 1, :], g1line[1, x : x + 1, :])
        )


def swap(v, pairs):
    n = lax.axis_size("dev")
    links = [(i * n + j, k * n + l) for (i, j), (k, l) in pairs]
    return lax.ppermute(v, ("group", "dev"), links + [(j, i) for i, j in links])


def share_chip(v):
    groups = [[i, i + 1] for i in range(0, lax.axis_size("group"), 2)]
    return lax.all_gather(v, "group", axis_index_groups=groups)


def cross_pairs(keep):
    devs = [d for d in range(lax.axis_size("dev")) if keep(d)]
    return [((i, d), (i + 1, d)) for i in range(1, lax.axis_size("group") - 1, 2) for d in devs]


def dev_pairs(start, keep):
    devs = [d for d in range(start, lax.axis_size("dev") - 1, 2) if keep(d)]
    return [((i, d), (i, d + 1)) for i in range(lax.axis_size("group")) for d in devs]


def is_end(d):
    return d % RUN == RUN - 1


def before_end(d):
    return d % RUN == RUN - 2


def body(g, b, n):
    block = (BX, BY, NZ)
    cross, cross2, chip, even, odd, f1z, g, b, w, d = call(
        load_kernel,
        [(X_ROWS, NZ)] * 3 + [(Y_ROWS, NZ)] * 2 + [(BX * BY, NZ)] + [block] * 4,
        g, b, n,
        hbm=3,
        vmem=None,
        scratch=[pltpu.VMEM(block, jnp.int32), (2, Y_ROWS, NZ), pltpu.SemaphoreType.DMA((3,))],
    )
    cross1 = swap(cross, cross_pairs(lambda d: not is_end(d)))
    even1 = swap(even, dev_pairs(0, lambda d: not before_end(d)))
    odd1 = swap(odd, dev_pairs(1, lambda d: not before_end(d + 1)))
    cross2 = swap(cross2, cross_pairs(is_end))
    even2, odd2, chip = call(again_kernel, [(Y_ROWS, NZ)] * 2 + [(X_ROWS, NZ)], even, odd, chip, even1)
    even2 = swap(even2, dev_pairs(0, before_end))
    odd2 = swap(odd2, dev_pairs(1, lambda d: before_end(d + 1)))
    chip = share_chip(chip)
    left, both = call(
        gather_kernel,
        [(X_ROWS, NZ), (2, Y_ROWS, NZ)],
        cross1, even1, odd1,
        cost=pl.CostEstimate(flops=2**34, bytes_accessed=0, transcendentals=0),
    )
    f2, f2low, f2high, c1, wc, left, both, cross, near = call(
        middle_kernel,
        [(10 * BY, NZ), (BX, NZ), (BX, NZ), (CX * CY, CZ), (CX * CY, CZ), (X_ROWS, NZ), (2, Y_ROWS, NZ)] + [(X2_ROWS, NZ)] * 2,
        g, b, w, d, left, cross2, chip, f1z, both, even2, odd2,
        scratch=[(16, NZ), (2, 16, NZ), (4, CX * BY, CZ)],
    )
    cleft = swap(cross, cross_pairs(lambda d: True))
    cchip = share_chip(near)
    even, even2, odd, f2, f2low, f2high, c1x, c2z = call(
        pack_c_kernel,
        [(Z_ROWS, CZ)] * 3 + [(10 * BY, NZ), (BX, NZ), (BX, NZ), (3 * CX * CY, CZ), (10 * CY, CZ)],
        g, b, w, left, chip, both, f2, f2low, f2high, c1, wc, cleft, cchip,
        scratch=[(13, 8, NZ), (5, 8, NZ), (8, CZ), (2, Z_ROWS, CZ)],
    )
    even1 = swap(even, dev_pairs(0, lambda d: not before_end(d)))
    odd = swap(odd, dev_pairs(1, lambda d: True))
    even2 = swap(even2, dev_pairs(0, before_end))
    (out,) = call(
        last_kernel,
        [block],
        g, b, w, left, chip, both, f2, f2low, f2high, c1x, wc, cleft, cchip, c2z, even1, odd, even2,
        scratch=[
            (2, Z_ROWS, CZ),
            (16, CZ), (2, 16, CZ), (2, 8, CZ), (2, 6 * BY + 16, CZ), (16, NZ), (8, NZ), (2, 16, NZ), (2, 8, NZ),
        ],
        hbm_out=True,
    )
    return out


def solution(mesh):
    s = P("group", "dev", None)
    return jax.shard_map(body, mesh=mesh, in_specs=(s, s, s), out_specs=s, check_vma=False)
```

```python
import jax
import jax.numpy as jnp
from jax import lax
from jax.sharding import PartitionSpec as P
from jax.experimental import pallas as pl
from jax.experimental.pallas import tpu as pltpu

OMEGA = 0.8
KEEP = 1.0 - OMEGA
VM = pl.BlockSpec(memory_space=pltpu.VMEM)
F32 = jnp.float32
BX, BY, NZ = 8, 16, 256
CX, CY, CZ = 4, 8, 128
RUN = 32


def call(kernel, outs, *args, scratch=(), hbm=0, hbm_out=False, vmem=8 * 2**20, cost=None):
    make = jax.ShapeDtypeStruct if hbm_out else pltpu.VMEM
    return pl.pallas_call(
        kernel,
        out_shape=[make(s, F32) for s in outs],
        in_specs=[pl.BlockSpec(memory_space=pltpu.HBM)] * hbm + [VM] * (len(args) - hbm),
        out_specs=[VM] * len(outs),
        scratch_shapes=[pltpu.VMEM(s, F32) if isinstance(s, tuple) else s for s in scratch],
        compiler_params=pltpu.CompilerParams(vmem_limit_bytes=vmem),
        cost_estimate=cost,
    )(*args)


def beside_z(v):
    lane = lax.broadcasted_iota(jnp.int32, v.shape, 1)
    last = v.shape[1] - 1
    below = jnp.where(lane == 0, 0.0, pltpu.roll(v, 1, 1))
    above = jnp.where(lane == last, 0.0, pltpu.roll(v, last, 1))
    return below + above


def shift_y(v, low, high):
    row = lax.broadcasted_iota(jnp.int32, v.shape, 0)
    last = v.shape[0] - 1
    below = jnp.where(row == 0, low, pltpu.roll(v, 1, 0))
    above = jnp.where(row == last, high, pltpu.roll(v, last, 0))
    return below, above


def beside_y(v, low, high):
    below, above = shift_y(v, low, high)
    return below + above


def slab(ref, k, rows=BY):
    return ref[k * rows : (k + 1) * rows, :]


def by_row(n, rows):
    total = 0.0
    for k, v in rows.items():
        at = lax.broadcasted_iota(jnp.int32, (n, v.shape[1]), 0)
        total = jnp.where(at == k, v, total)
    return total


def row(ref, k):
    return ref[k : k + 1, :]


def lanes(v, index):
    return jnp.take_along_axis(v, index, axis=1)


def pair_z(low, high):
    lane = lax.broadcasted_iota(jnp.int32, low.shape, 1)
    index = (2 * lane) % CZ
    first = jnp.where(lane < CZ // 2, lanes(low, index), lanes(high, index))
    second = jnp.where(lane < CZ // 2, lanes(low, index + 1), lanes(high, index + 1))
    return first + second


def spread_z(v):
    half = lax.broadcasted_iota(jnp.int32, v.shape, 1) // 2
    return lanes(v, half), lanes(v, half + CZ // 2)


def diag_of(n):
    return 6.0 + 0.25 * n.astype(F32)


def place(x):
    odd = lax.axis_index("group") % 2
    return x + odd * (BX - 1 - 2 * x)


def partner(ref):
    return ref.at[1 - lax.axis_index("group") % 2]


def side_of_dev():
    return lax.axis_index("dev") % 2


Y_G, Y_P, Y_W, Y_Q, Y_G2, Y_W2 = 0, 8, 16, 24, 32, 34
Y_ROWS = 40
X_ROWS = 7 * BY


def load_kernel(
    g_hbm, b_hbm, n_hbm, cross, cross2, chip, even, odd, f1z, g, b, w, d, n, both, sems
):
    copies = [
        pltpu.make_async_copy(src, dst, sems.at[k])
        for k, (src, dst) in enumerate(((g_hbm, g), (b_hbm, b), (n_hbm, n)))
    ]
    for c in copies:
        c.start()
    for c in copies:
        c.wait()
    for x in range(BX):
        diag = diag_of(n[x])
        d[x] = diag
        w[x] = OMEGA / diag
    for out, layers in ((cross, (0, 1, 2)), (chip, (7, 6, 5))):
        for k in range(3):
            out[k * BY : (k + 1) * BY, :] = g[place(layers[k])]
        for k in range(2):
            out[(3 + k) * BY : (4 + k) * BY, :] = w[place(layers[k])]
            out[(5 + k) * BY : (6 + k) * BY, :] = b[place(layers[k])]
    zero = jnp.zeros((BY, NZ), F32)
    for x in range(BX):
        at = place(x)
        here, wx, bx = g[at], w[at], b[at]
        before = g[place(x - 1)] if x else zero
        after = g[place(x + 1)] if x < BX - 1 else zero
        f = KEEP * here + wx * (bx + before + after + beside_z(here) + beside_y(here, 0.0, 0.0))
        f1z[x * BY : (x + 1) * BY, :] = f
        for s, (y, inner) in enumerate(((0, 1), (BY - 1, BY - 2))):
            rows = [
                (Y_G + x, here[y : y + 1]),
                (Y_P + x, f[y : y + 1]),
                (Y_W + x, wx[y : y + 1]),
                (Y_Q + x, wx[y : y + 1] * (bx[y : y + 1] + f[inner : inner + 1])),
            ]
            if x in (0, 7):
                rows += [(Y_G2 + x // 7, here[inner : inner + 1]), (Y_W2 + x // 7, wx[inner : inner + 1])]
            for k, v in rows:
                both[s, k : k + 1, :] = v
    p = side_of_dev()
    even[...] = both[1 - p]
    odd[...] = both[p]
    cross2[...] = cross[...]


class Wide:
    def __init__(self, g, b, w, left, right):
        self.own, self.left, self.right = (g, w, b), left, partner(right)

    def _get(self, which, base, x, y):
        if 0 <= x < BX:
            v = self.own[which]
            return v[place(x)] if y is None else v[place(x), y : y + 1, :]
        ref, k = (self.left, -1 - x) if x < 0 else (self.right, x - BX)
        return slab(ref, base + k) if y is None else row(ref, (base + k) * BY + y)

    def guess(self, x, y=None):
        return self._get(0, 0, x, y)

    def w(self, x, y=None):
        return self._get(1, 3, x, y)

    def rhs(self, x, y=None):
        return self._get(2, 5, x, y)


def take(both, even, odd):
    p = side_of_dev()
    both[1 - p] = even
    both[p] = odd


def again_kernel(even, odd, chip, met, even2, odd2, chip2):
    chip2[...] = chip[...]
    even2[...] = even[...]
    odd2[...] = odd[...]


def gather_kernel(cross, even, odd, left, both):
    left[...] = cross[...]
    take(both, even[...], odd[...])


X2_D = 3 * BY
X2_ROWS = X2_D + 16


def diagonal_rows(edge):
    at, inner = (0, 1) if edge == 0 else (7, 6)
    return (Y_G + at, Y_G2 + edge, Y_G + inner, Y_P + at, Y_W + at, Y_W2 + edge, Y_W + inner)


def middle_kernel(
    g, b, w, d, left1, cross2, chip, f1z, both1, even2, odd2,
    f2, f2low, f2high, c1, wc, left, both, lo, hi, col, line, sums,
):
    left[...] = left1[...] + cross2[...]
    a = Wide(g, b, w, left, chip)
    p = side_of_dev()
    both[p] = both1[p] + odd2[...]
    both[1 - p] = both1[1 - p] + even2[...]
    low, high = both.at[0], both.at[1]
    rows = lax.broadcasted_iota(jnp.int32, (BY, NZ), 0)
    f1 = {}
    for x in range(-2, 10):
        if 0 <= x < BX:
            k = Y_G + x
            beyond = jnp.where(rows == 0, row(low, k), jnp.where(rows == BY - 1, row(high, k), 0.0))
            if x == 0:
                beyond = beyond + a.guess(-1)
            if x == BX - 1:
                beyond = beyond + a.guess(BX)
            f1[x] = slab(f1z, x) + a.w(x) * beyond
        else:
            here = a.guess(x)
            f1[x] = KEEP * here + a.w(x) * (
                a.rhs(x) + a.guess(x - 1) + a.guess(x + 1) + beside_z(here) + beside_y(here, 0.0, 0.0)
            )
    for s, (side, y, out) in enumerate(((low, 0, f2low), (high, BY - 1, f2high))):
        for x in range(BX):
            col[x : x + 1, :] = a.guess(x, y)
        line[s, 0:16, :] = jnp.zeros((16, NZ), F32)
        line[s, 1:9, :] = side[Y_P : Y_P + 8, :] + side[Y_W : Y_W + 8, :] * col[0:8, :]
        for x in range(BX):
            col[x : x + 1, :] = f1[x][y : y + 1]
        mid = line[s, 1:9, :]
        out[...] = (
            KEEP * mid
            + side[Y_Q : Y_Q + 8, :]
            + side[Y_W : Y_W + 8, :] * (line[s, 0:8, :] + line[s, 2:10, :] + beside_z(mid) + col[0:8, :])
        )
        for edge, pack in enumerate((lo, hi)):
            for k, r in enumerate(diagonal_rows(edge)):
                at = X2_D + 7 * s + k
                pack[at : at + 1, :] = row(side, r)
    for pack in (lo, hi):
        pack[X2_D + 14 :, :] = jnp.zeros((2, NZ), F32)
    sec = {}
    for x in range(-1, 9):
        f = f1[x]
        sec[x] = KEEP * f + a.w(x) * (
            a.rhs(x)
            + f1[x - 1]
            + f1[x + 1]
            + beside_z(f)
            + beside_y(f, line[0, x + 1 : x + 2, :], line[1, x + 1 : x + 2, :])
        )
        f2[(x + 1) * BY : (x + 2) * BY, :] = sec[x]
    lo[2 * BY : X2_D, :] = sec[1]
    hi[2 * BY : X2_D, :] = sec[6]
    for x in range(0, 8):
        f = sec[x]
        r = (
            a.rhs(x)
            - d[place(x)] * f
            + sec[x - 1]
            + sec[x + 1]
            + beside_z(f)
            + beside_y(f, row(f2low, x), row(f2high, x))
        )
        if x % 2:
            pairs = pairs + r
            points = points + d[place(x)]
            at = (x // 2) * BY
            for half in range(2):
                sums[half, at : at + BY, :] = pairs[:, half * CZ : (half + 1) * CZ]
                sums[2 + half, at : at + BY, :] = points[:, half * CZ : (half + 1) * CZ]
        else:
            pairs, points = r, d[place(x)]
    doubled = [
        sums[k, pl.ds(0, CX * CY, stride=2), :] + sums[k, pl.ds(1, CX * CY, stride=2), :] for k in range(4)
    ]
    total = pair_z(doubled[0], doubled[1])
    diags = pair_z(doubled[2], doubled[3])
    weight = OMEGA / (0.5 * diags - 18.0)
    first = weight * (0.5 * total)
    c1[...] = first
    wc[...] = weight
    for x in range(CX):
        for out, k in ((lo, x), (hi, CX - 1 - x)):
            out[k * CY : (k + 1) * CY, 0:CZ] = first[x * CY : (x + 1) * CY]
            out[k * CY : (k + 1) * CY, CZ:] = weight[x * CY : (x + 1) * CY]


class Coarse:
    def __init__(self, c1x, wc, left, right):
        self.c1x, self.wc, self.left, self.right = c1x, wc, left, right

    def first(self, x):
        return slab(self.c1x, x + CX, CY)

    def w(self, x):
        if 0 <= x < CX:
            return slab(self.wc, x, CY)
        ref, k = (self.left, -1 - x) if x < 0 else (self.right, x - CX)
        return ref[k * CY : (k + 1) * CY, CZ:]


def corner_terms(a, low, high, relays, put):
    for e, (xe, xi, xn, xm) in enumerate(((0, 1, -1, -2), (7, 6, 8, 9))):
        for s, (side, y, yi) in enumerate(((low, 0, 1), (high, BY - 1, BY - 2))):
            own = [row(side, r) for r in diagonal_rows(e)]
            far = [row(relays[e], X2_D + 7 * s + k) for k in range(7)]
            corner, beside = a.guess(xe, y), a.guess(xn, y)
            w_corner, w_beside = a.w(xe, y), a.w(xn, y)
            put(2 * e + s, far[:5] + [beside + own[0], w_beside, a.w(xm, y), a.w(xn, yi), own[4], own[5], own[6], w_corner])
            put(4 + 2 * e + s, own[:5] + [corner + far[0], w_corner, a.w(xi, y), a.w(xe, yi), far[4], far[5], far[6], w_beside])


def corner_sums(t):
    g1, g2, g3, part, wd, near, wx, wx2, wxs, wy, wy2, wys, wq = (t[k] for k in range(13))
    dq = jnp.where(wq > 0.0, OMEGA / jnp.where(wq > 0.0, wq, 1.0), 0.0)
    by_y = wy * g1
    by_x = wx * g1
    diagonal = part + wd * near
    at_q = wq * (by_x + by_y)
    at_y = KEEP * by_y + wy * (beside_z(by_y) + diagonal + wy2 * g2)
    at_x = KEEP * by_x + wx * (beside_z(by_x) + diagonal + wx2 * g3)
    at_ys = wys * by_y
    at_xs = wxs * by_x
    total = at_y + at_x + beside_z(at_q) - dq * at_q + 2.0 * at_q + at_ys + at_xs
    return at_q, at_y, at_x, at_ys, at_xs, 0.5 * pair_z(total[:, :CZ], total[:, CZ:])


Z_C, Z_P, Z_W, Z_Q, Z_R, Z_V, Z_S, Z_K = 0, 10, 20, 30, 38, 44, 50, 66
Z_ROWS = 72


def pack_c_kernel(
    g, b, w, left, chip, both, f2in, f2lowin, f2highin, c1, wc, cleft, cchip,
    even, even2, odd, f2, f2low, f2high, c1x, c2z, table, terms, rows, sides,
):
    fine = Wide(g, b, w, left, chip)
    cright = partner(cchip)

    def put(i, values):
        for k, v in enumerate(values):
            table[k, i : i + 1, :] = v

    corner_terms(fine, both.at[0], both.at[1], (cleft, cright), put)
    *parts, share = corner_sums(table)
    for k, v in enumerate(parts):
        terms[k] = v
    rows[...] = share
    a = Coarse(c1x, wc, cleft, cright)
    for x in range(1, CX):
        c1x[(CX - 1 - x) * CY : (CX - x) * CY, :] = cleft[x * CY : (x + 1) * CY, 0:CZ]
        c1x[(x + 2 * CX) * CY : (x + 2 * CX + 1) * CY, :] = cright[x * CY : (x + 1) * CY, 0:CZ]
    for x in range(1, CX - 1):
        c1x[(x + CX) * CY : (x + CX + 1) * CY, :] = slab(c1, x, CY)
    term = lambda k, e, s: terms[k, 2 * e + s : 2 * e + s + 1, :]
    for e, (xe, xn, cxe, cxn) in enumerate(((0, -1, 0, -1), (7, 8, 3, 4))):
        at = (xe + 1) * BY
        f2[at : at + BY, :] = f2in[at : at + BY, :] + by_row(BY, {0: term(0, e, 0), BY - 1: term(0, e, 1)})
        at = (xn + 1) * BY
        f2[at : at + BY, :] = f2in[at : at + BY, :] + by_row(
            BY, {0: term(2, e, 0), 1: term(4, e, 0), BY - 2: term(4, e, 1), BY - 1: term(2, e, 1)}
        )
        for i, cx in ((2 * e, cxe), (2 * e + 4, cxn)):
            at = (cx + CX) * CY
            given = slab(c1, cx, CY) if 0 <= cx < CX else (cleft if cx < 0 else cright)[0:CY, 0:CZ]
            c1x[at : at + CY, :] = given + a.w(cx) * by_row(CY, {0: row(rows, i), CY - 1: row(rows, i + 1)})
    f2[2 * BY : 8 * BY, :] = f2in[2 * BY : 8 * BY, :]
    for s, (side, sidein) in enumerate(((f2low, f2lowin), (f2high, f2highin))):
        side[...] = sidein[...] + by_row(
            BX, {0: term(1, 0, s), 1: term(3, 0, s), BX - 2: term(3, 1, s), BX - 1: term(1, 1, s)}
        )
    lo, hi = sides.at[0], sides.at[1]
    second = {}
    for x in range(-3, 7):
        c, cw = a.first(x), a.w(x)
        second[x] = (1.0 + KEEP) * c + cw * (
            a.first(x - 1) + a.first(x + 1) + beside_z(c) + beside_y(c, 0.0, 0.0)
        )
        c2z[(x + 3) * CY : (x + 4) * CY, :] = second[x]
        for out, y in ((lo, 0), (hi, CY - 1)):
            for base, v in ((Z_C, c), (Z_P, second[x]), (Z_W, cw)):
                k = base + x + 3
                out[k : k + 1, :] = v[y : y + 1]
    for x in range(-2, 6):
        s, c, cw = second[x], a.first(x), a.w(x)
        below, above = shift_y(s, 0.0, 0.0)
        inner = {0: above, 1: below}
        for side, (out, y, y2) in enumerate(((lo, 0, 1), (hi, CY - 1, CY - 2))):
            k = Z_Q + x + 2
            out[k : k + 1, :] = (c + cw * inner[side])[y : y + 1]
        if -1 <= x <= 4:
            part = KEEP * s + c + cw * (second[x - 1] + second[x + 1] + beside_z(s))
            for side, (out, y, y2) in enumerate(((lo, 0, 1), (hi, CY - 1, CY - 2))):
                k = Z_R + x + 1
                out[k : k + 1, :] = (part + cw * inner[side])[y2 : y2 + 1]
                k = Z_V + x + 1
                out[k : k + 1, :] = cw[y2 : y2 + 1]
    for out, y, inner in ((lo, 0, 1), (hi, BY - 1, BY - 2)):
        for x in range(BX):
            at = (x + 1) * BY
            v = fine.w(x, y) * (fine.rhs(x, y) + row(f2, at + inner))
            for half in range(2):
                k = Z_S + 2 * x + half
                out[k : k + 1, :] = v[:, half * CZ : (half + 1) * CZ]
        for j, x in enumerate((-1, 8)):
            at = (x + 1) * BY + y
            v = f2[at : at + 1, :]
            for half in range(2):
                k = Z_K + 2 * j + half
                out[k : k + 1, :] = v[:, half * CZ : (half + 1) * CZ]
    p = side_of_dev()
    even[...] = sides[1 - p]
    even2[...] = sides[1 - p]
    odd[...] = sides[p]


def last_kernel(
    g, b, w, left, chip, both, f2, f2low, f2high, c1x, wc, cleft, cchip, c2z, even1, odd, even2,
    out, cboth, col, line, line3, corr, col2, s1, gline, g1line,
):
    wide = Wide(g, b, w, left, chip)
    a = Coarse(c1x, wc, cleft, partner(cchip))
    take(cboth, even1[...] + even2[...], odd[...])
    low, high, clow, chigh = both.at[0], both.at[1], cboth.at[0], cboth.at[1]
    crow = lax.broadcasted_iota(jnp.int32, (CY, CZ), 0)
    c2 = {}
    for x in range(-3, 7):
        k = Z_C + x + 3
        beyond = jnp.where(crow == 0, row(clow, k), jnp.where(crow == CY - 1, row(chigh, k), 0.0))
        c2[x] = slab(c2z, x + 3, CY) + a.w(x) * beyond
    sides = ((clow, 0), (chigh, CY - 1))
    for s, (side, y) in enumerate(sides):
        for x in range(-3, 7):
            col[x + 3 : x + 4, :] = a.first(x)[y : y + 1]
        line[s, 0:10, :] = side[Z_P : Z_P + 10, :] + side[Z_W : Z_W + 10, :] * col[0:10, :]
        for x in range(-2, 6):
            col[x + 2 : x + 3, :] = c2[x][y : y + 1]
        mid = line[s, 1:9, :]
        line3[s, 0:8, :] = (
            KEEP * mid
            + side[Z_Q : Z_Q + 8, :]
            + side[Z_W + 1 : Z_W + 9, :]
            * (line[s, 0:8, :] + line[s, 2:10, :] + beside_z(mid) + col[0:8, :])
        )
    c3 = {}
    for x in range(-2, 6):
        c = c2[x]
        c3[x] = KEEP * c + a.first(x) + a.w(x) * (
            c2[x - 1]
            + c2[x + 1]
            + beside_z(c)
            + beside_y(c, line[0, x + 3 : x + 4, :], line[1, x + 3 : x + 4, :])
        )
    for x in range(-1, 5):
        c = c3[x]
        c4 = KEEP * c + a.first(x) + a.w(x) * (
            c3[x - 1]
            + c3[x + 1]
            + beside_z(c)
            + beside_y(c, line3[0, x + 2 : x + 3, :], line3[1, x + 2 : x + 3, :])
        )
        for half, v in enumerate(spread_z(c4)):
            corr[half, pl.ds((x + 1) * BY, CY, stride=2), :] = v
            corr[half, pl.ds((x + 1) * BY + 1, CY, stride=2), :] = v
    for s, (side, y) in enumerate(sides):
        for x in range(-1, 5):
            col[x + 1 : x + 2, :] = c3[x][y : y + 1]
        mid = line3[s, 1:7, :]
        third = side[Z_R : Z_R + 6, :] + side[Z_V : Z_V + 6, :] * line[s, 2:8, :]
        fourth = (
            KEEP * mid
            + side[Z_C + 2 : Z_C + 8, :]
            + side[Z_W + 2 : Z_W + 8, :]
            * (line3[s, 0:6, :] + line3[s, 2:8, :] + beside_z(mid) + third + col[0:6, :])
        )
        for half, v in enumerate(spread_z(fourth)):
            corr[half, 6 * BY + 8 * s : 6 * BY + 8 * s + 6, :] = v

    def corr_at(k, n):
        return jnp.concatenate([corr[0, k : k + n, :], corr[1, k : k + n, :]], axis=1)

    g0 = {}
    for x in range(-2, 10):
        if x == -2:
            f = slab(cleft, 2)
        elif x == 9:
            f = slab(a.right, 2)
        else:
            f = slab(f2, x + 1)
        g0[x] = f + corr_at((x + 2) // 2 * BY, BY)
    for s, (cside, side, y, f2side) in enumerate(((clow, low, 0, f2low), (chigh, high, BY - 1, f2high))):
        base = 6 * BY + 8 * s
        for x in range(-1, 9):
            k = base + (x + 2) // 2
            col2[x + 1 : x + 2, :] = corr_at(k, 1)
        gline[s, 1:9, :] = f2side[...] + col2[1:9, :]
        for j, x in enumerate((-1, 8)):
            k = Z_K + 2 * j
            gline[s, x + 1 : x + 2, 0:CZ] = row(cside, k) + col2[x + 1 : x + 2, 0:CZ]
            gline[s, x + 1 : x + 2, CZ:] = row(cside, k + 1) + col2[x + 1 : x + 2, CZ:]
        for x in range(BX):
            k = Z_S + 2 * x
            s1[x : x + 1, 0:CZ] = row(cside, k)
            s1[x : x + 1, CZ:] = row(cside, k + 1)
        moved = col2[1:9, :]
        for x in range(BX):
            col2[x : x + 1, :] = g0[x][y : y + 1]
        mid = gline[s, 1:9, :]
        g1line[s, 0:8, :] = (
            KEEP * mid
            + s1[0:8, :]
            + side[Y_W : Y_W + 8, :]
            * (moved + gline[s, 0:8, :] + gline[s, 2:10, :] + beside_z(mid) + col2[0:8, :])
        )
    g1 = {}
    for x in range(-1, 9):
        f = g0[x]
        g1[x] = KEEP * f + wide.w(x) * (
            wide.rhs(x)
            + g0[x - 1]
            + g0[x + 1]
            + beside_z(f)
            + beside_y(f, gline[0, x + 1 : x + 2, :], gline[1, x + 1 : x + 2, :])
        )
    for x in range(BX):
        f = g1[x]
        out[place(x)] = KEEP * f + wide.w(x) * (
            wide.rhs(x)
            + g1[x - 1]
            + g1[x + 1]
            + beside_z(f)
            + beside_y(f, g1line[0, x : x + 1, :], g1line[1, x : x + 1, :])
        )


def send(v, links):
    n = lax.axis_size("dev")
    return lax.ppermute(v, ("group", "dev"), [(i * n + j, k * n + l) for (i, j), (k, l) in links])


def back(links):
    return [(j, i) for i, j in links]


def swap(v, pairs):
    return send(v, pairs + back(pairs))


def share_chip(v):
    groups = [[i, i + 1] for i in range(0, lax.axis_size("group"), 2)]
    return lax.all_gather(v, "group", axis_index_groups=groups)


def cross_pairs(keep):
    devs = [d for d in range(lax.axis_size("dev")) if keep(d)]
    return [((i, d), (i + 1, d)) for i in range(1, lax.axis_size("group") - 1, 2) for d in devs]


def dev_pairs(start, keep):
    devs = [d for d in range(start, lax.axis_size("dev") - 1, 2) if keep(d)]
    return [((i, d), (i, d + 1)) for i in range(lax.axis_size("group")) for d in devs]


def is_start(d):
    return d % RUN == 0


def in_middle(d):
    return not (is_start(d) or before_end(d))


def is_end(d):
    return d % RUN == RUN - 1


def before_end(d):
    return d % RUN == RUN - 2


def body(g, b, n):
    block = (BX, BY, NZ)
    cross, cross2, chip, even, odd, f1z, g, b, w, d = call(
        load_kernel,
        [(X_ROWS, NZ)] * 3 + [(Y_ROWS, NZ)] * 2 + [(BX * BY, NZ)] + [block] * 4,
        g, b, n,
        hbm=3,
        vmem=None,
        scratch=[pltpu.VMEM(block, jnp.int32), (2, Y_ROWS, NZ), pltpu.SemaphoreType.DMA((3,))],
    )
    cross1 = swap(cross, cross_pairs(lambda d: not is_end(d)))
    even1 = swap(even, dev_pairs(0, lambda d: not before_end(d)))
    odd1 = swap(odd, dev_pairs(1, lambda d: not before_end(d + 1)))
    cross2 = swap(cross2, cross_pairs(is_end))
    even2, odd2, chip = call(again_kernel, [(Y_ROWS, NZ)] * 2 + [(X_ROWS, NZ)], even, odd, chip, even1)
    even2 = swap(even2, dev_pairs(0, before_end))
    odd2 = swap(odd2, dev_pairs(1, lambda d: before_end(d + 1)))
    chip = share_chip(chip)
    left, both = call(
        gather_kernel,
        [(X_ROWS, NZ), (2, Y_ROWS, NZ)],
        cross1, even1, odd1,
        cost=pl.CostEstimate(flops=2**34, bytes_accessed=0, transcendentals=0),
    )
    f2, f2low, f2high, c1, wc, left, both, cross, near = call(
        middle_kernel,
        [(10 * BY, NZ), (BX, NZ), (BX, NZ), (CX * CY, CZ), (CX * CY, CZ), (X_ROWS, NZ), (2, Y_ROWS, NZ)] + [(X2_ROWS, NZ)] * 2,
        g, b, w, d, left, cross2, chip, f1z, both, even2, odd2,
        scratch=[(16, NZ), (2, 16, NZ), (4, CX * BY, CZ)],
    )
    cleft = swap(cross, cross_pairs(lambda d: True))
    cchip = share_chip(near)
    even, even2, odd, f2, f2low, f2high, c1x, c2z = call(
        pack_c_kernel,
        [(Z_ROWS, CZ)] * 3 + [(10 * BY, NZ), (BX, NZ), (BX, NZ), (3 * CX * CY, CZ), (10 * CY, CZ)],
        g, b, w, left, chip, both, f2, f2low, f2high, c1, wc, cleft, cchip,
        scratch=[(13, 8, NZ), (5, 8, NZ), (8, CZ), (2, Z_ROWS, CZ)],
    )
    inner, start, end = (dev_pairs(0, keep) for keep in (in_middle, is_start, before_end))
    even1 = send(even, inner + back(inner) + back(start))
    odd = swap(odd, dev_pairs(1, lambda d: True))
    even2 = send(even2, end + back(end) + start)
    (out,) = call(
        last_kernel,
        [block],
        g, b, w, left, chip, both, f2, f2low, f2high, c1x, wc, cleft, cchip, c2z, even1, odd, even2,
        scratch=[
            (2, Z_ROWS, CZ),
            (16, CZ), (2, 16, CZ), (2, 8, CZ), (2, 6 * BY + 16, CZ), (16, NZ), (8, NZ), (2, 16, NZ), (2, 8, NZ),
        ],
        hbm_out=True,
    )
    return out


def solution(mesh):
    s = P("group", "dev", None)
    return jax.shard_map(body, mesh=mesh, in_specs=(s, s, s), out_specs=s, check_vma=False)
```

```python
import jax
import jax.numpy as jnp
from jax import lax
from jax.sharding import PartitionSpec as P
from jax.experimental import pallas as pl
from jax.experimental.pallas import tpu as pltpu

OMEGA = 0.8
KEEP = 1.0 - OMEGA
VM = pl.BlockSpec(memory_space=pltpu.VMEM)
F32 = jnp.float32
BX, BY, NZ = 8, 16, 256
CX, CY, CZ = 4, 8, 128
RUN = 32


def call(kernel, outs, *args, scratch=(), hbm=0, hbm_out=False, vmem=8 * 2**20, cost=None):
    make = jax.ShapeDtypeStruct if hbm_out else pltpu.VMEM
    return pl.pallas_call(
        kernel,
        out_shape=[make(s, F32) for s in outs],
        in_specs=[pl.BlockSpec(memory_space=pltpu.HBM)] * hbm + [VM] * (len(args) - hbm),
        out_specs=[VM] * len(outs),
        scratch_shapes=[pltpu.VMEM(s, F32) if isinstance(s, tuple) else s for s in scratch],
        compiler_params=pltpu.CompilerParams(vmem_limit_bytes=vmem),
        cost_estimate=cost,
    )(*args)


def beside_z(v):
    lane = lax.broadcasted_iota(jnp.int32, v.shape, 1)
    last = v.shape[1] - 1
    below = jnp.where(lane == 0, 0.0, pltpu.roll(v, 1, 1))
    above = jnp.where(lane == last, 0.0, pltpu.roll(v, last, 1))
    return below + above


def shift_y(v, low, high):
    row = lax.broadcasted_iota(jnp.int32, v.shape, 0)
    last = v.shape[0] - 1
    below = jnp.where(row == 0, low, pltpu.roll(v, 1, 0))
    above = jnp.where(row == last, high, pltpu.roll(v, last, 0))
    return below, above


def beside_y(v, low, high):
    below, above = shift_y(v, low, high)
    return below + above


def slab(ref, k, rows=BY):
    return ref[k * rows : (k + 1) * rows, :]


def by_row(n, rows):
    total = 0.0
    for k, v in rows.items():
        at = lax.broadcasted_iota(jnp.int32, (n, v.shape[1]), 0)
        total = jnp.where(at == k, v, total)
    return total


def row(ref, k):
    return ref[k : k + 1, :]


def lanes(v, index):
    return jnp.take_along_axis(v, index, axis=1)


def pair_z(low, high):
    lane = lax.broadcasted_iota(jnp.int32, low.shape, 1)
    index = (2 * lane) % CZ
    first = jnp.where(lane < CZ // 2, lanes(low, index), lanes(high, index))
    second = jnp.where(lane < CZ // 2, lanes(low, index + 1), lanes(high, index + 1))
    return first + second


def spread_z(v):
    half = lax.broadcasted_iota(jnp.int32, v.shape, 1) // 2
    return lanes(v, half), lanes(v, half + CZ // 2)


def diag_of(n):
    return 6.0 + 0.25 * n.astype(F32)


def place(x):
    odd = lax.axis_index("group") % 2
    return x + odd * (BX - 1 - 2 * x)


def partner(ref):
    return ref.at[1 - lax.axis_index("group") % 2]


def side_of_dev():
    return lax.axis_index("dev") % 2


Y_G, Y_P, Y_W, Y_Q, Y_G2, Y_W2 = 0, 8, 16, 24, 32, 34
Y_ROWS = 40
X_W = 7 * BY
X_ROWS = X_W + 2 * CY


def tile(base, k):
    return slice(base + k // 2 * CY, base + (k // 2 + 1) * CY), slice(k % 2 * CZ, (k % 2 + 1) * CZ)


def load_kernel(
    g_hbm, b_hbm, n_hbm, cross, cross2, chip, even, odd, f1z, g, b, w, d, wc, n, both, sums, sems
):
    copies = [
        pltpu.make_async_copy(src, dst, sems.at[k])
        for k, (src, dst) in enumerate(((g_hbm, g), (b_hbm, b), (n_hbm, n)))
    ]
    for c in copies:
        c.start()
    for c in copies:
        c.wait()
    for x in range(BX):
        diag = diag_of(n[x])
        d[x] = diag
        w[x] = OMEGA / diag
    for out, layers in ((cross, (0, 1, 2)), (chip, (7, 6, 5))):
        for k in range(3):
            out[k * BY : (k + 1) * BY, :] = g[place(layers[k])]
        for k in range(2):
            out[(3 + k) * BY : (4 + k) * BY, :] = w[place(layers[k])]
            out[(5 + k) * BY : (6 + k) * BY, :] = b[place(layers[k])]
    for k in range(CX):
        points = d[place(2 * k)] + d[place(2 * k + 1)]
        for half in range(2):
            sums[half, k * BY : (k + 1) * BY, :] = points[:, half * CZ : (half + 1) * CZ]
    halves = [sums[k, pl.ds(0, CX * CY, stride=2), :] + sums[k, pl.ds(1, CX * CY, stride=2), :] for k in range(2)]
    weight = OMEGA / (0.5 * pair_z(*halves) - 18.0)
    wc[...] = weight
    for k in range(CX):
        v = weight[k * CY : (k + 1) * CY]
        cross[tile(X_W, k)] = v
        chip[tile(X_W, CX - 1 - k)] = v
    zero = jnp.zeros((BY, NZ), F32)
    for x in range(BX):
        at = place(x)
        here, wx, bx = g[at], w[at], b[at]
        before = g[place(x - 1)] if x else zero
        after = g[place(x + 1)] if x < BX - 1 else zero
        f = KEEP * here + wx * (bx + before + after + beside_z(here) + beside_y(here, 0.0, 0.0))
        f1z[x * BY : (x + 1) * BY, :] = f
        for s, (y, inner) in enumerate(((0, 1), (BY - 1, BY - 2))):
            rows = [
                (Y_G + x, here[y : y + 1]),
                (Y_P + x, f[y : y + 1]),
                (Y_W + x, wx[y : y + 1]),
                (Y_Q + x, wx[y : y + 1] * (bx[y : y + 1] + f[inner : inner + 1])),
            ]
            if x in (0, 7):
                rows += [(Y_G2 + x // 7, here[inner : inner + 1]), (Y_W2 + x // 7, wx[inner : inner + 1])]
            for k, v in rows:
                both[s, k : k + 1, :] = v
    p = side_of_dev()
    even[...] = both[1 - p]
    odd[...] = both[p]
    cross2[...] = cross[...]


class Wide:
    def __init__(self, g, b, w, left, right):
        self.own, self.left, self.right = (g, w, b), left, partner(right)

    def _get(self, which, base, x, y):
        if 0 <= x < BX:
            v = self.own[which]
            return v[place(x)] if y is None else v[place(x), y : y + 1, :]
        ref, k = (self.left, -1 - x) if x < 0 else (self.right, x - BX)
        return slab(ref, base + k) if y is None else row(ref, (base + k) * BY + y)

    def guess(self, x, y=None):
        return self._get(0, 0, x, y)

    def w(self, x, y=None):
        return self._get(1, 3, x, y)

    def rhs(self, x, y=None):
        return self._get(2, 5, x, y)


def take(both, even, odd):
    p = side_of_dev()
    both[1 - p] = even
    both[p] = odd


def again_kernel(even, odd, chip, met, even2, odd2, chip2):
    chip2[...] = chip[...]
    even2[...] = even[...]
    odd2[...] = odd[...]


def gather_kernel(cross, even, odd, left, both):
    left[...] = cross[...]
    take(both, even[...], odd[...])


X2_D = 2 * BY
X2_ROWS = X2_D + 16


def diagonal_rows(edge):
    at, inner = (0, 1) if edge == 0 else (7, 6)
    return (Y_G + at, Y_G2 + edge, Y_G + inner, Y_P + at, Y_W + at, Y_W2 + edge, Y_W + inner)


def middle_kernel(
    g, b, w, d, wc, left1, cross2, chip, f1z, both1, even2, odd2,
    f2, f2low, f2high, c1, left, both, lo, hi, col, line, sums,
):
    left[...] = left1[...] + cross2[...]
    a = Wide(g, b, w, left, chip)
    p = side_of_dev()
    both[p] = both1[p] + odd2[...]
    both[1 - p] = both1[1 - p] + even2[...]
    low, high = both.at[0], both.at[1]
    rows = lax.broadcasted_iota(jnp.int32, (BY, NZ), 0)
    f1 = {}
    for x in range(-2, 10):
        if 0 <= x < BX:
            k = Y_G + x
            beyond = jnp.where(rows == 0, row(low, k), jnp.where(rows == BY - 1, row(high, k), 0.0))
            if x == 0:
                beyond = beyond + a.guess(-1)
            if x == BX - 1:
                beyond = beyond + a.guess(BX)
            f1[x] = slab(f1z, x) + a.w(x) * beyond
        else:
            here = a.guess(x)
            f1[x] = KEEP * here + a.w(x) * (
                a.rhs(x) + a.guess(x - 1) + a.guess(x + 1) + beside_z(here) + beside_y(here, 0.0, 0.0)
            )
    for s, (side, y, out) in enumerate(((low, 0, f2low), (high, BY - 1, f2high))):
        for x in range(BX):
            col[x : x + 1, :] = a.guess(x, y)
        line[s, 0:16, :] = jnp.zeros((16, NZ), F32)
        line[s, 1:9, :] = side[Y_P : Y_P + 8, :] + side[Y_W : Y_W + 8, :] * col[0:8, :]
        for x in range(BX):
            col[x : x + 1, :] = f1[x][y : y + 1]
        mid = line[s, 1:9, :]
        out[...] = (
            KEEP * mid
            + side[Y_Q : Y_Q + 8, :]
            + side[Y_W : Y_W + 8, :] * (line[s, 0:8, :] + line[s, 2:10, :] + beside_z(mid) + col[0:8, :])
        )
        for edge, pack in enumerate((lo, hi)):
            for k, r in enumerate(diagonal_rows(edge)):
                at = X2_D + 7 * s + k
                pack[at : at + 1, :] = row(side, r)
    for pack in (lo, hi):
        pack[X2_D + 14 :, :] = jnp.zeros((2, NZ), F32)
    sec = {}
    for x in range(-1, 9):
        f = f1[x]
        sec[x] = KEEP * f + a.w(x) * (
            a.rhs(x)
            + f1[x - 1]
            + f1[x + 1]
            + beside_z(f)
            + beside_y(f, line[0, x + 1 : x + 2, :], line[1, x + 1 : x + 2, :])
        )
        f2[(x + 1) * BY : (x + 2) * BY, :] = sec[x]
    lo[BY:X2_D, :] = sec[1]
    hi[BY:X2_D, :] = sec[6]
    for x in range(0, 8):
        f = sec[x]
        r = (
            a.rhs(x)
            - d[place(x)] * f
            + sec[x - 1]
            + sec[x + 1]
            + beside_z(f)
            + beside_y(f, row(f2low, x), row(f2high, x))
        )
        if x % 2:
            pairs = pairs + r
            at = (x // 2) * BY
            for half in range(2):
                sums[half, at : at + BY, :] = pairs[:, half * CZ : (half + 1) * CZ]
        else:
            pairs = r
    halves = [sums[k, pl.ds(0, CX * CY, stride=2), :] + sums[k, pl.ds(1, CX * CY, stride=2), :] for k in range(2)]
    first = wc[...] * (0.5 * pair_z(*halves))
    c1[...] = first
    for x in range(CX):
        v = first[x * CY : (x + 1) * CY]
        lo[tile(0, x)] = v
        hi[tile(0, CX - 1 - x)] = v


class Coarse:
    def __init__(self, c1x, wc, left, right):
        self.c1x, self.wc, self.left, self.right = c1x, wc, left, right

    def first(self, x):
        return slab(self.c1x, x + CX, CY)

    def w(self, x):
        if 0 <= x < CX:
            return slab(self.wc, x, CY)
        ref, k = (self.left, -1 - x) if x < 0 else (self.right, x - CX)
        return ref[tile(X_W, k)]


def corner_terms(a, low, high, relays, put):
    for e, (xe, xi, xn, xm) in enumerate(((0, 1, -1, -2), (7, 6, 8, 9))):
        for s, (side, y, yi) in enumerate(((low, 0, 1), (high, BY - 1, BY - 2))):
            own = [row(side, r) for r in diagonal_rows(e)]
            far = [row(relays[e], X2_D + 7 * s + k) for k in range(7)]
            corner, beside = a.guess(xe, y), a.guess(xn, y)
            w_corner, w_beside = a.w(xe, y), a.w(xn, y)
            put(2 * e + s, far[:5] + [beside + own[0], w_beside, a.w(xm, y), a.w(xn, yi), own[4], own[5], own[6], w_corner])
            put(4 + 2 * e + s, own[:5] + [corner + far[0], w_corner, a.w(xi, y), a.w(xe, yi), far[4], far[5], far[6], w_beside])


def corner_sums(t):
    g1, g2, g3, part, wd, near, wx, wx2, wxs, wy, wy2, wys, wq = (t[k] for k in range(13))
    dq = jnp.where(wq > 0.0, OMEGA / jnp.where(wq > 0.0, wq, 1.0), 0.0)
    by_y = wy * g1
    by_x = wx * g1
    diagonal = part + wd * near
    at_q = wq * (by_x + by_y)
    at_y = KEEP * by_y + wy * (beside_z(by_y) + diagonal + wy2 * g2)
    at_x = KEEP * by_x + wx * (beside_z(by_x) + diagonal + wx2 * g3)
    at_ys = wys * by_y
    at_xs = wxs * by_x
    total = at_y + at_x + beside_z(at_q) - dq * at_q + 2.0 * at_q + at_ys + at_xs
    return at_q, at_y, at_x, at_ys, at_xs, 0.5 * pair_z(total[:, :CZ], total[:, CZ:])


Z_C, Z_P, Z_W, Z_Q, Z_R, Z_V, Z_S, Z_K = 0, 10, 20, 30, 38, 44, 50, 66
Z_ROWS = 72


def pack_c_kernel(
    g, b, w, left, chip, both, f2in, f2lowin, f2highin, c1, wc, cleft, cchip,
    even, even2, odd, f2, f2low, f2high, c1x, c2z, table, terms, rows, sides,
):
    fine = Wide(g, b, w, left, chip)
    cright = partner(cchip)

    def put(i, values):
        for k, v in enumerate(values):
            table[k, i : i + 1, :] = v

    corner_terms(fine, both.at[0], both.at[1], (cleft, cright), put)
    *parts, share = corner_sums(table)
    for k, v in enumerate(parts):
        terms[k] = v
    rows[...] = share
    a = Coarse(c1x, wc, fine.left, fine.right)
    for x in range(1, CX):
        c1x[(CX - 1 - x) * CY : (CX - x) * CY, :] = cleft[tile(0, x)]
        c1x[(x + 2 * CX) * CY : (x + 2 * CX + 1) * CY, :] = cright[tile(0, x)]
    for x in range(1, CX - 1):
        c1x[(x + CX) * CY : (x + CX + 1) * CY, :] = slab(c1, x, CY)
    term = lambda k, e, s: terms[k, 2 * e + s : 2 * e + s + 1, :]
    for e, (xe, xn, cxe, cxn) in enumerate(((0, -1, 0, -1), (7, 8, 3, 4))):
        at = (xe + 1) * BY
        f2[at : at + BY, :] = f2in[at : at + BY, :] + by_row(BY, {0: term(0, e, 0), BY - 1: term(0, e, 1)})
        at = (xn + 1) * BY
        f2[at : at + BY, :] = f2in[at : at + BY, :] + by_row(
            BY, {0: term(2, e, 0), 1: term(4, e, 0), BY - 2: term(4, e, 1), BY - 1: term(2, e, 1)}
        )
        for i, cx in ((2 * e, cxe), (2 * e + 4, cxn)):
            at = (cx + CX) * CY
            given = slab(c1, cx, CY) if 0 <= cx < CX else (cleft if cx < 0 else cright)[tile(0, 0)]
            c1x[at : at + CY, :] = given + a.w(cx) * by_row(CY, {0: row(rows, i), CY - 1: row(rows, i + 1)})
    f2[2 * BY : 8 * BY, :] = f2in[2 * BY : 8 * BY, :]
    for s, (side, sidein) in enumerate(((f2low, f2lowin), (f2high, f2highin))):
        side[...] = sidein[...] + by_row(
            BX, {0: term(1, 0, s), 1: term(3, 0, s), BX - 2: term(3, 1, s), BX - 1: term(1, 1, s)}
        )
    lo, hi = sides.at[0], sides.at[1]
    second = {}
    for x in range(-3, 7):
        c, cw = a.first(x), a.w(x)
        second[x] = (1.0 + KEEP) * c + cw * (
            a.first(x - 1) + a.first(x + 1) + beside_z(c) + beside_y(c, 0.0, 0.0)
        )
        c2z[(x + 3) * CY : (x + 4) * CY, :] = second[x]
        for out, y in ((lo, 0), (hi, CY - 1)):
            for base, v in ((Z_C, c), (Z_P, second[x]), (Z_W, cw)):
                k = base + x + 3
                out[k : k + 1, :] = v[y : y + 1]
    for x in range(-2, 6):
        s, c, cw = second[x], a.first(x), a.w(x)
        below, above = shift_y(s, 0.0, 0.0)
        inner = {0: above, 1: below}
        for side, (out, y, y2) in enumerate(((lo, 0, 1), (hi, CY - 1, CY - 2))):
            k = Z_Q + x + 2
            out[k : k + 1, :] = (c + cw * inner[side])[y : y + 1]
        if -1 <= x <= 4:
            part = KEEP * s + c + cw * (second[x - 1] + second[x + 1] + beside_z(s))
            for side, (out, y, y2) in enumerate(((lo, 0, 1), (hi, CY - 1, CY - 2))):
                k = Z_R + x + 1
                out[k : k + 1, :] = (part + cw * inner[side])[y2 : y2 + 1]
                k = Z_V + x + 1
                out[k : k + 1, :] = cw[y2 : y2 + 1]
    for out, y, inner in ((lo, 0, 1), (hi, BY - 1, BY - 2)):
        for x in range(BX):
            at = (x + 1) * BY
            v = fine.w(x, y) * (fine.rhs(x, y) + row(f2, at + inner))
            for half in range(2):
                k = Z_S + 2 * x + half
                out[k : k + 1, :] = v[:, half * CZ : (half + 1) * CZ]
        for j, x in enumerate((-1, 8)):
            at = (x + 1) * BY + y
            v = f2[at : at + 1, :]
            for half in range(2):
                k = Z_K + 2 * j + half
                out[k : k + 1, :] = v[:, half * CZ : (half + 1) * CZ]
    p = side_of_dev()
    even[...] = sides[1 - p]
    even2[...] = sides[1 - p]
    odd[...] = sides[p]


def last_kernel(
    g, b, w, left, chip, both, f2, f2low, f2high, c1x, wc, cleft, cchip, c2z, even1, odd, even2,
    out, cboth, col, line, line3, corr, col2, s1, gline, g1line,
):
    wide = Wide(g, b, w, left, chip)
    a = Coarse(c1x, wc, wide.left, wide.right)
    cright = partner(cchip)
    take(cboth, even1[...] + even2[...], odd[...])
    low, high, clow, chigh = both.at[0], both.at[1], cboth.at[0], cboth.at[1]
    crow = lax.broadcasted_iota(jnp.int32, (CY, CZ), 0)
    c2 = {}
    for x in range(-3, 7):
        k = Z_C + x + 3
        beyond = jnp.where(crow == 0, row(clow, k), jnp.where(crow == CY - 1, row(chigh, k), 0.0))
        c2[x] = slab(c2z, x + 3, CY) + a.w(x) * beyond
    sides = ((clow, 0), (chigh, CY - 1))
    for s, (side, y) in enumerate(sides):
        for x in range(-3, 7):
            col[x + 3 : x + 4, :] = a.first(x)[y : y + 1]
        line[s, 0:10, :] = side[Z_P : Z_P + 10, :] + side[Z_W : Z_W + 10, :] * col[0:10, :]
        for x in range(-2, 6):
            col[x + 2 : x + 3, :] = c2[x][y : y + 1]
        mid = line[s, 1:9, :]
        line3[s, 0:8, :] = (
            KEEP * mid
            + side[Z_Q : Z_Q + 8, :]
            + side[Z_W + 1 : Z_W + 9, :]
            * (line[s, 0:8, :] + line[s, 2:10, :] + beside_z(mid) + col[0:8, :])
        )
    c3 = {}
    for x in range(-2, 6):
        c = c2[x]
        c3[x] = KEEP * c + a.first(x) + a.w(x) * (
            c2[x - 1]
            + c2[x + 1]
            + beside_z(c)
            + beside_y(c, line[0, x + 3 : x + 4, :], line[1, x + 3 : x + 4, :])
        )
    for x in range(-1, 5):
        c = c3[x]
        c4 = KEEP * c + a.first(x) + a.w(x) * (
            c3[x - 1]
            + c3[x + 1]
            + beside_z(c)
            + beside_y(c, line3[0, x + 2 : x + 3, :], line3[1, x + 2 : x + 3, :])
        )
        for half, v in enumerate(spread_z(c4)):
            corr[half, pl.ds((x + 1) * BY, CY, stride=2), :] = v
            corr[half, pl.ds((x + 1) * BY + 1, CY, stride=2), :] = v
    for s, (side, y) in enumerate(sides):
        for x in range(-1, 5):
            col[x + 1 : x + 2, :] = c3[x][y : y + 1]
        mid = line3[s, 1:7, :]
        third = side[Z_R : Z_R + 6, :] + side[Z_V : Z_V + 6, :] * line[s, 2:8, :]
        fourth = (
            KEEP * mid
            + side[Z_C + 2 : Z_C + 8, :]
            + side[Z_W + 2 : Z_W + 8, :]
            * (line3[s, 0:6, :] + line3[s, 2:8, :] + beside_z(mid) + third + col[0:6, :])
        )
        for half, v in enumerate(spread_z(fourth)):
            corr[half, 6 * BY + 8 * s : 6 * BY + 8 * s + 6, :] = v

    def corr_at(k, n):
        return jnp.concatenate([corr[0, k : k + n, :], corr[1, k : k + n, :]], axis=1)

    g0 = {}
    for x in range(-2, 10):
        if x == -2:
            f = slab(cleft, 1)
        elif x == 9:
            f = slab(cright, 1)
        else:
            f = slab(f2, x + 1)
        g0[x] = f + corr_at((x + 2) // 2 * BY, BY)
    for s, (cside, side, y, f2side) in enumerate(((clow, low, 0, f2low), (chigh, high, BY - 1, f2high))):
        base = 6 * BY + 8 * s
        for x in range(-1, 9):
            k = base + (x + 2) // 2
            col2[x + 1 : x + 2, :] = corr_at(k, 1)
        gline[s, 1:9, :] = f2side[...] + col2[1:9, :]
        for j, x in enumerate((-1, 8)):
            k = Z_K + 2 * j
            gline[s, x + 1 : x + 2, 0:CZ] = row(cside, k) + col2[x + 1 : x + 2, 0:CZ]
            gline[s, x + 1 : x + 2, CZ:] = row(cside, k + 1) + col2[x + 1 : x + 2, CZ:]
        for x in range(BX):
            k = Z_S + 2 * x
            s1[x : x + 1, 0:CZ] = row(cside, k)
            s1[x : x + 1, CZ:] = row(cside, k + 1)
        moved = col2[1:9, :]
        for x in range(BX):
            col2[x : x + 1, :] = g0[x][y : y + 1]
        mid = gline[s, 1:9, :]
        g1line[s, 0:8, :] = (
            KEEP * mid
            + s1[0:8, :]
            + side[Y_W : Y_W + 8, :]
            * (moved + gline[s, 0:8, :] + gline[s, 2:10, :] + beside_z(mid) + col2[0:8, :])
        )
    g1 = {}
    for x in range(-1, 9):
        f = g0[x]
        g1[x] = KEEP * f + wide.w(x) * (
            wide.rhs(x)
            + g0[x - 1]
            + g0[x + 1]
            + beside_z(f)
            + beside_y(f, gline[0, x + 1 : x + 2, :], gline[1, x + 1 : x + 2, :])
        )
    for x in range(BX):
        f = g1[x]
        out[place(x)] = KEEP * f + wide.w(x) * (
            wide.rhs(x)
            + g1[x - 1]
            + g1[x + 1]
            + beside_z(f)
            + beside_y(f, g1line[0, x : x + 1, :], g1line[1, x : x + 1, :])
        )


def swap(v, pairs):
    n = lax.axis_size("dev")
    links = [(i * n + j, k * n + l) for (i, j), (k, l) in pairs]
    return lax.ppermute(v, ("group", "dev"), links + [(j, i) for i, j in links])


def share_chip(v):
    groups = [[i, i + 1] for i in range(0, lax.axis_size("group"), 2)]
    return lax.all_gather(v, "group", axis_index_groups=groups)


def cross_pairs(keep):
    devs = [d for d in range(lax.axis_size("dev")) if keep(d)]
    return [((i, d), (i + 1, d)) for i in range(1, lax.axis_size("group") - 1, 2) for d in devs]


def dev_pairs(start, keep):
    devs = [d for d in range(start, lax.axis_size("dev") - 1, 2) if keep(d)]
    return [((i, d), (i, d + 1)) for i in range(lax.axis_size("group")) for d in devs]


def is_end(d):
    return d % RUN == RUN - 1


def before_end(d):
    return d % RUN == RUN - 2


def body(g, b, n):
    block = (BX, BY, NZ)
    cross, cross2, chip, even, odd, f1z, g, b, w, d, wc = call(
        load_kernel,
        [(X_ROWS, NZ)] * 3 + [(Y_ROWS, NZ)] * 2 + [(BX * BY, NZ)] + [block] * 4 + [(CX * CY, CZ)],
        g, b, n,
        hbm=3,
        vmem=None,
        scratch=[pltpu.VMEM(block, jnp.int32), (2, Y_ROWS, NZ), (2, CX * BY, CZ), pltpu.SemaphoreType.DMA((3,))],
    )
    cross1 = swap(cross, cross_pairs(lambda d: not is_end(d)))
    even1 = swap(even, dev_pairs(0, lambda d: not before_end(d)))
    odd1 = swap(odd, dev_pairs(1, lambda d: not before_end(d + 1)))
    cross2 = swap(cross2, cross_pairs(is_end))
    even2, odd2, chip = call(again_kernel, [(Y_ROWS, NZ)] * 2 + [(X_ROWS, NZ)], even, odd, chip, even1)
    even2 = swap(even2, dev_pairs(0, before_end))
    odd2 = swap(odd2, dev_pairs(1, lambda d: before_end(d + 1)))
    chip = share_chip(chip)
    left, both = call(
        gather_kernel,
        [(X_ROWS, NZ), (2, Y_ROWS, NZ)],
        cross1, even1, odd1,
        cost=pl.CostEstimate(flops=2**34, bytes_accessed=0, transcendentals=0),
    )
    f2, f2low, f2high, c1, left, both, cross, near = call(
        middle_kernel,
        [(10 * BY, NZ), (BX, NZ), (BX, NZ), (CX * CY, CZ), (X_ROWS, NZ), (2, Y_ROWS, NZ)] + [(X2_ROWS, NZ)] * 2,
        g, b, w, d, wc, left, cross2, chip, f1z, both, even2, odd2,
        scratch=[(16, NZ), (2, 16, NZ), (2, CX * BY, CZ)],
    )
    cleft = swap(cross, cross_pairs(lambda d: True))
    cchip = share_chip(near)
    even, even2, odd, f2, f2low, f2high, c1x, c2z = call(
        pack_c_kernel,
        [(Z_ROWS, CZ)] * 3 + [(10 * BY, NZ), (BX, NZ), (BX, NZ), (3 * CX * CY, CZ), (10 * CY, CZ)],
        g, b, w, left, chip, both, f2, f2low, f2high, c1, wc, cleft, cchip,
        scratch=[(13, 8, NZ), (5, 8, NZ), (8, CZ), (2, Z_ROWS, CZ)],
    )
    even1 = swap(even, dev_pairs(0, lambda d: not before_end(d)))
    odd = swap(odd, dev_pairs(1, lambda d: True))
    even2 = swap(even2, dev_pairs(0, before_end))
    (out,) = call(
        last_kernel,
        [block],
        g, b, w, left, chip, both, f2, f2low, f2high, c1x, wc, cleft, cchip, c2z, even1, odd, even2,
        scratch=[
            (2, Z_ROWS, CZ),
            (16, CZ), (2, 16, CZ), (2, 8, CZ), (2, 6 * BY + 16, CZ), (16, NZ), (8, NZ), (2, 16, NZ), (2, 8, NZ),
        ],
        hbm_out=True,
    )
    return out


def solution(mesh):
    s = P("group", "dev", None)
    return jax.shard_map(body, mesh=mesh, in_specs=(s, s, s), out_specs=s, check_vma=False)
```

```python
import jax
import jax.numpy as jnp
from jax import lax
from jax.sharding import PartitionSpec as P
from jax.experimental import pallas as pl
from jax.experimental.pallas import tpu as pltpu

OMEGA = 0.8
KEEP = 1.0 - OMEGA
VM = pl.BlockSpec(memory_space=pltpu.VMEM)
F32 = jnp.float32
BX, BY, NZ = 8, 16, 256
CX, CY, CZ = 4, 8, 128
RUN = 32


def call(kernel, outs, *args, scratch=(), hbm=0, hbm_out=False, vmem=8 * 2**20, cost=None):
    make = jax.ShapeDtypeStruct if hbm_out else pltpu.VMEM
    return pl.pallas_call(
        kernel,
        out_shape=[make(s, F32) for s in outs],
        in_specs=[pl.BlockSpec(memory_space=pltpu.HBM)] * hbm + [VM] * (len(args) - hbm),
        out_specs=[VM] * len(outs),
        scratch_shapes=[pltpu.VMEM(s, F32) if isinstance(s, tuple) else s for s in scratch],
        compiler_params=pltpu.CompilerParams(vmem_limit_bytes=vmem),
        cost_estimate=cost,
    )(*args)


def beside_z(v):
    lane = lax.broadcasted_iota(jnp.int32, v.shape, 1)
    last = v.shape[1] - 1
    below = jnp.where(lane == 0, 0.0, pltpu.roll(v, 1, 1))
    above = jnp.where(lane == last, 0.0, pltpu.roll(v, last, 1))
    return below + above


def shift_y(v, low, high):
    row = lax.broadcasted_iota(jnp.int32, v.shape, 0)
    last = v.shape[0] - 1
    below = jnp.where(row == 0, low, pltpu.roll(v, 1, 0))
    above = jnp.where(row == last, high, pltpu.roll(v, last, 0))
    return below, above


def beside_y(v, low, high):
    below, above = shift_y(v, low, high)
    return below + above


def slab(ref, k, rows=BY):
    return ref[k * rows : (k + 1) * rows, :]


def by_row(n, rows):
    total = 0.0
    for k, v in rows.items():
        at = lax.broadcasted_iota(jnp.int32, (n, v.shape[1]), 0)
        total = jnp.where(at == k, v, total)
    return total


def row(ref, k):
    return ref[k : k + 1, :]


def lanes(v, index):
    return jnp.take_along_axis(v, index, axis=1)


def pair_z(low, high):
    lane = lax.broadcasted_iota(jnp.int32, low.shape, 1)
    index = (2 * lane) % CZ
    first = jnp.where(lane < CZ // 2, lanes(low, index), lanes(high, index))
    second = jnp.where(lane < CZ // 2, lanes(low, index + 1), lanes(high, index + 1))
    return first + second


def spread_z(v):
    half = lax.broadcasted_iota(jnp.int32, v.shape, 1) // 2
    return lanes(v, half), lanes(v, half + CZ // 2)


def diag_of(n):
    return 6.0 + 0.25 * n.astype(F32)


def place(x):
    odd = lax.axis_index("group") % 2
    return x + odd * (BX - 1 - 2 * x)


def partner(ref):
    return ref.at[1 - lax.axis_index("group") % 2]


def side_of_dev():
    return lax.axis_index("dev") % 2


Y_G, Y_P, Y_W, Y_Q, Y_G2, Y_W2 = 0, 8, 16, 24, 32, 34
Y_ROWS = 40
X_W = 7 * BY
X_ROWS = X_W + 2 * CY


def tile(base, k):
    return slice(base + k // 2 * CY, base + (k // 2 + 1) * CY), slice(k % 2 * CZ, (k % 2 + 1) * CZ)


def load_kernel(
    g_hbm, b_hbm, n_hbm, cross, cross2, chip, even, odd, f1z, g, b, w, d, wc, n, both, sums, sems
):
    copies = [
        pltpu.make_async_copy(src, dst, sems.at[k])
        for k, (src, dst) in enumerate(((g_hbm, g), (b_hbm, b), (n_hbm, n)))
    ]
    for c in copies:
        c.start()
    for c in copies:
        c.wait()
    for x in range(BX):
        diag = diag_of(n[x])
        d[x] = diag
        w[x] = OMEGA / diag
    for out, layers in ((cross, (0, 1, 2)), (chip, (7, 6, 5))):
        for k in range(3):
            out[k * BY : (k + 1) * BY, :] = g[place(layers[k])]
        for k in range(2):
            out[(3 + k) * BY : (4 + k) * BY, :] = w[place(layers[k])]
            out[(5 + k) * BY : (6 + k) * BY, :] = b[place(layers[k])]
    for k in range(CX):
        points = d[place(2 * k)] + d[place(2 * k + 1)]
        for half in range(2):
            sums[half, k * BY : (k + 1) * BY, :] = points[:, half * CZ : (half + 1) * CZ]
    halves = [sums[k, pl.ds(0, CX * CY, stride=2), :] + sums[k, pl.ds(1, CX * CY, stride=2), :] for k in range(2)]
    weight = OMEGA / (0.5 * pair_z(*halves) - 18.0)
    wc[...] = weight
    for k in range(CX):
        v = weight[k * CY : (k + 1) * CY]
        cross[tile(X_W, k)] = v
        chip[tile(X_W, CX - 1 - k)] = v
    zero = jnp.zeros((BY, NZ), F32)
    for x in range(BX):
        at = place(x)
        here, wx, bx = g[at], w[at], b[at]
        before = g[place(x - 1)] if x else zero
        after = g[place(x + 1)] if x < BX - 1 else zero
        f = KEEP * here + wx * (bx + before + after + beside_z(here) + beside_y(here, 0.0, 0.0))
        f1z[x * BY : (x + 1) * BY, :] = f
        for s, (y, inner) in enumerate(((0, 1), (BY - 1, BY - 2))):
            rows = [
                (Y_G + x, here[y : y + 1]),
                (Y_P + x, f[y : y + 1]),
                (Y_W + x, wx[y : y + 1]),
                (Y_Q + x, wx[y : y + 1] * (bx[y : y + 1] + f[inner : inner + 1])),
            ]
            if x in (0, 7):
                rows += [(Y_G2 + x // 7, here[inner : inner + 1]), (Y_W2 + x // 7, wx[inner : inner + 1])]
            for k, v in rows:
                both[s, k : k + 1, :] = v
    p = side_of_dev()
    even[...] = both[1 - p]
    odd[...] = both[p]
    cross2[...] = cross[...]


class Wide:
    def __init__(self, g, b, w, left, right):
        self.own, self.left, self.right = (g, w, b), left, partner(right)

    def _get(self, which, base, x, y):
        if 0 <= x < BX:
            v = self.own[which]
            return v[place(x)] if y is None else v[place(x), y : y + 1, :]
        ref, k = (self.left, -1 - x) if x < 0 else (self.right, x - BX)
        return slab(ref, base + k) if y is None else row(ref, (base + k) * BY + y)

    def guess(self, x, y=None):
        return self._get(0, 0, x, y)

    def w(self, x, y=None):
        return self._get(1, 3, x, y)

    def rhs(self, x, y=None):
        return self._get(2, 5, x, y)


def take(both, even, odd):
    p = side_of_dev()
    both[1 - p] = even
    both[p] = odd


def again_kernel(even, odd, chip, met, even2, odd2, chip2):
    chip2[...] = chip[...]
    even2[...] = even[...]
    odd2[...] = odd[...]


def gather_kernel(cross, even, odd, left, both):
    left[...] = cross[...]
    take(both, even[...], odd[...])


X2_D = 2 * BY
X2_ROWS = X2_D + 16


def diagonal_rows(edge):
    at, inner = (0, 1) if edge == 0 else (7, 6)
    return (Y_G + at, Y_G2 + edge, Y_G + inner, Y_P + at, Y_W + at, Y_W2 + edge, Y_W + inner)


def middle_kernel(
    g, b, w, d, wc, left1, cross2, chip, f1z, both1, even2, odd2,
    f2, f2low, f2high, c1, left, both, lo, hi, col, line, sums,
):
    left[...] = left1[...] + cross2[...]
    a = Wide(g, b, w, left, chip)
    p = side_of_dev()
    both[p] = both1[p] + odd2[...]
    both[1 - p] = both1[1 - p] + even2[...]
    low, high = both.at[0], both.at[1]
    rows = lax.broadcasted_iota(jnp.int32, (BY, NZ), 0)
    f1 = {}
    for x in range(-2, 10):
        if 0 <= x < BX:
            k = Y_G + x
            beyond = jnp.where(rows == 0, row(low, k), jnp.where(rows == BY - 1, row(high, k), 0.0))
            if x == 0:
                beyond = beyond + a.guess(-1)
            if x == BX - 1:
                beyond = beyond + a.guess(BX)
            f1[x] = slab(f1z, x) + a.w(x) * beyond
        else:
            here = a.guess(x)
            f1[x] = KEEP * here + a.w(x) * (
                a.rhs(x) + a.guess(x - 1) + a.guess(x + 1) + beside_z(here) + beside_y(here, 0.0, 0.0)
            )
    for s, (side, y, out) in enumerate(((low, 0, f2low), (high, BY - 1, f2high))):
        for x in range(BX):
            col[x : x + 1, :] = a.guess(x, y)
        line[s, 0:16, :] = jnp.zeros((16, NZ), F32)
        line[s, 1:9, :] = side[Y_P : Y_P + 8, :] + side[Y_W : Y_W + 8, :] * col[0:8, :]
        for x in range(BX):
            col[x : x + 1, :] = f1[x][y : y + 1]
        mid = line[s, 1:9, :]
        out[...] = (
            KEEP * mid
            + side[Y_Q : Y_Q + 8, :]
            + side[Y_W : Y_W + 8, :] * (line[s, 0:8, :] + line[s, 2:10, :] + beside_z(mid) + col[0:8, :])
        )
        for edge, pack in enumerate((lo, hi)):
            for k, r in enumerate(diagonal_rows(edge)):
                at = X2_D + 7 * s + k
                pack[at : at + 1, :] = row(side, r)
    for pack in (lo, hi):
        pack[X2_D + 14 :, :] = jnp.zeros((2, NZ), F32)
    sec = {}
    for x in range(-1, 9):
        f = f1[x]
        sec[x] = KEEP * f + a.w(x) * (
            a.rhs(x)
            + f1[x - 1]
            + f1[x + 1]
            + beside_z(f)
            + beside_y(f, line[0, x + 1 : x + 2, :], line[1, x + 1 : x + 2, :])
        )
        f2[(x + 1) * BY : (x + 2) * BY, :] = sec[x]
    lo[BY:X2_D, :] = sec[1]
    hi[BY:X2_D, :] = sec[6]
    for x in range(0, 8):
        f = sec[x]
        r = (
            a.rhs(x)
            - d[place(x)] * f
            + sec[x - 1]
            + sec[x + 1]
            + beside_z(f)
            + beside_y(f, row(f2low, x), row(f2high, x))
        )
        if x % 2:
            pairs = pairs + r
            at = (x // 2) * BY
            for half in range(2):
                sums[half, at : at + BY, :] = pairs[:, half * CZ : (half + 1) * CZ]
        else:
            pairs = r
    halves = [sums[k, pl.ds(0, CX * CY, stride=2), :] + sums[k, pl.ds(1, CX * CY, stride=2), :] for k in range(2)]
    first = wc[...] * (0.5 * pair_z(*halves))
    c1[...] = first
    for x in range(CX):
        v = first[x * CY : (x + 1) * CY]
        lo[tile(0, x)] = v
        hi[tile(0, CX - 1 - x)] = v


class Coarse:
    def __init__(self, c1x, wc, left, right):
        self.c1x, self.wc, self.left, self.right = c1x, wc, left, right

    def first(self, x):
        return slab(self.c1x, x + CX, CY)

    def w(self, x):
        if 0 <= x < CX:
            return slab(self.wc, x, CY)
        ref, k = (self.left, -1 - x) if x < 0 else (self.right, x - CX)
        return ref[tile(X_W, k)]


def corner_terms(a, low, high, relays, put):
    for e, (xe, xi, xn, xm) in enumerate(((0, 1, -1, -2), (7, 6, 8, 9))):
        for s, (side, y, yi) in enumerate(((low, 0, 1), (high, BY - 1, BY - 2))):
            own = [row(side, r) for r in diagonal_rows(e)]
            far = [row(relays[e], X2_D + 7 * s + k) for k in range(7)]
            corner, beside = a.guess(xe, y), a.guess(xn, y)
            w_corner, w_beside = a.w(xe, y), a.w(xn, y)
            put(2 * e + s, far[:5] + [beside + own[0], w_beside, a.w(xm, y), a.w(xn, yi), own[4], own[5], own[6], w_corner])
            put(4 + 2 * e + s, own[:5] + [corner + far[0], w_corner, a.w(xi, y), a.w(xe, yi), far[4], far[5], far[6], w_beside])


def corner_sums(t):
    g1, g2, g3, part, wd, near, wx, wx2, wxs, wy, wy2, wys, wq = (t[k] for k in range(13))
    dq = jnp.where(wq > 0.0, OMEGA / jnp.where(wq > 0.0, wq, 1.0), 0.0)
    by_y = wy * g1
    by_x = wx * g1
    diagonal = part + wd * near
    at_q = wq * (by_x + by_y)
    at_y = KEEP * by_y + wy * (beside_z(by_y) + diagonal + wy2 * g2)
    at_x = KEEP * by_x + wx * (beside_z(by_x) + diagonal + wx2 * g3)
    at_ys = wys * by_y
    at_xs = wxs * by_x
    total = at_y + at_x + beside_z(at_q) - dq * at_q + 2.0 * at_q + at_ys + at_xs
    return at_q, at_y, at_x, at_ys, at_xs, 0.5 * pair_z(total[:, :CZ], total[:, CZ:])


Z_C, Z_P, Z_W, Z_Q, Z_R, Z_V, Z_S, Z_K = 0, 10, 20, 30, 38, 44, 50, 66
Z_ROWS = 72


def pack_c_kernel(
    g, b, w, left, chip, both, f2in, f2lowin, f2highin, c1, wc, cleft, cchip,
    even, even2, odd, f2, f2low, f2high, c1x, c2z, table, terms, rows, sides,
):
    fine = Wide(g, b, w, left, chip)
    cright = partner(cchip)

    def put(i, values):
        for k, v in enumerate(values):
            table[k, i : i + 1, :] = v

    corner_terms(fine, both.at[0], both.at[1], (cleft, cright), put)
    *parts, share = corner_sums(table)
    for k, v in enumerate(parts):
        terms[k] = v
    rows[...] = share
    a = Coarse(c1x, wc, fine.left, fine.right)
    for x in range(1, CX):
        c1x[(CX - 1 - x) * CY : (CX - x) * CY, :] = cleft[tile(0, x)]
        c1x[(x + 2 * CX) * CY : (x + 2 * CX + 1) * CY, :] = cright[tile(0, x)]
    for x in range(1, CX - 1):
        c1x[(x + CX) * CY : (x + CX + 1) * CY, :] = slab(c1, x, CY)
    term = lambda k, e, s: terms[k, 2 * e + s : 2 * e + s + 1, :]
    for e, (xe, xn, cxe, cxn) in enumerate(((0, -1, 0, -1), (7, 8, 3, 4))):
        at = (xe + 1) * BY
        f2[at : at + BY, :] = f2in[at : at + BY, :] + by_row(BY, {0: term(0, e, 0), BY - 1: term(0, e, 1)})
        at = (xn + 1) * BY
        f2[at : at + BY, :] = f2in[at : at + BY, :] + by_row(
            BY, {0: term(2, e, 0), 1: term(4, e, 0), BY - 2: term(4, e, 1), BY - 1: term(2, e, 1)}
        )
        for i, cx in ((2 * e, cxe), (2 * e + 4, cxn)):
            at = (cx + CX) * CY
            given = slab(c1, cx, CY) if 0 <= cx < CX else (cleft if cx < 0 else cright)[tile(0, 0)]
            c1x[at : at + CY, :] = given + a.w(cx) * by_row(CY, {0: row(rows, i), CY - 1: row(rows, i + 1)})
    f2[2 * BY : 8 * BY, :] = f2in[2 * BY : 8 * BY, :]
    for s, (side, sidein) in enumerate(((f2low, f2lowin), (f2high, f2highin))):
        side[...] = sidein[...] + by_row(
            BX, {0: term(1, 0, s), 1: term(3, 0, s), BX - 2: term(3, 1, s), BX - 1: term(1, 1, s)}
        )
    lo, hi = sides.at[0], sides.at[1]
    second = {}
    for x in range(-3, 7):
        c, cw = a.first(x), a.w(x)
        second[x] = (1.0 + KEEP) * c + cw * (
            a.first(x - 1) + a.first(x + 1) + beside_z(c) + beside_y(c, 0.0, 0.0)
        )
        c2z[(x + 3) * CY : (x + 4) * CY, :] = second[x]
        for out, y in ((lo, 0), (hi, CY - 1)):
            for base, v in ((Z_C, c), (Z_P, second[x]), (Z_W, cw)):
                k = base + x + 3
                out[k : k + 1, :] = v[y : y + 1]
    for x in range(-2, 6):
        s, c, cw = second[x], a.first(x), a.w(x)
        below, above = shift_y(s, 0.0, 0.0)
        inner = {0: above, 1: below}
        for side, (out, y, y2) in enumerate(((lo, 0, 1), (hi, CY - 1, CY - 2))):
            k = Z_Q + x + 2
            out[k : k + 1, :] = (c + cw * inner[side])[y : y + 1]
        if -1 <= x <= 4:
            part = KEEP * s + c + cw * (second[x - 1] + second[x + 1] + beside_z(s))
            for side, (out, y, y2) in enumerate(((lo, 0, 1), (hi, CY - 1, CY - 2))):
                k = Z_R + x + 1
                out[k : k + 1, :] = (part + cw * inner[side])[y2 : y2 + 1]
                k = Z_V + x + 1
                out[k : k + 1, :] = cw[y2 : y2 + 1]
    for out, y, inner in ((lo, 0, 1), (hi, BY - 1, BY - 2)):
        for x in range(BX):
            at = (x + 1) * BY
            v = fine.w(x, y) * (fine.rhs(x, y) + row(f2, at + inner))
            for half in range(2):
                k = Z_S + 2 * x + half
                out[k : k + 1, :] = v[:, half * CZ : (half + 1) * CZ]
        for j, x in enumerate((-1, 8)):
            at = (x + 1) * BY + y
            v = f2[at : at + 1, :]
            for half in range(2):
                k = Z_K + 2 * j + half
                out[k : k + 1, :] = v[:, half * CZ : (half + 1) * CZ]
    p = side_of_dev()
    even[...] = sides[1 - p]
    even2[...] = sides[1 - p]
    odd[...] = sides[p]


def last_kernel(
    g, b, w, left, chip, both, f2, f2low, f2high, c1x, wc, cleft, cchip, c2z, even1, odd, even2,
    out, cboth, col, line, line3, corr, col2, s1, gline, g1line,
):
    wide = Wide(g, b, w, left, chip)
    a = Coarse(c1x, wc, wide.left, wide.right)
    cright = partner(cchip)
    take(cboth, even1[...] + even2[...], odd[...])
    low, high, clow, chigh = both.at[0], both.at[1], cboth.at[0], cboth.at[1]
    crow = lax.broadcasted_iota(jnp.int32, (CY, CZ), 0)
    c2 = {}
    for x in range(-3, 7):
        k = Z_C + x + 3
        beyond = jnp.where(crow == 0, row(clow, k), jnp.where(crow == CY - 1, row(chigh, k), 0.0))
        c2[x] = slab(c2z, x + 3, CY) + a.w(x) * beyond
    sides = ((clow, 0), (chigh, CY - 1))
    for s, (side, y) in enumerate(sides):
        for x in range(-3, 7):
            col[x + 3 : x + 4, :] = a.first(x)[y : y + 1]
        line[s, 0:10, :] = side[Z_P : Z_P + 10, :] + side[Z_W : Z_W + 10, :] * col[0:10, :]
        for x in range(-2, 6):
            col[x + 2 : x + 3, :] = c2[x][y : y + 1]
        mid = line[s, 1:9, :]
        line3[s, 0:8, :] = (
            KEEP * mid
            + side[Z_Q : Z_Q + 8, :]
            + side[Z_W + 1 : Z_W + 9, :]
            * (line[s, 0:8, :] + line[s, 2:10, :] + beside_z(mid) + col[0:8, :])
        )
    c3 = {}
    for x in range(-2, 6):
        c = c2[x]
        c3[x] = KEEP * c + a.first(x) + a.w(x) * (
            c2[x - 1]
            + c2[x + 1]
            + beside_z(c)
            + beside_y(c, line[0, x + 3 : x + 4, :], line[1, x + 3 : x + 4, :])
        )
    for x in range(-1, 5):
        c = c3[x]
        c4 = KEEP * c + a.first(x) + a.w(x) * (
            c3[x - 1]
            + c3[x + 1]
            + beside_z(c)
            + beside_y(c, line3[0, x + 2 : x + 3, :], line3[1, x + 2 : x + 3, :])
        )
        for half, v in enumerate(spread_z(c4)):
            corr[half, pl.ds((x + 1) * BY, CY, stride=2), :] = v
            corr[half, pl.ds((x + 1) * BY + 1, CY, stride=2), :] = v
    for s, (side, y) in enumerate(sides):
        for x in range(-1, 5):
            col[x + 1 : x + 2, :] = c3[x][y : y + 1]
        mid = line3[s, 1:7, :]
        third = side[Z_R : Z_R + 6, :] + side[Z_V : Z_V + 6, :] * line[s, 2:8, :]
        fourth = (
            KEEP * mid
            + side[Z_C + 2 : Z_C + 8, :]
            + side[Z_W + 2 : Z_W + 8, :]
            * (line3[s, 0:6, :] + line3[s, 2:8, :] + beside_z(mid) + third + col[0:6, :])
        )
        for half, v in enumerate(spread_z(fourth)):
            corr[half, 6 * BY + 8 * s : 6 * BY + 8 * s + 6, :] = v

    def corr_at(k, n):
        return jnp.concatenate([corr[0, k : k + n, :], corr[1, k : k + n, :]], axis=1)

    g0 = {}
    for x in range(-2, 10):
        if x == -2:
            f = slab(cleft, 1)
        elif x == 9:
            f = slab(cright, 1)
        else:
            f = slab(f2, x + 1)
        g0[x] = f + corr_at((x + 2) // 2 * BY, BY)
    for s, (cside, side, y, f2side) in enumerate(((clow, low, 0, f2low), (chigh, high, BY - 1, f2high))):
        base = 6 * BY + 8 * s
        for x in range(-1, 9):
            k = base + (x + 2) // 2
            col2[x + 1 : x + 2, :] = corr_at(k, 1)
        gline[s, 1:9, :] = f2side[...] + col2[1:9, :]
        for j, x in enumerate((-1, 8)):
            k = Z_K + 2 * j
            gline[s, x + 1 : x + 2, 0:CZ] = row(cside, k) + col2[x + 1 : x + 2, 0:CZ]
            gline[s, x + 1 : x + 2, CZ:] = row(cside, k + 1) + col2[x + 1 : x + 2, CZ:]
        for x in range(BX):
            k = Z_S + 2 * x
            s1[x : x + 1, 0:CZ] = row(cside, k)
            s1[x : x + 1, CZ:] = row(cside, k + 1)
        moved = col2[1:9, :]
        for x in range(BX):
            col2[x : x + 1, :] = g0[x][y : y + 1]
        mid = gline[s, 1:9, :]
        g1line[s, 0:8, :] = (
            KEEP * mid
            + s1[0:8, :]
            + side[Y_W : Y_W + 8, :]
            * (moved + gline[s, 0:8, :] + gline[s, 2:10, :] + beside_z(mid) + col2[0:8, :])
        )
    g1 = {}
    for x in range(-1, 9):
        f = g0[x]
        g1[x] = KEEP * f + wide.w(x) * (
            wide.rhs(x)
            + g0[x - 1]
            + g0[x + 1]
            + beside_z(f)
            + beside_y(f, gline[0, x + 1 : x + 2, :], gline[1, x + 1 : x + 2, :])
        )
    for x in range(BX):
        f = g1[x]
        out[place(x)] = KEEP * f + wide.w(x) * (
            wide.rhs(x)
            + g1[x - 1]
            + g1[x + 1]
            + beside_z(f)
            + beside_y(f, g1line[0, x : x + 1, :], g1line[1, x : x + 1, :])
        )


def send(v, links):
    n = lax.axis_size("dev")
    return lax.ppermute(v, ("group", "dev"), [(i * n + j, k * n + l) for (i, j), (k, l) in links])


def back(links):
    return [(j, i) for i, j in links]


def swap(v, pairs):
    return send(v, pairs + back(pairs))


def share_chip(v):
    groups = [[i, i + 1] for i in range(0, lax.axis_size("group"), 2)]
    return lax.all_gather(v, "group", axis_index_groups=groups)


def cross_pairs(keep):
    devs = [d for d in range(lax.axis_size("dev")) if keep(d)]
    return [((i, d), (i + 1, d)) for i in range(1, lax.axis_size("group") - 1, 2) for d in devs]


def dev_pairs(start, keep):
    devs = [d for d in range(start, lax.axis_size("dev") - 1, 2) if keep(d)]
    return [((i, d), (i, d + 1)) for i in range(lax.axis_size("group")) for d in devs]


def is_start(d):
    return d % RUN == 0


def in_middle(d):
    return not (is_start(d) or before_end(d))


def is_end(d):
    return d % RUN == RUN - 1


def before_end(d):
    return d % RUN == RUN - 2


def body(g, b, n):
    block = (BX, BY, NZ)
    cross, cross2, chip, even, odd, f1z, g, b, w, d, wc = call(
        load_kernel,
        [(X_ROWS, NZ)] * 3 + [(Y_ROWS, NZ)] * 2 + [(BX * BY, NZ)] + [block] * 4 + [(CX * CY, CZ)],
        g, b, n,
        hbm=3,
        vmem=None,
        scratch=[pltpu.VMEM(block, jnp.int32), (2, Y_ROWS, NZ), (2, CX * BY, CZ), pltpu.SemaphoreType.DMA((3,))],
    )
    cross1 = swap(cross, cross_pairs(lambda d: not is_end(d)))
    even1 = swap(even, dev_pairs(0, lambda d: not before_end(d)))
    odd1 = swap(odd, dev_pairs(1, lambda d: not before_end(d + 1)))
    cross2 = swap(cross2, cross_pairs(is_end))
    even2, odd2, chip = call(again_kernel, [(Y_ROWS, NZ)] * 2 + [(X_ROWS, NZ)], even, odd, chip, even1)
    even2 = swap(even2, dev_pairs(0, before_end))
    odd2 = swap(odd2, dev_pairs(1, lambda d: before_end(d + 1)))
    chip = share_chip(chip)
    left, both = call(
        gather_kernel,
        [(X_ROWS, NZ), (2, Y_ROWS, NZ)],
        cross1, even1, odd1,
        cost=pl.CostEstimate(flops=2**34, bytes_accessed=0, transcendentals=0),
    )
    f2, f2low, f2high, c1, left, both, cross, near = call(
        middle_kernel,
        [(10 * BY, NZ), (BX, NZ), (BX, NZ), (CX * CY, CZ), (X_ROWS, NZ), (2, Y_ROWS, NZ)] + [(X2_ROWS, NZ)] * 2,
        g, b, w, d, wc, left, cross2, chip, f1z, both, even2, odd2,
        scratch=[(16, NZ), (2, 16, NZ), (2, CX * BY, CZ)],
    )
    cleft = swap(cross, cross_pairs(lambda d: True))
    cchip = share_chip(near)
    even, even2, odd, f2, f2low, f2high, c1x, c2z = call(
        pack_c_kernel,
        [(Z_ROWS, CZ)] * 3 + [(10 * BY, NZ), (BX, NZ), (BX, NZ), (3 * CX * CY, CZ), (10 * CY, CZ)],
        g, b, w, left, chip, both, f2, f2low, f2high, c1, wc, cleft, cchip,
        scratch=[(13, 8, NZ), (5, 8, NZ), (8, CZ), (2, Z_ROWS, CZ)],
    )
    inner, start, end = (dev_pairs(0, keep) for keep in (in_middle, is_start, before_end))
    even1 = send(even, inner + back(inner) + back(start))
    odd = swap(odd, dev_pairs(1, lambda d: True))
    even2 = send(even2, end + back(end) + start)
    (out,) = call(
        last_kernel,
        [block],
        g, b, w, left, chip, both, f2, f2low, f2high, c1x, wc, cleft, cchip, c2z, even1, odd, even2,
        scratch=[
            (2, Z_ROWS, CZ),
            (16, CZ), (2, 16, CZ), (2, 8, CZ), (2, 6 * BY + 16, CZ), (16, NZ), (8, NZ), (2, 16, NZ), (2, 8, NZ),
        ],
        hbm_out=True,
    )
    return out


def solution(mesh):
    s = P("group", "dev", None)
    return jax.shard_map(body, mesh=mesh, in_specs=(s, s, s), out_specs=s, check_vma=False)
```
